32 devices in a mesh: clip: 4 (over y, x), sp: 8 (over z, core).
Axes of the slice: x: 2, y: 2, z: 4, core: 2. Of those that a mesh axis runs over, the one named last changes fastest.
Arguments:
- tokens: bfloat16 [4, 16, 2048, 384], P('clip', None, 'sp'), may hold values from -6 to 6
- conditioning: bfloat16 [4, 384], P('clip'), may hold values from -6 to 6
- timesteps: int32 [4], P('clip'), may hold values from 0 to 999, as said below
- out_grad: bfloat16 [4, 16, 2048, 384], P('clip', None, 'sp'), may hold values from -6 to 6
- ada_weight: bfloat16 [384, 3456], replicated, may hold values from -0.4375 to 0.4375
- ada_bias: float32 [3456], replicated, may hold values from -3 to 3
- spatial_proj: bfloat16 [384, 1152], replicated, may hold values from -0.3125 to 0.3125
- spatial_bias: float32 [768], replicated, may hold values from -3 to 3
- spatial_out: bfloat16 [384, 384], replicated, may hold values from -6 to 6
- spatial_out_bias: float32 [384], replicated, may hold values from -2 to 2
- temporal_proj: bfloat16 [384, 1152], replicated, may hold values from -0.3125 to 0.3125
- temporal_bias: float32 [768], replicated, may hold values from -3 to 3
- temporal_out: bfloat16 [384, 384], replicated, may hold values from -0.75 to 0.75
- temporal_out_bias: float32 [384], replicated, may hold values from -2 to 2
- hidden_in: bfloat16 [384, 1536], replicated, may hold values from -0.3125 to 0.3125
- hidden_in_bias: float32 [1536], replicated, may hold values from -3 to 3
- hidden_out: bfloat16 [1536, 384], replicated, may hold values from -0.15625 to 0.15625
- hidden_out_bias: float32 [384], replicated, may hold values from -2 to 2
Outputs:
- block_out: bfloat16 [4, 16, 2048, 384], P('clip', None, 'sp')
- input_grad: bfloat16 [4, 16, 2048, 384], P('clip', None, 'sp')
- grad_ada_weight: float32 [384, 3456], replicated
- grad_ada_bias: float32 [3456], replicated
- grad_spatial_proj: float32 [384, 1152], replicated
- grad_spatial_bias: float32 [768], replicated
- grad_spatial_out: float32 [384, 384], replicated
- grad_spatial_out_bias: float32 [384], replicated
- grad_temporal_proj: float32 [384, 1152], replicated
- grad_temporal_bias: float32 [768], replicated
- grad_temporal_out: float32 [384, 384], replicated
- grad_temporal_out_bias: float32 [384], replicated
- grad_hidden_in: float32 [384, 1536], replicated
- grad_hidden_in_bias: float32 [1536], replicated
- grad_hidden_out: float32 [1536, 384], replicated
- grad_hidden_out_bias: float32 [384], replicated
The draws below stay inside these ranges and needn't reach their ends.
Inputs may be any that keep to these rules, and one draw needn't show every extreme that they name: One diffusion timestep a clip; later timesteps are more common, and some clip has the last one, 999.
All inputs are finite; a program needn't handle non-finite values.
Results may differ from the reference program's by a relative error of at most 0.025.
The reference program's roundings to bfloat16 on the way count: a program that leaves them out, or rounds other values in their place, can miss the bound.
Values may be sent and summed in bfloat16 or wider, within the bound.
A program may use at most 1.125 GiB of HBM per device.

```python
import math
import jax
import jax.numpy as jnp
from jax import lax

D = 384
HEADS = 6
HEAD_DIM = 64
FF = 1536
FRAMES = 16
TSTEPS = 1000
PATCHES = 2048
CLIPS = 4


def draw_timesteps(key, part):
    key = jax.random.fold_in(key, 11)
    subkeys = jax.random.split(key, 4)
    first = jax.random.randint(subkeys[0], (CLIPS,), 0, TSTEPS)
    second = jax.random.randint(subkeys[1], (CLIPS,), 0, TSTEPS)
    chosen = jnp.maximum(first, second)
    order = jax.random.permutation(subkeys[2], CLIPS)
    early = jax.random.randint(subkeys[3], (), TSTEPS // 8, TSTEPS // 4)
    chosen = chosen.at[order[0]].set(TSTEPS - 1)
    chosen = chosen.at[order[1]].set(early)
    return chosen.astype(jnp.int32)


def block_scale(rng, shape, cuts, least, top_value):
    def one(axis_at, shards_of):
        heights = jax.random.uniform(jax.random.fold_in(jax.random.fold_in(rng, 6), axis_at), (shards_of,), jnp.float32, least / len(cuts), top_value / len(cuts))
        return jnp.repeat(jnp.exp(heights), shape[axis_at] // shards_of).reshape((-1,) + (1,) * (len(shape) - axis_at - 1))

    loudness = one(*cuts[0])
    for cut in cuts[1:]:
        loudness = loudness * one(*cut)
    return loudness


def normal_values(stream_key, shape, deviation, most, shards=(), dtype=jnp.bfloat16):
    array = jax.random.normal(stream_key, shape, jnp.float32) * deviation
    if len(shards) > 0:
        array = block_scale(stream_key, shape, shards, -0.22, 0.18) * array
    return jnp.clip(array, min=-most, max=most).astype(dtype)


def setup_inputs(seed: int = 0) -> dict:
    seeds = jax.random.split(jax.random.key(seed), 19)
    tokens = normal_values(seeds[0], (CLIPS, FRAMES, PATCHES, D), 1.0, 6.0, ((0, 4), (2, 8)))
    conditioning = normal_values(seeds[1], (CLIPS, D), 1.0, 6.0, ((0, 4),))
    timesteps = draw_timesteps(jax.random.fold_in(seeds[18], 71), 0)
    out_grad = normal_values(seeds[3], (CLIPS, FRAMES, PATCHES, D), 1.0, 6.0, ((0, 4), (2, 8)))
    ada_weight = normal_values(seeds[4], (D, 9 * D), (D // 2) ** -0.5, 0.4375)
    ada_bias = normal_values(seeds[5], (9 * D,), 0.5, 3.0, (), jnp.float32)
    spatial_proj = normal_values(seeds[6], (D, 3 * D), D ** -0.5, 0.3125)
    spatial_bias = normal_values(seeds[7], (2 * D,), 0.5, 3.0, (), jnp.float32)
    spatial_out = normal_values(seeds[8], (D, D), (max(1, 3 * D // PATCHES)) ** -0.5, 6.0)
    spatial_out_bias = normal_values(seeds[9], (D,), 0.3, 2.0, (), jnp.float32)
    temporal_proj = normal_values(seeds[10], (D, 3 * D), D ** -0.5, 0.3125)
    temporal_bias = normal_values(seeds[11], (2 * D,), 0.5, 3.0, (), jnp.float32)
    temporal_out = normal_values(seeds[12], (D, D), (max(1, D // 6)) ** -0.5, 0.75)
    temporal_out_bias = normal_values(seeds[13], (D,), 0.3, 2.0, (), jnp.float32)
    hidden_in = normal_values(seeds[14], (D, FF), D ** -0.5, 0.3125)
    hidden_in_bias = normal_values(seeds[15], (FF,), 0.5, 3.0, (), jnp.float32)
    hidden_out = normal_values(seeds[16], (FF, D), FF ** -0.5, 0.15625)
    hidden_out_bias = normal_values(seeds[17], (D,), 0.3, 2.0, (), jnp.float32)
    return dict(tokens=tokens, conditioning=conditioning, timesteps=timesteps, out_grad=out_grad, ada_weight=ada_weight, ada_bias=ada_bias, spatial_proj=spatial_proj, spatial_bias=spatial_bias, spatial_out=spatial_out, spatial_out_bias=spatial_out_bias, temporal_proj=temporal_proj, temporal_bias=temporal_bias, temporal_out=temporal_out, temporal_out_bias=temporal_out_bias, hidden_in=hidden_in, hidden_in_bias=hidden_in_bias, hidden_out=hidden_out, hidden_out_bias=hidden_out_bias)


@jax.custom_vjp
def low(v):
    return lax.optimization_barrier(v.astype(jnp.bfloat16)).astype(jnp.float32)

@jax.custom_vjp
def low_back(v):
    return v

def low_keep(v):
    return (low(v), None)

def low_pass(kept, grad):
    return (grad,)

def back_keep(v):
    return (v, None)

def back_low(kept, grad):
    return (low(grad),)
low.defvjp(low_keep, low_pass)
low_back.defvjp(back_keep, back_low)

def contract(pattern, left_term, right_term):
    return jnp.einsum(pattern, left_term, right_term, precision=lax.Precision.HIGHEST)

def modulate(field, shift, scale):
    centred = field - lax.optimization_barrier(jnp.mean(field, axis=-1, keepdims=True))
    normed = centred * lax.rsqrt(lax.optimization_barrier(jnp.mean(centred * centred, axis=-1, keepdims=True)) + 1e-06)
    return normed * (1.0 + scale) + shift

def loss_weights(timesteps):
    phase = (timesteps.astype(jnp.float32) / TSTEPS + 0.008) / 1.008 * (0.5 * math.pi)
    slope = jnp.tan(phase)
    return jnp.minimum(1.0, 5.0 * slope * slope)

def softmax_mix(scores, values, pattern):
    row_max = lax.optimization_barrier(jnp.max(scores, axis=-1, keepdims=True))
    exponent = jnp.exp(scores - row_max)
    soft_weights = low(exponent / lax.optimization_barrier(jnp.sum(exponent, axis=-1, keepdims=True)))
    return contract(pattern, soft_weights, values)

def project_heads(hidden, weight, bias):
    mixed = contract('fpd,de->fpe', hidden, weight)
    width = weight.shape[0]
    parts = (mixed[..., :width] + bias[:width], mixed[..., width:2 * width], mixed[..., 2 * width:] + bias[width:])
    return [low_back(low(part)).reshape(part.shape[:-1] + (HEADS, HEAD_DIM)) for part in parts]

def frame_attention(block):
    queries, keys, values = block
    scores = low_back(contract('qhe,khe->hqk', queries, keys)) * HEAD_DIM ** (-0.5)
    return softmax_mix(scores, values, 'hqk,khe->qhe')

def branch_out(mixed, weight, bias):
    joined = low_back(low(mixed.reshape(mixed.shape[:2] + (D,))))
    return low_back(contract('fpd,de->fpe', joined, weight) + bias)

def clip_block(field, cond_row, ada_weight, ada_bias, spatial_proj, spatial_bias, spatial_out, spatial_out_bias, temporal_proj, temporal_bias, temporal_out, temporal_out_bias, hidden_in, hidden_in_bias, hidden_out, hidden_out_bias):
    modes = (contract('d,de->e', low(jax.nn.silu(cond_row)), ada_weight) + ada_bias).reshape(9, D)
    hidden = low(modulate(field, modes[0], modes[1]))
    queries, keys, values = project_heads(hidden, spatial_proj, spatial_bias)
    mixed = lax.map(jax.checkpoint(frame_attention), (queries, keys, values))
    field = field + modes[2] * branch_out(mixed, spatial_out, spatial_out_bias)
    hidden = low(modulate(field, modes[3], modes[4]))
    queries, keys, values = project_heads(hidden, temporal_proj, temporal_bias)
    scores = low_back(contract('fphe,gphe->phfg', queries, keys)) * HEAD_DIM ** (-0.5)
    mixed = softmax_mix(scores, values, 'phfg,gphe->fphe')
    field = field + modes[5] * branch_out(mixed, temporal_out, temporal_out_bias)
    hidden = low(modulate(field, modes[6], modes[7]))
    inner = low_back(contract('fpd,dk->fpk', hidden, hidden_in) + hidden_in_bias)
    active = low(jax.nn.gelu(inner, approximate=True))
    branch = low_back(contract('fpk,kd->fpd', active, hidden_out) + hidden_out_bias)
    return field + modes[8] * branch

def reference(tokens, conditioning, timesteps, out_grad, ada_weight, ada_bias, spatial_proj, spatial_bias, spatial_out, spatial_out_bias, temporal_proj, temporal_bias, temporal_out, temporal_out_bias, hidden_in, hidden_in_bias, hidden_out, hidden_out_bias):
    params = tuple((item.astype(jnp.float32) for item in (ada_weight, ada_bias, spatial_proj, spatial_bias, spatial_out, spatial_out_bias, temporal_proj, temporal_bias, temporal_out, temporal_out_bias, hidden_in, hidden_in_bias, hidden_out, hidden_out_bias)))
    weights = loss_weights(timesteps)

    def per_clip(totals, inputs):
        field, cond_row, cotangent, weight = inputs

        def forward(field_in, *param_list):
            return clip_block(field_in, cond_row, *param_list)
        result, pullback = jax.vjp(forward, field, *params)
        grads = pullback(cotangent * weight)
        totals = tuple((total + grad for total, grad in zip(totals, grads[1:])))
        return (totals, (result.astype(jnp.bfloat16), grads[0].astype(jnp.bfloat16)))
    start = tuple((jnp.zeros(item.shape, jnp.float32) for item in params))
    totals, outputs = lax.scan(per_clip, start, (tokens.astype(jnp.float32), conditioning.astype(jnp.float32), out_grad.astype(jnp.float32), weights))
    return (outputs[0], outputs[1], totals[0], totals[1], totals[2], totals[3], totals[4], totals[5], totals[6], totals[7], totals[8], totals[9], totals[10], totals[11], totals[12], totals[13])
```

```python
from functools import partial, reduce
import math

import jax
import jax.numpy as jnp
from jax import lax
from jax.experimental import pallas as pl
from jax.experimental.pallas import tpu as pltpu
from jax.sharding import PartitionSpec as P

HEADS = 6
HEAD_DIM = 64
FRAME_BLOCK = 8
TSTEPS = 1000
GELU_RATE = math.sqrt(2.0 / math.pi)


def modulate(field, shift, scale):
    centred = field - jnp.mean(field, axis=-1, keepdims=True)
    normed = centred * lax.rsqrt(jnp.mean(centred * centred, axis=-1, keepdims=True) + 1e-06)
    return normed * (1.0 + scale) + shift


def loss_weights(timesteps):
    phase = (timesteps.astype(jnp.float32) / TSTEPS + 0.008) / 1.008 * (0.5 * math.pi)
    slope = jnp.tan(phase)
    return jnp.minimum(1.0, 5.0 * slope * slope)


def split_heads(array):
    return array.reshape(array.shape[:-1] + (HEADS, HEAD_DIM))


def join_heads(array):
    return array.reshape(array.shape[:-2] + (HEADS * HEAD_DIM,))


def attend(queries, keys, values):
    scores = jnp.einsum(
        "csqhe,cskhe->cshqk", queries, keys, preferred_element_type=jnp.float32
    ) * HEAD_DIM ** (-0.5)
    row_max = jnp.max(scores, axis=-1, keepdims=True)
    exponent = jnp.exp(scores - row_max)
    total = jnp.sum(exponent, axis=-1, keepdims=True)
    soft_weights = (exponent / total).astype(jnp.bfloat16)
    mixed = jnp.einsum(
        "cshqk,cskhe->csqhe", soft_weights, values, preferred_element_type=jnp.float32
    )
    return (mixed, row_max[..., 0] + jnp.log(total[..., 0]))


def probabilities(queries, keys, values, grads, log_total):
    scores = jnp.einsum(
        "csqhe,cskhe->cshqk", queries, keys, preferred_element_type=jnp.float32
    ) * HEAD_DIM ** (-0.5)
    soft_weights = jnp.exp(scores - log_total[..., None])
    grad_weights = jnp.einsum(
        "csqhe,cskhe->cshqk", grads, values, preferred_element_type=jnp.float32
    )
    return (soft_weights, grad_weights)


def query_pass(queries, keys, values, grads, log_total):
    soft_weights, grad_weights = probabilities(queries, keys, values, grads, log_total)
    delta = jnp.sum(soft_weights * grad_weights, axis=-1)
    grad_scores = (soft_weights * (grad_weights - delta[..., None]) * HEAD_DIM ** (-0.5)).astype(
        jnp.bfloat16
    )
    grad_queries = jnp.einsum(
        "cshqk,cskhe->csqhe", grad_scores, keys, preferred_element_type=jnp.float32
    )
    return (grad_queries, delta)


def key_pass(queries, keys, values, grads, log_total, delta):
    soft_weights, grad_weights = probabilities(queries, keys, values, grads, log_total)
    grad_scores = (soft_weights * (grad_weights - delta[..., None]) * HEAD_DIM ** (-0.5)).astype(
        jnp.bfloat16
    )
    grad_keys = jnp.einsum(
        "cshqk,csqhe->cskhe", grad_scores, queries, preferred_element_type=jnp.float32
    )
    grad_values = jnp.einsum(
        "cshqk,csqhe->cskhe",
        soft_weights.astype(jnp.bfloat16),
        grads,
        preferred_element_type=jnp.float32,
    )
    return jnp.concatenate([join_heads(grad_keys), join_heads(grad_values)], axis=-1)


def column_sums(array):
    return jnp.sum(array.astype(jnp.float32), axis=(0, 1, 2))


def body(
    tokens,
    conditioning,
    timesteps,
    out_grad,
    ada_weight,
    ada_bias,
    spatial_proj,
    spatial_bias,
    spatial_out,
    spatial_out_bias,
    temporal_proj,
    temporal_bias,
    temporal_out,
    temporal_out_bias,
    hidden_in,
    hidden_in_bias,
    hidden_out,
    hidden_out_bias,
):
    clips, frames, stripe, width = tokens.shape
    blocks = frames // FRAME_BLOCK
    scale_factor = HEAD_DIM ** (-0.5)
    field = tokens.astype(jnp.float32)
    cond_act = jax.nn.silu(conditioning.astype(jnp.float32)).astype(jnp.bfloat16)
    modes = jnp.dot(cond_act, ada_weight, preferred_element_type=jnp.float32) + ada_bias
    modes = modes.reshape(clips, 9, 1, 1, width)
    hidden_one, back_one = jax.vjp(modulate, field, modes[:, 0], modes[:, 1])
    hidden_one = hidden_one.astype(jnp.bfloat16)
    query_mix = jnp.einsum(
        "cfpd,de->cfpe", hidden_one, spatial_proj[:, :width], preferred_element_type=jnp.float32
    )
    queries = (query_mix + spatial_bias[:width]).astype(jnp.bfloat16)
    keyval_mix = jnp.einsum(
        "cfpd,de->cfpe", hidden_one, spatial_proj[:, width:], preferred_element_type=jnp.float32
    )
    keyval_bias = jnp.concatenate([jnp.zeros((width,), jnp.float32), spatial_bias[width:]])
    keyvals = (keyval_mix + keyval_bias).astype(jnp.bfloat16)
    query_heads = split_heads(queries)
    mixed_parts = []
    log_parts = []
    for index in range(blocks):
        first = index * FRAME_BLOCK
        whole = lax.all_gather(keyvals[:, first : first + FRAME_BLOCK], "sp", axis=2, tiled=True)
        mixed_part, log_part = attend(
            query_heads[:, first : first + FRAME_BLOCK],
            split_heads(whole[..., :width]),
            split_heads(whole[..., width:]),
        )
        mixed_parts.append(join_heads(mixed_part))
        log_parts.append(log_part)
    attn_one = jnp.concatenate(mixed_parts, axis=1).astype(jnp.bfloat16)
    spatial_log = jnp.concatenate(log_parts, axis=1)
    branch_one = (
        jnp.einsum("cfpd,de->cfpe", attn_one, spatial_out, preferred_element_type=jnp.float32)
        + spatial_out_bias
    )
    field_one = field + modes[:, 2] * branch_one
    hidden_two, back_two = jax.vjp(modulate, field_one, modes[:, 3], modes[:, 4])
    hidden_two = hidden_two.astype(jnp.bfloat16)
    time_mix = jnp.einsum(
        "cfpd,de->cfpe", hidden_two, temporal_proj, preferred_element_type=jnp.float32
    )
    time_queries = split_heads((time_mix[..., :width] + temporal_bias[:width]).astype(jnp.bfloat16))
    time_keys = split_heads(time_mix[..., width : 2 * width].astype(jnp.bfloat16))
    time_values = split_heads(
        (time_mix[..., 2 * width :] + temporal_bias[width:]).astype(jnp.bfloat16)
    )
    time_scores = (
        jnp.einsum(
            "cfphe,cgphe->cphfg", time_queries, time_keys, preferred_element_type=jnp.float32
        )
        * scale_factor
    )
    time_max = jnp.max(time_scores, axis=-1, keepdims=True)
    time_exponent = jnp.exp(time_scores - time_max)
    time_weights = time_exponent / jnp.sum(time_exponent, axis=-1, keepdims=True)
    time_rounded = time_weights.astype(jnp.bfloat16)
    attn_two = join_heads(
        jnp.einsum(
            "cphfg,cgphe->cfphe", time_rounded, time_values, preferred_element_type=jnp.float32
        )
    ).astype(jnp.bfloat16)
    branch_two = (
        jnp.einsum("cfpd,de->cfpe", attn_two, temporal_out, preferred_element_type=jnp.float32)
        + temporal_out_bias
    )
    field_two = field_one + modes[:, 5] * branch_two
    hidden_three, back_three = jax.vjp(modulate, field_two, modes[:, 6], modes[:, 7])
    hidden_three = hidden_three.astype(jnp.bfloat16)
    inner = (
        jnp.einsum("cfpd,dk->cfpk", hidden_three, hidden_in, preferred_element_type=jnp.float32)
        + hidden_in_bias
    )
    active, gelu_back = jax.vjp(partial(jax.nn.gelu, approximate=True), inner)
    active = active.astype(jnp.bfloat16)
    branch_three = (
        jnp.einsum("cfpk,kd->cfpd", active, hidden_out, preferred_element_type=jnp.float32)
        + hidden_out_bias
    )
    block_out = (field_two + modes[:, 8] * branch_three).astype(jnp.bfloat16)
    weights = loss_weights(timesteps)
    grad_field = out_grad.astype(jnp.float32) * weights[:, None, None, None]
    grad_gate_three = jnp.sum(grad_field * branch_three, axis=(1, 2))
    grad_branch = (modes[:, 8] * grad_field).astype(jnp.bfloat16)
    grad_hidden_out = jnp.einsum(
        "cfpk,cfpd->kd", active, grad_branch, preferred_element_type=jnp.float32
    )
    grad_hidden_out_bias = column_sums(grad_branch)
    grad_active = jnp.einsum(
        "cfpd,kd->cfpk", grad_branch, hidden_out, preferred_element_type=jnp.float32
    )
    grad_inner = gelu_back(grad_active)[0].astype(jnp.bfloat16)
    grad_hidden_in = jnp.einsum(
        "cfpd,cfpk->dk", hidden_three, grad_inner, preferred_element_type=jnp.float32
    )
    grad_hidden_in_bias = column_sums(grad_inner)
    grad_hidden = jnp.einsum(
        "cfpk,dk->cfpd", grad_inner, hidden_in, preferred_element_type=jnp.float32
    )
    grad_input, grad_shift_three, grad_scale_three = back_three(grad_hidden)
    grad_field = grad_field + grad_input
    grad_gate_two = jnp.sum(grad_field * branch_two, axis=(1, 2))
    grad_branch = (modes[:, 5] * grad_field).astype(jnp.bfloat16)
    grad_temporal_out = jnp.einsum(
        "cfpd,cfpe->de", attn_two, grad_branch, preferred_element_type=jnp.float32
    )
    grad_temporal_out_bias = column_sums(grad_branch)
    grad_attn = split_heads(
        jnp.einsum(
            "cfpe,de->cfpd", grad_branch, temporal_out, preferred_element_type=jnp.float32
        ).astype(jnp.bfloat16)
    )
    grad_weights = jnp.einsum(
        "cfphe,cgphe->cphfg", grad_attn, time_values, preferred_element_type=jnp.float32
    )
    delta = jnp.sum(time_weights * grad_weights, axis=-1, keepdims=True)
    grad_scores = (time_weights * (grad_weights - delta) * scale_factor).astype(jnp.bfloat16)
    grad_time_queries = jnp.einsum(
        "cphfg,cgphe->cfphe", grad_scores, time_keys, preferred_element_type=jnp.float32
    )
    grad_time_keys = jnp.einsum(
        "cphfg,cfphe->cgphe", grad_scores, time_queries, preferred_element_type=jnp.float32
    )
    grad_time_values = jnp.einsum(
        "cphfg,cfphe->cgphe", time_rounded, grad_attn, preferred_element_type=jnp.float32
    )
    grad_time_mix = jnp.concatenate(
        [join_heads(grad_time_queries), join_heads(grad_time_keys), join_heads(grad_time_values)],
        axis=-1,
    ).astype(jnp.bfloat16)
    grad_temporal_proj = jnp.einsum(
        "cfpd,cfpe->de", hidden_two, grad_time_mix, preferred_element_type=jnp.float32
    )
    grad_temporal_bias = jnp.concatenate(
        [column_sums(grad_time_mix[..., :width]), column_sums(grad_time_mix[..., 2 * width :])]
    )
    grad_hidden = jnp.einsum(
        "cfpe,de->cfpd", grad_time_mix, temporal_proj, preferred_element_type=jnp.float32
    )
    grad_input, grad_shift_two, grad_scale_two = back_two(grad_hidden)
    grad_field = grad_field + grad_input
    grad_gate_one = jnp.sum(grad_field * branch_one, axis=(1, 2))
    grad_branch = (modes[:, 2] * grad_field).astype(jnp.bfloat16)
    grad_spatial_out = jnp.einsum(
        "cfpd,cfpe->de", attn_one, grad_branch, preferred_element_type=jnp.float32
    )
    grad_spatial_out_bias = column_sums(grad_branch)
    grad_attn = jnp.einsum(
        "cfpe,de->cfpd", grad_branch, spatial_out, preferred_element_type=jnp.float32
    ).astype(jnp.bfloat16)
    query_parts = []
    key_parts = []
    for index in range(blocks):
        first = index * FRAME_BLOCK
        whole = lax.all_gather(keyvals[:, first : first + FRAME_BLOCK], "sp", axis=2, tiled=True)
        piece = query_heads[:, first : first + FRAME_BLOCK]
        grad_piece = split_heads(grad_attn[:, first : first + FRAME_BLOCK])
        log_piece = spatial_log[:, first : first + FRAME_BLOCK]
        grad_query_part, delta = query_pass(
            piece,
            split_heads(whole[..., :width]),
            split_heads(whole[..., width:]),
            grad_piece,
            log_piece,
        )
        term = key_pass(
            piece,
            split_heads(whole[..., :width]),
            split_heads(whole[..., width:]),
            grad_piece,
            log_piece,
            delta,
        )
        owned = lax.psum_scatter(
            jnp.transpose(term, (2, 0, 1, 3)).astype(jnp.bfloat16),
            "sp",
            scatter_dimension=0,
            tiled=True,
        ).astype(jnp.float32)
        query_parts.append(join_heads(grad_query_part))
        key_parts.append(jnp.transpose(owned, (1, 2, 0, 3)))
    grad_queries = jnp.concatenate(query_parts, axis=1)
    grad_keyvals = jnp.concatenate(key_parts, axis=1)
    grad_queries = grad_queries.astype(jnp.bfloat16)
    grad_keyvals = grad_keyvals.astype(jnp.bfloat16)
    grad_spatial_proj = jnp.concatenate(
        [
            jnp.einsum(
                "cfpd,cfpe->de", hidden_one, grad_queries, preferred_element_type=jnp.float32
            ),
            jnp.einsum(
                "cfpd,cfpe->de", hidden_one, grad_keyvals, preferred_element_type=jnp.float32
            ),
        ],
        axis=1,
    )
    grad_spatial_bias = jnp.concatenate(
        [column_sums(grad_queries), column_sums(grad_keyvals[..., width:])]
    )
    grad_hidden = jnp.einsum(
        "cfpe,de->cfpd", grad_queries, spatial_proj[:, :width], preferred_element_type=jnp.float32
    )
    grad_hidden = grad_hidden + jnp.einsum(
        "cfpe,de->cfpd", grad_keyvals, spatial_proj[:, width:], preferred_element_type=jnp.float32
    )
    grad_input, grad_shift_one, grad_scale_one = back_one(grad_hidden)
    input_grad = (grad_field + grad_input).astype(jnp.bfloat16)
    grad_modes = jnp.stack(
        [
            grad_shift_one.reshape(clips, width),
            grad_scale_one.reshape(clips, width),
            grad_gate_one,
            grad_shift_two.reshape(clips, width),
            grad_scale_two.reshape(clips, width),
            grad_gate_two,
            grad_shift_three.reshape(clips, width),
            grad_scale_three.reshape(clips, width),
            grad_gate_three,
        ],
        axis=1,
    ).reshape(clips, 9 * width)
    grad_ada_weight = jnp.dot(
        cond_act.astype(jnp.float32).T, grad_modes, precision=lax.Precision.HIGHEST
    )
    grad_ada_bias = jnp.sum(grad_modes, axis=0)
    summed = lax.psum(
        (
            grad_ada_weight,
            grad_ada_bias,
            grad_spatial_proj,
            grad_spatial_bias,
            grad_spatial_out,
            grad_spatial_out_bias,
            grad_temporal_proj,
            grad_temporal_bias,
            grad_temporal_out,
            grad_temporal_out_bias,
            grad_hidden_in,
            grad_hidden_in_bias,
            grad_hidden_out,
            grad_hidden_out_bias,
        ),
        ("clip", "sp"),
    )
    return (
        block_out,
        input_grad,
        summed[0],
        summed[1],
        summed[2],
        summed[3],
        summed[4],
        summed[5],
        summed[6],
        summed[7],
        summed[8],
        summed[9],
        summed[10],
        summed[11],
        summed[12],
        summed[13],
    )


MXB = jnp.bfloat16
F32 = jnp.float32
TILE = 16
VMEM_BYTES = 60 * 2**20


def dot(left, right):
    return jnp.dot(left, right, preferred_element_type=F32)


def dot_nt(left, right):
    return lax.dot_general(left, right, (((1,), (1,)), ((), ())), preferred_element_type=F32)


def dot_tn(left, right):
    return lax.dot_general(left, right, (((0,), (0,)), ((), ())), preferred_element_type=F32)


def turned(array):
    return array.astype(F32).T.astype(array.dtype)


def normalise(field):
    centred = field - jnp.mean(field, axis=-1, keepdims=True)
    rate = lax.rsqrt(jnp.mean(centred * centred, axis=-1, keepdims=True) + 1e-06)
    return centred * rate, rate


def normalise_back(grad, normed, rate, scale):
    inner = grad * (1.0 + scale)
    mean = jnp.mean(inner, axis=-1, keepdims=True)
    slope = jnp.mean(inner * normed, axis=-1, keepdims=True)
    return rate * (inner - mean - normed * slope)


def eight_rows(array):
    return jnp.sum(array.reshape(array.shape[0] // 8, 8, array.shape[1]), axis=0)


def low_lanes():
    return lax.broadcasted_iota(jnp.int32, (1, 2 * HEAD_DIM), 1) < HEAD_DIM


def halves(pair):
    low = low_lanes()
    zero = jnp.zeros_like(pair)
    return jnp.where(low, pair, zero), jnp.where(low, zero, pair)


def spatial_forward(
    x_ref, modes_ref, proj_ref, bias_ref, q_ref, k_ref, v_ref, attn_ref, log_ref, turned_ref, rows, block, part
):
    tokens, width = x_ref.shape[1:]
    pairs = width // (2 * HEAD_DIM)
    shift = modes_ref[0:1, :]
    scale = modes_ref[1:2, :]

    def project(index, carry):
        at = pl.ds(pl.multiple_of(index * rows, rows), rows)
        normed, _ = normalise(x_ref[0, at, :].astype(F32))
        hidden = (normed * (1.0 + scale) + shift).astype(MXB)
        mixed = dot(hidden, proj_ref[...]) + bias_ref[...]
        q_ref[0, at, :] = mixed[:, :width].astype(MXB)
        k_ref[0, at, :] = mixed[:, width : 2 * width].astype(MXB)
        value = mixed[:, 2 * width :].astype(MXB)
        v_ref[0, at, :] = value
        across = turned(value)
        for head in range(2 * pairs):
            turned_ref[head, :HEAD_DIM, at] = across[head * HEAD_DIM : (head + 1) * HEAD_DIM]
        return carry

    turned_ref[:, HEAD_DIM:, :] = jnp.ones((2 * pairs, turned_ref.shape[1] - HEAD_DIM, tokens), MXB)
    lax.fori_loop(0, tokens // rows, project, 0)

    def attend_block(index, carry):
        pair = lax.rem(index, pairs)
        at = pl.ds(pl.multiple_of(lax.div(index, pairs) * block, block), block)
        lanes = pl.ds(pl.multiple_of(pair * 2 * HEAD_DIM, 2 * HEAD_DIM), 2 * HEAD_DIM)
        scores = []
        tops = []
        for query in halves(q_ref[0, at, lanes] * MXB(HEAD_DIM**-0.5)):
            each = [
                dot_nt(k_ref[0, first : first + part, lanes], query) for first in range(0, tokens, part)
            ]
            top = [jnp.max(s.reshape(part // 8, 8, block), axis=0) for s in each]
            scores.append(each)
            tops.append(jnp.max(reduce(jnp.maximum, top), axis=0, keepdims=True))
        mixed = []
        for half in range(2):
            total = jnp.zeros((turned_ref.shape[1], block), F32)
            for number, s in enumerate(scores[half]):
                weights = jnp.exp(s - tops[half]).astype(MXB)
                values = turned_ref[2 * pair + half, :, number * part : (number + 1) * part]
                total = total + dot(values, weights)
            mass = total[HEAD_DIM : HEAD_DIM + 1]
            log_ref[0, pair, half : half + 1, at] = tops[half] + jnp.log(mass)
            mixed.append(total[:HEAD_DIM] / mass)
        attn_ref[0, at, lanes] = jnp.concatenate(mixed, axis=0).T.astype(MXB)
        return carry

    lax.fori_loop(0, pairs * (tokens // block), attend_block, 0)


def spatial_backward(
    da_ref, attn_ref, q_ref, k_ref, v_ref, log_ref, x_ref, modes_ref, proj_turned_ref,
    dx_ref, grad_proj_ref, sums_ref, bias_sums_ref,
    mix_ref, delta_ref, dk_ref, dv_ref, rows, block, part,
):
    tokens, width = x_ref.shape[1:]
    pairs = width // (2 * HEAD_DIM)
    scale_factor = HEAD_DIM**-0.5

    @pl.when(pl.program_id(0) == 0)
    def _():
        grad_proj_ref[...] = jnp.zeros_like(grad_proj_ref)
        sums_ref[...] = jnp.zeros_like(sums_ref)
        bias_sums_ref[...] = jnp.zeros_like(bias_sums_ref)

    head_of = lax.broadcasted_iota(jnp.int32, (8, width), 1) // HEAD_DIM
    picks = jnp.where(head_of == lax.broadcasted_iota(jnp.int32, (8, width), 0), 1.0, 0.0).astype(MXB)

    def deltas(index, carry):
        at = pl.ds(pl.multiple_of(index * rows, rows), rows)
        product = da_ref[0, at, :].astype(F32) * attn_ref[0, at, :].astype(F32)
        high = product.astype(MXB)
        rest = (product - high.astype(F32)).astype(MXB)
        summed = dot_nt(picks, high) + dot_nt(picks, rest)
        for pair in range(pairs):
            delta_ref[pair, 0:2, at] = summed[2 * pair : 2 * pair + 2]
        return carry

    lax.fori_loop(0, tokens // rows, deltas, 0)

    for pair in range(pairs):
        first_lane = 2 * HEAD_DIM * pair
        lanes = slice(first_lane, first_lane + 2 * HEAD_DIM)
        dk_ref[...] = jnp.zeros_like(dk_ref)
        dv_ref[...] = jnp.zeros_like(dv_ref)
        keys_across = turned(k_ref[0, :, lanes])

        def queries_block(index, carry, pair=pair, lanes=lanes, keys_across=keys_across):
            at = pl.ds(pl.multiple_of(index * block, block), block)
            query = halves(q_ref[0, at, lanes] * MXB(scale_factor))
            grad = halves(da_ref[0, at, lanes])
            query_both = jnp.concatenate(query, axis=0)
            grad_both = jnp.concatenate(grad, axis=0)
            grad_query = [jnp.zeros((HEAD_DIM, block), F32), jnp.zeros((HEAD_DIM, block), F32)]
            for first in range(0, tokens, part):
                span = slice(first, first + part)
                keys = k_ref[0, span, lanes]
                values = v_ref[0, span, lanes]
                weights = []
                grad_scores = []
                for half in range(2):
                    scores = dot_nt(keys, query[half])
                    exact = jnp.exp(scores - log_ref[0, pair, half : half + 1, at])
                    grad_weights = dot_nt(values, grad[half])
                    term = (exact * (grad_weights - delta_ref[pair, half : half + 1, at])).astype(MXB)
                    weights.append(exact.astype(MXB))
                    grad_scores.append(term)
                    grad_query[half] = grad_query[half] + dot(
                        keys_across[half * HEAD_DIM : (half + 1) * HEAD_DIM, span], term
                    )
                dv_ref[span, :] += dot(jnp.concatenate(weights, axis=1), grad_both)
                dk_ref[span, :] += dot(jnp.concatenate(grad_scores, axis=1), query_both)
            mix_ref[at, lanes] = (jnp.concatenate(grad_query, axis=0).T * scale_factor).astype(MXB)
            return carry

        lax.fori_loop(0, tokens // block, queries_block, 0)
        mix_ref[:, width + first_lane : width + first_lane + 2 * HEAD_DIM] = dk_ref[...].astype(MXB)
        mix_ref[:, 2 * width + first_lane : 2 * width + first_lane + 2 * HEAD_DIM] = dv_ref[...].astype(MXB)

    shift = modes_ref[0:1, :]
    scale = modes_ref[1:2, :]

    def finish(index, carry):
        at = pl.ds(pl.multiple_of(index * rows, rows), rows)
        normed, rate = normalise(x_ref[0, at, :].astype(F32))
        hidden = (normed * (1.0 + scale) + shift).astype(MXB)
        grad_mix = mix_ref[at, :]
        grad_proj_ref[...] += dot_tn(hidden, grad_mix)
        bias_sums_ref[...] += eight_rows(grad_mix.astype(F32))
        grad_hidden = dot(grad_mix, proj_turned_ref[...])
        sums_ref[0] += eight_rows(grad_hidden)
        sums_ref[1] += eight_rows(grad_hidden * normed)
        dx_ref[0, at, :] = normalise_back(grad_hidden, normed, rate, scale).astype(MXB)
        return carry

    lax.fori_loop(0, tokens // rows, finish, 0)


def middle(
    x_ref, attn_ref, og_ref, weight_ref, modes_ref, mask_ref,
    so_ref, so_turned_ref, so_bias_ref, t_ref, t_turned_ref, t_bias_ref, to_ref, to_turned_ref, to_bias_ref,
    in_ref, in_turned_ref, in_bias_ref, out_ref, out_turned_ref, out_bias_ref,
    block_ref, g1_ref, da_ref,
    grad_so_ref, grad_t_ref, grad_to_ref, grad_in_ref, grad_out_ref, sums_ref, t_sums_ref, in_sums_ref,
):
    frames, tile, width = x_ref.shape
    count = frames * tile
    pairs = width // (2 * HEAD_DIM)
    scale_factor = HEAD_DIM**-0.5

    @pl.when(pl.program_id(0) == 0)
    def _():
        for ref in (grad_so_ref, grad_t_ref, grad_to_ref, grad_in_ref, grad_out_ref, sums_ref, t_sums_ref, in_sums_ref):
            ref[...] = jnp.zeros_like(ref)

    def mode(row):
        return modes_ref[row : row + 1, :]

    field = x_ref[...].reshape(count, width).astype(F32)
    attn_one = attn_ref[...].reshape(count, width)
    branch_one = dot(attn_one, so_ref[...]) + so_bias_ref[...]
    field_one = field + mode(2) * branch_one
    normed_two, rate_two = normalise(field_one)
    hidden_two = (normed_two * (1.0 + mode(4)) + mode(3)).astype(MXB)
    mixed = (dot(hidden_two, t_ref[...]) + t_bias_ref[...]).astype(MXB)
    mask = mask_ref[...]
    exact = []
    rounded = []
    queries = []
    keys_across = []
    attn_parts = []
    for pair in range(pairs):
        lanes = slice(2 * HEAD_DIM * pair, 2 * HEAD_DIM * (pair + 1))
        query = halves(mixed[:, lanes] * MXB(scale_factor))
        keys = mixed[:, width:][:, lanes]
        values_across = turned(mixed[:, 2 * width :][:, lanes])
        queries.append(query)
        keys_across.append(turned(keys))
        parts = []
        for half in range(2):
            scores = dot_nt(keys, query[half]) + mask
            exponent = jnp.exp(scores - jnp.max(scores, axis=0, keepdims=True))
            weights = exponent / jnp.sum(exponent, axis=0, keepdims=True)
            exact.append(weights)
            rounded.append(weights.astype(MXB))
            parts.append(dot(values_across[half * HEAD_DIM : (half + 1) * HEAD_DIM], rounded[-1]))
        attn_parts.append(jnp.concatenate(parts, axis=0).T.astype(MXB))
    attn_two = jnp.concatenate(attn_parts, axis=1)
    branch_two = dot(attn_two, to_ref[...]) + to_bias_ref[...]
    field_two = field_one + mode(5) * branch_two
    normed_three, rate_three = normalise(field_two)
    hidden_three = (normed_three * (1.0 + mode(7)) + mode(6)).astype(MXB)
    inner = dot(hidden_three, in_ref[...]) + in_bias_ref[...]
    square = inner * inner
    bend = jnp.tanh(inner * (GELU_RATE + GELU_RATE * 0.044715 * square))
    half_up = 0.5 + 0.5 * bend
    active = (inner * half_up).astype(MXB)
    slope = half_up + inner * (0.5 - 0.5 * bend * bend) * (GELU_RATE + 3.0 * GELU_RATE * 0.044715 * square)
    branch_three = dot(active, out_ref[...]) + out_bias_ref[...]
    block_ref[...] = (field_two + mode(8) * branch_three).astype(MXB).reshape(frames, tile, width)

    grad_field = og_ref[...].reshape(count, width).astype(F32) * weight_ref[...]
    sums_ref[8] += eight_rows(grad_field * branch_three)
    grad_branch = (mode(8) * grad_field).astype(MXB)
    grad_out_ref[...] += dot_tn(grad_branch, active)
    sums_ref[11] += eight_rows(grad_branch.astype(F32))
    grad_inner = (dot(grad_branch, out_turned_ref[...]) * slope).astype(MXB)
    grad_in_ref[...] += dot_tn(hidden_three, grad_inner)
    in_sums_ref[...] += eight_rows(grad_inner.astype(F32))
    grad_hidden = dot(grad_inner, in_turned_ref[...])
    sums_ref[6] += eight_rows(grad_hidden)
    sums_ref[7] += eight_rows(grad_hidden * normed_three)
    grad_field = grad_field + normalise_back(grad_hidden, normed_three, rate_three, mode(7))

    sums_ref[5] += eight_rows(grad_field * branch_two)
    grad_branch = (mode(5) * grad_field).astype(MXB)
    grad_to_ref[...] += dot_tn(attn_two, grad_branch)
    sums_ref[10] += eight_rows(grad_branch.astype(F32))
    grad_attn = dot(grad_branch, to_turned_ref[...]).astype(MXB)
    grad_queries = []
    grad_keys = []
    grad_values = []
    for pair in range(pairs):
        lanes = slice(2 * HEAD_DIM * pair, 2 * HEAD_DIM * (pair + 1))
        grad = halves(grad_attn[:, lanes])
        values = mixed[:, 2 * width :][:, lanes]
        grad_query = []
        terms = []
        for half in range(2):
            weights = exact[2 * pair + half]
            grad_weights = dot_nt(values, grad[half])
            delta = jnp.sum(weights * grad_weights, axis=0, keepdims=True)
            term = (weights * (grad_weights - delta)).astype(MXB)
            terms.append(term)
            grad_query.append(dot(keys_across[pair][half * HEAD_DIM : (half + 1) * HEAD_DIM], term))
        both = jnp.concatenate(terms, axis=1)
        grad_queries.append((jnp.concatenate(grad_query, axis=0).T * scale_factor).astype(MXB))
        grad_keys.append(dot(both, jnp.concatenate(queries[pair], axis=0)).astype(MXB))
        grad_values.append(
            dot(
                jnp.concatenate([rounded[2 * pair], rounded[2 * pair + 1]], axis=1),
                jnp.concatenate(grad, axis=0),
            ).astype(MXB)
        )
    grad_mix = jnp.concatenate(grad_queries + grad_keys + grad_values, axis=1)
    grad_t_ref[...] += dot_tn(hidden_two, grad_mix)
    t_sums_ref[...] += eight_rows(grad_mix.astype(F32))
    grad_hidden = dot(grad_mix, t_turned_ref[...])
    sums_ref[3] += eight_rows(grad_hidden)
    sums_ref[4] += eight_rows(grad_hidden * normed_two)
    grad_field = grad_field + normalise_back(grad_hidden, normed_two, rate_two, mode(4))

    sums_ref[2] += eight_rows(grad_field * branch_one)
    grad_branch = (mode(2) * grad_field).astype(MXB)
    grad_so_ref[...] += dot_tn(attn_one, grad_branch)
    sums_ref[9] += eight_rows(grad_branch.astype(F32))
    g1_ref[...] = grad_field.reshape(frames, tile, width)
    da_ref[...] = dot(grad_branch, so_turned_ref[...]).astype(MXB).reshape(frames, tile, width)


def whole_spec(shape):
    rank = len(shape)
    return pl.BlockSpec(shape, lambda *_: (0,) * rank, pipeline_mode=pl.Buffered(1))


def acc_spec(shape):
    rank = len(shape)
    return pl.BlockSpec(shape, lambda *_: (0,) * rank)


def params():
    return pltpu.CompilerParams(vmem_limit_bytes=VMEM_BYTES)


def fast_body(
    tokens, conditioning, timesteps, out_grad, ada_weight, ada_bias, spatial_proj, spatial_bias, spatial_out,
    spatial_out_bias, temporal_proj, temporal_bias, temporal_out, temporal_out_bias, hidden_in, hidden_in_bias,
    hidden_out, hidden_out_bias,
):
    _, frames, stripe, width = tokens.shape
    hidden = hidden_in.shape[1]
    pairs = width // (2 * HEAD_DIM)
    cond_act = jax.nn.silu(conditioning.astype(F32)).astype(MXB)
    modes = (jnp.dot(cond_act, ada_weight, preferred_element_type=F32) + ada_bias).reshape(9, width)

    def to_frames(array):
        return lax.all_to_all(array, "sp", split_axis=0, concat_axis=1, tiled=True)

    def to_patches(array):
        return lax.all_to_all(array, "sp", split_axis=1, concat_axis=0, tiled=True)

    def widen(bias):
        return jnp.concatenate([bias[:width], jnp.zeros((width,), F32), bias[width:]])[None, :]

    x_patches = tokens[0]
    x_frames = to_frames(x_patches)
    mine, patches = x_frames.shape[:2]
    frame_spec = pl.BlockSpec((1, patches, width), lambda f: (f, 0, 0))
    log_spec = pl.BlockSpec((1, pairs, 2, patches), lambda f: (f, 0, 0, 0))
    frame_shape = jax.ShapeDtypeStruct((mine, patches, width), MXB)
    queries, keys, values, attn_frames, logs = pl.pallas_call(
        partial(spatial_forward, rows=256, block=min(1024, patches), part=512),
        grid=(mine,),
        in_specs=[frame_spec, whole_spec((9, width)), whole_spec((width, 3 * width)), whole_spec((1, 3 * width))],
        out_specs=[frame_spec] * 4 + [log_spec],
        out_shape=[frame_shape] * 4 + [jax.ShapeDtypeStruct((mine, pairs, 2, patches), F32)],
        scratch_shapes=[pltpu.VMEM((2 * pairs, HEAD_DIM + 16, patches), MXB)],
        compiler_params=params(),
    )(x_frames, modes, spatial_proj, widen(spatial_bias))
    attn_patches = to_patches(attn_frames)

    slope = jnp.tan((timesteps.astype(F32) / TSTEPS + 0.008) / 1.008 * (0.5 * math.pi))
    loss_weight = jnp.minimum(1.0, 5.0 * slope * slope).reshape(1, 1)
    count = frames * TILE
    place = jnp.arange(count) % TILE
    mask = jnp.where(place[:, None] == place[None, :], 0.0, -1e30).astype(F32)
    tile_spec = pl.BlockSpec((frames, TILE, width), lambda i: (0, i, 0))
    small = (
        loss_weight * jnp.ones((1, width), F32), modes, mask,
        spatial_out, spatial_out.T, spatial_out_bias[None, :],
        temporal_proj, temporal_proj.T, widen(temporal_bias),
        temporal_out, temporal_out.T, temporal_out_bias[None, :],
        hidden_in, hidden_in.T, hidden_in_bias[None, :],
        hidden_out, hidden_out.T, hidden_out_bias[None, :],
    )
    sums_shapes = [
        (width, width), (width, 3 * width), (width, width), (width, hidden), (width, hidden),
        (12, 8, width), (8, 3 * width), (8, hidden),
    ]
    out_shapes = [
        jax.ShapeDtypeStruct((frames, stripe, width), MXB),
        jax.ShapeDtypeStruct((frames, stripe, width), F32),
        jax.ShapeDtypeStruct((frames, stripe, width), MXB),
    ] + [jax.ShapeDtypeStruct(s, F32) for s in sums_shapes]
    (
        block_out, g1, da_patches, grad_so, grad_t, grad_to, grad_in, grad_out_turned, sums, t_sums, in_sums,
    ) = pl.pallas_call(
        middle,
        grid=(stripe // TILE,),
        in_specs=[tile_spec] * 3 + [whole_spec(a.shape) for a in small],
        out_specs=[tile_spec] * 3 + [acc_spec(s) for s in sums_shapes],
        out_shape=out_shapes,
        compiler_params=params(),
    )(x_patches, attn_patches, out_grad[0], *small)
    da_frames = to_frames(da_patches)

    sum_shapes = [(width, 3 * width), (2, 8, width), (8, 3 * width)]
    dx_frames, grad_sp, sp_sums, sp_bias_sums = pl.pallas_call(
        partial(spatial_backward, rows=256, block=min(1024, patches), part=512),
        grid=(mine,),
        in_specs=[frame_spec] * 5 + [log_spec, frame_spec, whole_spec((9, width)), whole_spec((3 * width, width))],
        out_specs=[frame_spec] + [acc_spec(s) for s in sum_shapes],
        out_shape=[frame_shape] + [jax.ShapeDtypeStruct(s, F32) for s in sum_shapes],
        scratch_shapes=[
            pltpu.VMEM((patches, 3 * width), MXB),
            pltpu.VMEM((pairs, 2, patches), F32),
            pltpu.VMEM((patches, 2 * HEAD_DIM), F32),
            pltpu.VMEM((patches, 2 * HEAD_DIM), F32),
        ],
        compiler_params=params(),
    )(da_frames, attn_frames, queries, keys, values, logs, x_frames, modes, spatial_proj.T)
    input_grad = (g1 + to_patches(dx_frames).astype(F32)).astype(MXB)

    clip_at = lax.axis_index("clip")
    clips = lax.axis_size("clip")
    vector = jnp.sum(sums, axis=1)
    sp_vector = jnp.sum(sp_sums, axis=1)
    grad_modes = jnp.concatenate([sp_vector, vector[2:9]], axis=0).reshape(1, 9 * width)
    mine_only = (jnp.arange(clips) == clip_at)[:, None]
    first_on_sp = (lax.axis_index("sp") == 0).astype(F32)
    early = lax.psum((grad_so, grad_t, grad_to, grad_in, grad_out_turned), ("clip", "sp"))
    sp_bias = jnp.sum(sp_bias_sums, axis=0)
    t_bias = jnp.sum(t_sums, axis=0)
    pieces = (
        jnp.where(mine_only, grad_modes, 0.0),
        jnp.where(mine_only, cond_act.astype(F32) * first_on_sp, 0.0),
        sp_bias,
        t_bias,
        jnp.sum(in_sums, axis=0),
        vector[9:12],
    )
    flat = jnp.concatenate([p.reshape(-1) for p in pieces])
    flat, grad_sp = lax.psum((flat, grad_sp), ("clip", "sp"))
    found = []
    start = 0
    for piece in pieces:
        found.append(flat[start : start + piece.size].reshape(piece.shape))
        start += piece.size
    all_modes, all_cond, sp_bias, t_bias, in_bias, out_biases = found
    grad_ada_weight = jnp.dot(all_cond.T, all_modes, precision=lax.Precision.HIGHEST)
    grad_ada_bias = jnp.sum(all_modes, axis=0)
    return (
        block_out[None],
        input_grad[None],
        grad_ada_weight,
        grad_ada_bias,
        grad_sp,
        jnp.concatenate([sp_bias[:width], sp_bias[2 * width :]]),
        early[0],
        out_biases[0],
        early[1],
        jnp.concatenate([t_bias[:width], t_bias[2 * width :]]),
        early[2],
        out_biases[1],
        early[3],
        in_bias,
        early[4].T,
        out_biases[2],
    )


def chosen(tokens, *others):
    _, frames, stripe, _ = tokens.shape
    if tokens.shape[0] == 1 and frames % lax.axis_size("sp") == 0 and stripe % TILE == 0:
        return fast_body(tokens, *others)
    return body(tokens, *others)


def solution(mesh):
    return jax.shard_map(
        chosen,
        mesh=mesh,
        in_specs=(
            P("clip", None, "sp", None),
            P("clip", None),
            P("clip"),
            P("clip", None, "sp", None),
            P(),
            P(),
            P(),
            P(),
            P(),
            P(),
            P(),
            P(),
            P(),
            P(),
            P(),
            P(),
            P(),
            P(),
        ),
        out_specs=(
            P("clip", None, "sp", None),
            P("clip", None, "sp", None),
            P(),
            P(),
            P(),
            P(),
            P(),
            P(),
            P(),
            P(),
            P(),
            P(),
            P(),
            P(),
            P(),
            P(),
        ),
        check_vma=False,
    )
```

```python
from functools import partial, reduce
import math

import jax
import jax.numpy as jnp
from jax import lax
from jax.experimental import pallas as pl
from jax.experimental.pallas import tpu as pltpu
from jax.sharding import PartitionSpec as P

HEADS = 6
HEAD_DIM = 64
FRAME_BLOCK = 8
TSTEPS = 1000
GELU_RATE = math.sqrt(2.0 / math.pi)


def modulate(field, shift, scale):
    centred = field - jnp.mean(field, axis=-1, keepdims=True)
    normed = centred * lax.rsqrt(jnp.mean(centred * centred, axis=-1, keepdims=True) + 1e-06)
    return normed * (1.0 + scale) + shift


def loss_weights(timesteps):
    phase = (timesteps.astype(jnp.float32) / TSTEPS + 0.008) / 1.008 * (0.5 * math.pi)
    slope = jnp.tan(phase)
    return jnp.minimum(1.0, 5.0 * slope * slope)


def split_heads(array):
    return array.reshape(array.shape[:-1] + (HEADS, HEAD_DIM))


def join_heads(array):
    return array.reshape(array.shape[:-2] + (HEADS * HEAD_DIM,))


def attend(queries, keys, values):
    scores = jnp.einsum(
        "csqhe,cskhe->cshqk", queries, keys, preferred_element_type=jnp.float32
    ) * HEAD_DIM ** (-0.5)
    row_max = jnp.max(scores, axis=-1, keepdims=True)
    exponent = jnp.exp(scores - row_max)
    total = jnp.sum(exponent, axis=-1, keepdims=True)
    soft_weights = (exponent / total).astype(jnp.bfloat16)
    mixed = jnp.einsum(
        "cshqk,cskhe->csqhe", soft_weights, values, preferred_element_type=jnp.float32
    )
    return (mixed, row_max[..., 0] + jnp.log(total[..., 0]))


def probabilities(queries, keys, values, grads, log_total):
    scores = jnp.einsum(
        "csqhe,cskhe->cshqk", queries, keys, preferred_element_type=jnp.float32
    ) * HEAD_DIM ** (-0.5)
    soft_weights = jnp.exp(scores - log_total[..., None])
    grad_weights = jnp.einsum(
        "csqhe,cskhe->cshqk", grads, values, preferred_element_type=jnp.float32
    )
    return (soft_weights, grad_weights)


def query_pass(queries, keys, values, grads, log_total):
    soft_weights, grad_weights = probabilities(queries, keys, values, grads, log_total)
    delta = jnp.sum(soft_weights * grad_weights, axis=-1)
    grad_scores = (soft_weights * (grad_weights - delta[..., None]) * HEAD_DIM ** (-0.5)).astype(
        jnp.bfloat16
    )
    grad_queries = jnp.einsum(
        "cshqk,cskhe->csqhe", grad_scores, keys, preferred_element_type=jnp.float32
    )
    return (grad_queries, delta)


def key_pass(queries, keys, values, grads, log_total, delta):
    soft_weights, grad_weights = probabilities(queries, keys, values, grads, log_total)
    grad_scores = (soft_weights * (grad_weights - delta[..., None]) * HEAD_DIM ** (-0.5)).astype(
        jnp.bfloat16
    )
    grad_keys = jnp.einsum(
        "cshqk,csqhe->cskhe", grad_scores, queries, preferred_element_type=jnp.float32
    )
    grad_values = jnp.einsum(
        "cshqk,csqhe->cskhe",
        soft_weights.astype(jnp.bfloat16),
        grads,
        preferred_element_type=jnp.float32,
    )
    return jnp.concatenate([join_heads(grad_keys), join_heads(grad_values)], axis=-1)


def column_sums(array):
    return jnp.sum(array.astype(jnp.float32), axis=(0, 1, 2))


def body(
    tokens,
    conditioning,
    timesteps,
    out_grad,
    ada_weight,
    ada_bias,
    spatial_proj,
    spatial_bias,
    spatial_out,
    spatial_out_bias,
    temporal_proj,
    temporal_bias,
    temporal_out,
    temporal_out_bias,
    hidden_in,
    hidden_in_bias,
    hidden_out,
    hidden_out_bias,
):
    clips, frames, stripe, width = tokens.shape
    blocks = frames // FRAME_BLOCK
    scale_factor = HEAD_DIM ** (-0.5)
    field = tokens.astype(jnp.float32)
    cond_act = jax.nn.silu(conditioning.astype(jnp.float32)).astype(jnp.bfloat16)
    modes = jnp.dot(cond_act, ada_weight, preferred_element_type=jnp.float32) + ada_bias
    modes = modes.reshape(clips, 9, 1, 1, width)
    hidden_one, back_one = jax.vjp(modulate, field, modes[:, 0], modes[:, 1])
    hidden_one = hidden_one.astype(jnp.bfloat16)
    query_mix = jnp.einsum(
        "cfpd,de->cfpe", hidden_one, spatial_proj[:, :width], preferred_element_type=jnp.float32
    )
    queries = (query_mix + spatial_bias[:width]).astype(jnp.bfloat16)
    keyval_mix = jnp.einsum(
        "cfpd,de->cfpe", hidden_one, spatial_proj[:, width:], preferred_element_type=jnp.float32
    )
    keyval_bias = jnp.concatenate([jnp.zeros((width,), jnp.float32), spatial_bias[width:]])
    keyvals = (keyval_mix + keyval_bias).astype(jnp.bfloat16)
    query_heads = split_heads(queries)
    mixed_parts = []
    log_parts = []
    for index in range(blocks):
        first = index * FRAME_BLOCK
        whole = lax.all_gather(keyvals[:, first : first + FRAME_BLOCK], "sp", axis=2, tiled=True)
        mixed_part, log_part = attend(
            query_heads[:, first : first + FRAME_BLOCK],
            split_heads(whole[..., :width]),
            split_heads(whole[..., width:]),
        )
        mixed_parts.append(join_heads(mixed_part))
        log_parts.append(log_part)
    attn_one = jnp.concatenate(mixed_parts, axis=1).astype(jnp.bfloat16)
    spatial_log = jnp.concatenate(log_parts, axis=1)
    branch_one = (
        jnp.einsum("cfpd,de->cfpe", attn_one, spatial_out, preferred_element_type=jnp.float32)
        + spatial_out_bias
    )
    field_one = field + modes[:, 2] * branch_one
    hidden_two, back_two = jax.vjp(modulate, field_one, modes[:, 3], modes[:, 4])
    hidden_two = hidden_two.astype(jnp.bfloat16)
    time_mix = jnp.einsum(
        "cfpd,de->cfpe", hidden_two, temporal_proj, preferred_element_type=jnp.float32
    )
    time_queries = split_heads((time_mix[..., :width] + temporal_bias[:width]).astype(jnp.bfloat16))
    time_keys = split_heads(time_mix[..., width : 2 * width].astype(jnp.bfloat16))
    time_values = split_heads(
        (time_mix[..., 2 * width :] + temporal_bias[width:]).astype(jnp.bfloat16)
    )
    time_scores = (
        jnp.einsum(
            "cfphe,cgphe->cphfg", time_queries, time_keys, preferred_element_type=jnp.float32
        )
        * scale_factor
    )
    time_max = jnp.max(time_scores, axis=-1, keepdims=True)
    time_exponent = jnp.exp(time_scores - time_max)
    time_weights = time_exponent / jnp.sum(time_exponent, axis=-1, keepdims=True)
    time_rounded = time_weights.astype(jnp.bfloat16)
    attn_two = join_heads(
        jnp.einsum(
            "cphfg,cgphe->cfphe", time_rounded, time_values, preferred_element_type=jnp.float32
        )
    ).astype(jnp.bfloat16)
    branch_two = (
        jnp.einsum("cfpd,de->cfpe", attn_two, temporal_out, preferred_element_type=jnp.float32)
        + temporal_out_bias
    )
    field_two = field_one + modes[:, 5] * branch_two
    hidden_three, back_three = jax.vjp(modulate, field_two, modes[:, 6], modes[:, 7])
    hidden_three = hidden_three.astype(jnp.bfloat16)
    inner = (
        jnp.einsum("cfpd,dk->cfpk", hidden_three, hidden_in, preferred_element_type=jnp.float32)
        + hidden_in_bias
    )
    active, gelu_back = jax.vjp(partial(jax.nn.gelu, approximate=True), inner)
    active = active.astype(jnp.bfloat16)
    branch_three = (
        jnp.einsum("cfpk,kd->cfpd", active, hidden_out, preferred_element_type=jnp.float32)
        + hidden_out_bias
    )
    block_out = (field_two + modes[:, 8] * branch_three).astype(jnp.bfloat16)
    weights = loss_weights(timesteps)
    grad_field = out_grad.astype(jnp.float32) * weights[:, None, None, None]
    grad_gate_three = jnp.sum(grad_field * branch_three, axis=(1, 2))
    grad_branch = (modes[:, 8] * grad_field).astype(jnp.bfloat16)
    grad_hidden_out = jnp.einsum(
        "cfpk,cfpd->kd", active, grad_branch, preferred_element_type=jnp.float32
    )
    grad_hidden_out_bias = column_sums(grad_branch)
    grad_active = jnp.einsum(
        "cfpd,kd->cfpk", grad_branch, hidden_out, preferred_element_type=jnp.float32
    )
    grad_inner = gelu_back(grad_active)[0].astype(jnp.bfloat16)
    grad_hidden_in = jnp.einsum(
        "cfpd,cfpk->dk", hidden_three, grad_inner, preferred_element_type=jnp.float32
    )
    grad_hidden_in_bias = column_sums(grad_inner)
    grad_hidden = jnp.einsum(
        "cfpk,dk->cfpd", grad_inner, hidden_in, preferred_element_type=jnp.float32
    )
    grad_input, grad_shift_three, grad_scale_three = back_three(grad_hidden)
    grad_field = grad_field + grad_input
    grad_gate_two = jnp.sum(grad_field * branch_two, axis=(1, 2))
    grad_branch = (modes[:, 5] * grad_field).astype(jnp.bfloat16)
    grad_temporal_out = jnp.einsum(
        "cfpd,cfpe->de", attn_two, grad_branch, preferred_element_type=jnp.float32
    )
    grad_temporal_out_bias = column_sums(grad_branch)
    grad_attn = split_heads(
        jnp.einsum(
            "cfpe,de->cfpd", grad_branch, temporal_out, preferred_element_type=jnp.float32
        ).astype(jnp.bfloat16)
    )
    grad_weights = jnp.einsum(
        "cfphe,cgphe->cphfg", grad_attn, time_values, preferred_element_type=jnp.float32
    )
    delta = jnp.sum(time_weights * grad_weights, axis=-1, keepdims=True)
    grad_scores = (time_weights * (grad_weights - delta) * scale_factor).astype(jnp.bfloat16)
    grad_time_queries = jnp.einsum(
        "cphfg,cgphe->cfphe", grad_scores, time_keys, preferred_element_type=jnp.float32
    )
    grad_time_keys = jnp.einsum(
        "cphfg,cfphe->cgphe", grad_scores, time_queries, preferred_element_type=jnp.float32
    )
    grad_time_values = jnp.einsum(
        "cphfg,cfphe->cgphe", time_rounded, grad_attn, preferred_element_type=jnp.float32
    )
    grad_time_mix = jnp.concatenate(
        [join_heads(grad_time_queries), join_heads(grad_time_keys), join_heads(grad_time_values)],
        axis=-1,
    ).astype(jnp.bfloat16)
    grad_temporal_proj = jnp.einsum(
        "cfpd,cfpe->de", hidden_two, grad_time_mix, preferred_element_type=jnp.float32
    )
    grad_temporal_bias = jnp.concatenate(
        [column_sums(grad_time_mix[..., :width]), column_sums(grad_time_mix[..., 2 * width :])]
    )
    grad_hidden = jnp.einsum(
        "cfpe,de->cfpd", grad_time_mix, temporal_proj, preferred_element_type=jnp.float32
    )
    grad_input, grad_shift_two, grad_scale_two = back_two(grad_hidden)
    grad_field = grad_field + grad_input
    grad_gate_one = jnp.sum(grad_field * branch_one, axis=(1, 2))
    grad_branch = (modes[:, 2] * grad_field).astype(jnp.bfloat16)
    grad_spatial_out = jnp.einsum(
        "cfpd,cfpe->de", attn_one, grad_branch, preferred_element_type=jnp.float32
    )
    grad_spatial_out_bias = column_sums(grad_branch)
    grad_attn = jnp.einsum(
        "cfpe,de->cfpd", grad_branch, spatial_out, preferred_element_type=jnp.float32
    ).astype(jnp.bfloat16)
    query_parts = []
    key_parts = []
    for index in range(blocks):
        first = index * FRAME_BLOCK
        whole = lax.all_gather(keyvals[:, first : first + FRAME_BLOCK], "sp", axis=2, tiled=True)
        piece = query_heads[:, first : first + FRAME_BLOCK]
        grad_piece = split_heads(grad_attn[:, first : first + FRAME_BLOCK])
        log_piece = spatial_log[:, first : first + FRAME_BLOCK]
        grad_query_part, delta = query_pass(
            piece,
            split_heads(whole[..., :width]),
            split_heads(whole[..., width:]),
            grad_piece,
            log_piece,
        )
        term = key_pass(
            piece,
            split_heads(whole[..., :width]),
            split_heads(whole[..., width:]),
            grad_piece,
            log_piece,
            delta,
        )
        owned = lax.psum_scatter(
            jnp.transpose(term, (2, 0, 1, 3)).astype(jnp.bfloat16),
            "sp",
            scatter_dimension=0,
            tiled=True,
        ).astype(jnp.float32)
        query_parts.append(join_heads(grad_query_part))
        key_parts.append(jnp.transpose(owned, (1, 2, 0, 3)))
    grad_queries = jnp.concatenate(query_parts, axis=1)
    grad_keyvals = jnp.concatenate(key_parts, axis=1)
    grad_queries = grad_queries.astype(jnp.bfloat16)
    grad_keyvals = grad_keyvals.astype(jnp.bfloat16)
    grad_spatial_proj = jnp.concatenate(
        [
            jnp.einsum(
                "cfpd,cfpe->de", hidden_one, grad_queries, preferred_element_type=jnp.float32
            ),
            jnp.einsum(
                "cfpd,cfpe->de", hidden_one, grad_keyvals, preferred_element_type=jnp.float32
            ),
        ],
        axis=1,
    )
    grad_spatial_bias = jnp.concatenate(
        [column_sums(grad_queries), column_sums(grad_keyvals[..., width:])]
    )
    grad_hidden = jnp.einsum(
        "cfpe,de->cfpd", grad_queries, spatial_proj[:, :width], preferred_element_type=jnp.float32
    )
    grad_hidden = grad_hidden + jnp.einsum(
        "cfpe,de->cfpd", grad_keyvals, spatial_proj[:, width:], preferred_element_type=jnp.float32
    )
    grad_input, grad_shift_one, grad_scale_one = back_one(grad_hidden)
    input_grad = (grad_field + grad_input).astype(jnp.bfloat16)
    grad_modes = jnp.stack(
        [
            grad_shift_one.reshape(clips, width),
            grad_scale_one.reshape(clips, width),
            grad_gate_one,
            grad_shift_two.reshape(clips, width),
            grad_scale_two.reshape(clips, width),
            grad_gate_two,
            grad_shift_three.reshape(clips, width),
            grad_scale_three.reshape(clips, width),
            grad_gate_three,
        ],
        axis=1,
    ).reshape(clips, 9 * width)
    grad_ada_weight = jnp.dot(
        cond_act.astype(jnp.float32).T, grad_modes, precision=lax.Precision.HIGHEST
    )
    grad_ada_bias = jnp.sum(grad_modes, axis=0)
    summed = lax.psum(
        (
            grad_ada_weight,
            grad_ada_bias,
            grad_spatial_proj,
            grad_spatial_bias,
            grad_spatial_out,
            grad_spatial_out_bias,
            grad_temporal_proj,
            grad_temporal_bias,
            grad_temporal_out,
            grad_temporal_out_bias,
            grad_hidden_in,
            grad_hidden_in_bias,
            grad_hidden_out,
            grad_hidden_out_bias,
        ),
        ("clip", "sp"),
    )
    return (
        block_out,
        input_grad,
        summed[0],
        summed[1],
        summed[2],
        summed[3],
        summed[4],
        summed[5],
        summed[6],
        summed[7],
        summed[8],
        summed[9],
        summed[10],
        summed[11],
        summed[12],
        summed[13],
    )


MXB = jnp.bfloat16
F32 = jnp.float32
TILE = 16
VMEM_BYTES = 60 * 2**20


def dot(left, right):
    return jnp.dot(left, right, preferred_element_type=F32)


def dot_nt(left, right):
    return lax.dot_general(left, right, (((1,), (1,)), ((), ())), preferred_element_type=F32)


def dot_tn(left, right):
    return lax.dot_general(left, right, (((0,), (0,)), ((), ())), preferred_element_type=F32)


def turned(array):
    return array.astype(F32).T.astype(array.dtype)


def normalise(field):
    centred = field - jnp.mean(field, axis=-1, keepdims=True)
    rate = lax.rsqrt(jnp.mean(centred * centred, axis=-1, keepdims=True) + 1e-06)
    return centred * rate, rate


def normalise_back(grad, normed, rate, scale):
    inner = grad * (1.0 + scale)
    mean = jnp.mean(inner, axis=-1, keepdims=True)
    slope = jnp.mean(inner * normed, axis=-1, keepdims=True)
    return rate * (inner - mean - normed * slope)


def eight_rows(array):
    return jnp.sum(array.reshape(array.shape[0] // 8, 8, array.shape[1]), axis=0)


def low_lanes():
    return lax.broadcasted_iota(jnp.int32, (1, 2 * HEAD_DIM), 1) < HEAD_DIM


def halves(pair):
    low = low_lanes()
    zero = jnp.zeros_like(pair)
    return jnp.where(low, pair, zero), jnp.where(low, zero, pair)


def others(count):
    me = lax.axis_index("sp")
    return me, [(step, lax.rem(me + step, count), lax.rem(me + count - step, count)) for step in range(1, count)]


def send(source, target, send_sem, recv_sem, peer):
    return pltpu.make_async_remote_copy(
        src_ref=source, dst_ref=target, send_sem=send_sem, recv_sem=recv_sem,
        device_id={"sp": peer}, device_id_type=pl.DeviceIdType.MESH,
    )


def greet(peers):
    barrier = pltpu.get_barrier_semaphore()
    for _, peer, _ in peers:
        pl.semaphore_signal(barrier, inc=1, device_id={"sp": peer}, device_id_type=pl.DeviceIdType.MESH)


def greeted(peers):
    pl.semaphore_wait(pltpu.get_barrier_semaphore(), len(peers))


def spatial_forward(
    tokens_ref, modes_ref, proj_ref, bias_ref,
    x_out, q_out, k_out, v_out, attn_out, patches_out, log_ref,
    x_ref, q_ref, k_ref, v_ref, attn_ref, turned_ref,
    x_send, x_recv, x_own, a_send, a_recv, a_own, save_sem,
    rows, block, part, count,
):
    mine, tokens, width = x_ref.shape
    stripe = tokens // count
    pairs = width // (2 * HEAD_DIM)
    near = block // stripe
    blocks = tokens // block
    me, peers = others(count)
    shift = modes_ref[0:1, :]
    scale = modes_ref[1:2, :]

    def x_copy(frame, step, peer):
        return send(
            tokens_ref.at[peer * mine + frame],
            x_ref.at[frame, pl.ds(pl.multiple_of(me * stripe, stripe), stripe), :],
            x_send.at[frame, step], x_recv.at[frame, step], peer,
        )

    def x_keep(frame):
        return pltpu.make_async_copy(
            tokens_ref.at[me * mine + frame],
            x_ref.at[frame, pl.ds(pl.multiple_of(me * stripe, stripe), stripe), :],
            x_own.at[frame],
        )

    def saves(frame):
        return [
            pltpu.make_async_copy(held.at[frame], kept.at[frame], save_sem.at[place, frame])
            for place, (held, kept) in enumerate(
                ((x_ref, x_out), (q_ref, q_out), (k_ref, k_out), (v_ref, v_out), (attn_ref, attn_out))
            )
        ]

    def a_copy(frame, pair, peer):
        lanes = pl.ds(pl.multiple_of(pair * 2 * HEAD_DIM, 2 * HEAD_DIM), 2 * HEAD_DIM)
        return send(
            attn_ref.at[frame, pl.ds(pl.multiple_of(peer * stripe, stripe), stripe), lanes],
            patches_out.at[me * mine + frame, :, lanes],
            a_send.at[frame, pair, peer], a_recv.at[frame, pair, me], peer,
        )

    def a_landed(frame, pair, peer):
        lanes = pl.ds(pl.multiple_of(pair * 2 * HEAD_DIM, 2 * HEAD_DIM), 2 * HEAD_DIM)
        return send(
            attn_ref.at[frame, pl.ds(pl.multiple_of(peer * stripe, stripe), stripe), lanes],
            patches_out.at[peer * mine + frame, :, lanes],
            a_send.at[frame, pair, peer], a_recv.at[frame, pair, peer], peer,
        )

    def a_keep(frame, pair):
        lanes = pl.ds(pl.multiple_of(pair * 2 * HEAD_DIM, 2 * HEAD_DIM), 2 * HEAD_DIM)
        return pltpu.make_async_copy(
            attn_ref.at[frame, pl.ds(pl.multiple_of(me * stripe, stripe), stripe), lanes],
            patches_out.at[me * mine + frame, :, lanes],
            a_own.at[frame, pair],
        )

    greet(peers)
    greeted(peers)
    order = sorted(range(1, count), key=lambda step: -min(step, count - step))
    for frame in range(mine):
        for step in order:
            x_copy(frame, step, lax.rem(me + step, count)).start()
        x_keep(frame).start()
    turned_ref[:, HEAD_DIM:, :] = jnp.ones((2 * pairs, turned_ref.shape[1] - HEAD_DIM, tokens), MXB)

    def one_frame(frame, carry):
        x_keep(frame).wait()
        for step, _, source in peers:
            x_copy(frame, step, source).wait_recv()
        saves(frame)[0].start()

        def project(index, carry):
            at = pl.ds(pl.multiple_of(index * rows, rows), rows)
            normed, _ = normalise(x_ref[frame, at, :].astype(F32))
            hidden = (normed * (1.0 + scale) + shift).astype(MXB)
            mixed = dot(hidden, proj_ref[...]) + bias_ref[...]
            q_ref[frame, at, :] = mixed[:, :width].astype(MXB)
            k_ref[frame, at, :] = mixed[:, width : 2 * width].astype(MXB)
            value = mixed[:, 2 * width :].astype(MXB)
            v_ref[frame, at, :] = value
            across = turned(value)
            for head in range(2 * pairs):
                turned_ref[head, :HEAD_DIM, at] = across[head * HEAD_DIM : (head + 1) * HEAD_DIM]
            return carry

        lax.fori_loop(0, tokens // rows, project, 0)
        for copy in saves(frame)[1:4]:
            copy.start()

        def attend_block(index, carry):
            pair = lax.rem(index, pairs)
            chunk = lax.rem(lax.div(index, pairs) + lax.div(me, near) + 1, blocks)
            at = pl.ds(pl.multiple_of(chunk * block, block), block)
            lanes = pl.ds(pl.multiple_of(pair * 2 * HEAD_DIM, 2 * HEAD_DIM), 2 * HEAD_DIM)
            scores = []
            tops = []
            for query in halves(q_ref[frame, at, lanes] * MXB(HEAD_DIM**-0.5)):
                each = [
                    dot_nt(k_ref[frame, first : first + part, lanes], query)
                    for first in range(0, tokens, part)
                ]
                top = [jnp.max(s.reshape(part // 8, 8, block), axis=0) for s in each]
                scores.append(each)
                tops.append(jnp.max(reduce(jnp.maximum, top), axis=0, keepdims=True))
            mixed = []
            for half in range(2):
                total = jnp.zeros((turned_ref.shape[1], block), F32)
                for number, s in enumerate(scores[half]):
                    weights = jnp.exp(s - tops[half]).astype(MXB)
                    values = turned_ref[2 * pair + half, :, number * part : (number + 1) * part]
                    total = total + dot(values, weights)
                mass = total[HEAD_DIM : HEAD_DIM + 1]
                log_ref[frame, pair, half : half + 1, at] = tops[half] + jnp.log(mass)
                mixed.append(total[:HEAD_DIM] / mass)
            attn_ref[frame, at, lanes] = jnp.concatenate(mixed, axis=0).T.astype(MXB)
            for place in range(near):
                peer = chunk * near + place

                @pl.when(peer != me)
                def _():
                    a_copy(frame, pair, peer).start()

                @pl.when(peer == me)
                def _():
                    a_keep(frame, pair).start()

            return carry

        lax.fori_loop(0, pairs * blocks, attend_block, 0)
        saves(frame)[4].start()
        return carry

    lax.fori_loop(0, mine, one_frame, 0)

    for frame in range(mine):
        for copy in saves(frame):
            copy.wait()
        for step, peer, _ in peers:
            x_copy(frame, step, peer).wait_send()
        for pair in range(pairs):
            a_keep(frame, pair).wait()
            for _, peer, _ in peers:
                a_copy(frame, pair, peer).wait_send()
                a_landed(frame, pair, peer).wait_recv()


def spatial_backward(
    da_ref, attn_ref, q_ref, k_ref, v_ref, log_ref, x_ref, modes_ref, proj_turned_ref,
    patches_out, grad_proj_ref, sums_ref, bias_sums_ref,
    dx_ref, mix_ref, delta_ref, dk_ref, dv_ref, send_sem, recv_sem, own_sem, rows, block, part, count,
):
    tokens, width = x_ref.shape[1:]
    mine = dx_ref.shape[0]
    stripe = tokens // count
    frame = pl.program_id(0)
    me, peers = others(count)

    def dx_copy(frame, peer):
        return send(
            dx_ref.at[frame, pl.ds(pl.multiple_of(peer * stripe, stripe), stripe), :],
            patches_out.at[me * mine + frame], send_sem.at[frame, peer], recv_sem.at[frame, me], peer,
        )

    def dx_landed(frame, peer):
        return send(
            dx_ref.at[frame, pl.ds(pl.multiple_of(peer * stripe, stripe), stripe), :],
            patches_out.at[peer * mine + frame], send_sem.at[frame, peer], recv_sem.at[frame, peer], peer,
        )

    def dx_keep(frame):
        return pltpu.make_async_copy(
            dx_ref.at[frame, pl.ds(pl.multiple_of(me * stripe, stripe), stripe), :],
            patches_out.at[me * mine + frame], own_sem.at[frame],
        )

    @pl.when(frame == 0)
    def _():
        greet(peers)

    pairs = width // (2 * HEAD_DIM)
    scale_factor = HEAD_DIM**-0.5

    @pl.when(frame == 0)
    def _():
        grad_proj_ref[...] = jnp.zeros_like(grad_proj_ref)
        sums_ref[...] = jnp.zeros_like(sums_ref)
        bias_sums_ref[...] = jnp.zeros_like(bias_sums_ref)

    head_of = lax.broadcasted_iota(jnp.int32, (8, width), 1) // HEAD_DIM
    picks = jnp.where(head_of == lax.broadcasted_iota(jnp.int32, (8, width), 0), 1.0, 0.0).astype(MXB)

    def deltas(index, carry):
        at = pl.ds(pl.multiple_of(index * rows, rows), rows)
        product = da_ref[0, at, :].astype(F32) * attn_ref[0, at, :].astype(F32)
        high = product.astype(MXB)
        rest = (product - high.astype(F32)).astype(MXB)
        summed = dot_nt(picks, high) + dot_nt(picks, rest)
        for pair in range(pairs):
            delta_ref[pair, 0:2, at] = summed[2 * pair : 2 * pair + 2]
        return carry

    lax.fori_loop(0, tokens // rows, deltas, 0)

    for pair in range(pairs):
        first_lane = 2 * HEAD_DIM * pair
        lanes = slice(first_lane, first_lane + 2 * HEAD_DIM)
        dk_ref[...] = jnp.zeros_like(dk_ref)
        dv_ref[...] = jnp.zeros_like(dv_ref)
        keys_across = turned(k_ref[0, :, lanes])

        def queries_block(index, carry, pair=pair, lanes=lanes, keys_across=keys_across):
            at = pl.ds(pl.multiple_of(index * block, block), block)
            query = halves(q_ref[0, at, lanes] * MXB(scale_factor))
            grad = halves(da_ref[0, at, lanes])
            query_both = jnp.concatenate(query, axis=0)
            grad_both = jnp.concatenate(grad, axis=0)
            grad_query = [jnp.zeros((HEAD_DIM, block), F32), jnp.zeros((HEAD_DIM, block), F32)]
            for first in range(0, tokens, part):
                span = slice(first, first + part)
                keys = k_ref[0, span, lanes]
                values = v_ref[0, span, lanes]
                weights = []
                grad_scores = []
                for half in range(2):
                    scores = dot_nt(keys, query[half])
                    exact = jnp.exp(scores - log_ref[0, pair, half : half + 1, at])
                    grad_weights = dot_nt(values, grad[half])
                    term = (exact * (grad_weights - delta_ref[pair, half : half + 1, at])).astype(MXB)
                    weights.append(exact.astype(MXB))
                    grad_scores.append(term)
                    grad_query[half] = grad_query[half] + dot(
                        keys_across[half * HEAD_DIM : (half + 1) * HEAD_DIM, span], term
                    )
                dv_ref[span, :] += dot(jnp.concatenate(weights, axis=1), grad_both)
                dk_ref[span, :] += dot(jnp.concatenate(grad_scores, axis=1), query_both)
            mix_ref[at, lanes] = (jnp.concatenate(grad_query, axis=0).T * scale_factor).astype(MXB)
            return carry

        lax.fori_loop(0, tokens // block, queries_block, 0)
        mix_ref[:, width + first_lane : width + first_lane + 2 * HEAD_DIM] = dk_ref[...].astype(MXB)
        mix_ref[:, 2 * width + first_lane : 2 * width + first_lane + 2 * HEAD_DIM] = dv_ref[...].astype(MXB)

    shift = modes_ref[0:1, :]
    scale = modes_ref[1:2, :]

    @pl.when(frame == 0)
    def _():
        greeted(peers)

    def finish(index, carry):
        peer = lax.rem(me + count // 2 + index, count)
        at = pl.ds(pl.multiple_of(peer * stripe, stripe), stripe)
        normed, rate = normalise(x_ref[0, at, :].astype(F32))
        hidden = (normed * (1.0 + scale) + shift).astype(MXB)
        grad_mix = mix_ref[at, :]
        grad_proj_ref[...] += dot_tn(hidden, grad_mix)
        bias_sums_ref[...] += eight_rows(grad_mix.astype(F32))
        grad_hidden = dot(grad_mix, proj_turned_ref[...])
        sums_ref[0] += eight_rows(grad_hidden)
        sums_ref[1] += eight_rows(grad_hidden * normed)
        dx_ref[frame, at, :] = normalise_back(grad_hidden, normed, rate, scale).astype(MXB)

        @pl.when(peer != me)
        def _():
            dx_copy(frame, peer).start()

        @pl.when(peer == me)
        def _():
            dx_keep(frame).start()

        return carry

    lax.fori_loop(0, count, finish, 0)

    @pl.when(frame == mine - 1)
    def _():
        for each in range(mine):
            dx_keep(each).wait()
            for _, peer, _ in peers:
                dx_copy(each, peer).wait_send()
                dx_landed(each, peer).wait_recv()


def middle(
    x_ref, attn_ref, og_ref, weight_ref, modes_ref, mask_ref,
    so_ref, so_turned_ref, so_bias_ref, t_ref, t_turned_ref, t_bias_ref, to_ref, to_turned_ref, to_bias_ref,
    in_ref, in_turned_ref, in_bias_ref, out_ref, out_turned_ref, out_bias_ref,
    block_ref, g1_ref, da_out,
    grad_so_ref, grad_t_ref, grad_to_ref, grad_in_ref, grad_out_ref, sums_ref, t_sums_ref, in_sums_ref,
    da_ref, send_sem, recv_sem, own_sem, peer_count,
):
    frames, tile, width = x_ref.shape
    count = frames * tile
    pairs = width // (2 * HEAD_DIM)
    scale_factor = HEAD_DIM**-0.5
    mine = frames // peer_count
    steps = pl.num_programs(0)
    stripe = da_out.shape[1] // peer_count
    at_step = pl.program_id(0)
    me, peers = others(peer_count)

    def da_copy(at_step, step, peer):
        first = pl.multiple_of(me * stripe + at_step * tile, tile)
        slot = lax.rem(at_step, 2)
        return send(
            da_ref.at[slot, pl.ds(peer * mine, mine)], da_out.at[:, pl.ds(first, tile), :],
            send_sem.at[slot, step], recv_sem.at[step], peer,
        )

    def da_keep(at_step):
        first = pl.multiple_of(me * stripe + at_step * tile, tile)
        slot = lax.rem(at_step, 2)
        return pltpu.make_async_copy(
            da_ref.at[slot, pl.ds(me * mine, mine)], da_out.at[:, pl.ds(first, tile), :], own_sem.at[slot]
        )

    def da_landed(step, source):
        rows = da_out.at[:, pl.ds(pl.multiple_of(source * stripe, stripe), stripe), :]
        return send(rows, rows, send_sem.at[0, step], recv_sem.at[step], source)

    @pl.when(at_step == 0)
    def _():
        greet(peers)
        for ref in (grad_so_ref, grad_t_ref, grad_to_ref, grad_in_ref, grad_out_ref, sums_ref, t_sums_ref, in_sums_ref):
            ref[...] = jnp.zeros_like(ref)

    def mode(row):
        return modes_ref[row : row + 1, :]

    field = x_ref[...].reshape(count, width).astype(F32)
    attn_one = attn_ref[...].reshape(count, width)
    branch_one = dot(attn_one, so_ref[...]) + so_bias_ref[...]
    field_one = field + mode(2) * branch_one
    normed_two, rate_two = normalise(field_one)
    hidden_two = (normed_two * (1.0 + mode(4)) + mode(3)).astype(MXB)
    mixed = (dot(hidden_two, t_ref[...]) + t_bias_ref[...]).astype(MXB)
    mask = mask_ref[...]
    exact = []
    rounded = []
    queries = []
    keys_across = []
    attn_parts = []
    for pair in range(pairs):
        lanes = slice(2 * HEAD_DIM * pair, 2 * HEAD_DIM * (pair + 1))
        query = halves(mixed[:, lanes] * MXB(scale_factor))
        keys = mixed[:, width:][:, lanes]
        values_across = turned(mixed[:, 2 * width :][:, lanes])
        queries.append(query)
        keys_across.append(turned(keys))
        parts = []
        for half in range(2):
            scores = dot_nt(keys, query[half]) + mask
            exponent = jnp.exp(scores - jnp.max(scores, axis=0, keepdims=True))
            weights = exponent / jnp.sum(exponent, axis=0, keepdims=True)
            exact.append(weights)
            rounded.append(weights.astype(MXB))
            parts.append(dot(values_across[half * HEAD_DIM : (half + 1) * HEAD_DIM], rounded[-1]))
        attn_parts.append(jnp.concatenate(parts, axis=0).T.astype(MXB))
    attn_two = jnp.concatenate(attn_parts, axis=1)
    branch_two = dot(attn_two, to_ref[...]) + to_bias_ref[...]
    field_two = field_one + mode(5) * branch_two
    normed_three, rate_three = normalise(field_two)
    hidden_three = (normed_three * (1.0 + mode(7)) + mode(6)).astype(MXB)
    inner = dot(hidden_three, in_ref[...]) + in_bias_ref[...]
    square = inner * inner
    bend = jnp.tanh(inner * (GELU_RATE + GELU_RATE * 0.044715 * square))
    half_up = 0.5 + 0.5 * bend
    active = (inner * half_up).astype(MXB)
    slope = half_up + inner * (0.5 - 0.5 * bend * bend) * (GELU_RATE + 3.0 * GELU_RATE * 0.044715 * square)
    branch_three = dot(active, out_ref[...]) + out_bias_ref[...]
    block_ref[...] = (field_two + mode(8) * branch_three).astype(MXB).reshape(frames, tile, width)

    grad_field = og_ref[...].reshape(count, width).astype(F32) * weight_ref[...]
    sums_ref[8] += eight_rows(grad_field * branch_three)
    grad_branch = (mode(8) * grad_field).astype(MXB)
    grad_out_ref[...] += dot_tn(grad_branch, active)
    sums_ref[11] += eight_rows(grad_branch.astype(F32))
    grad_inner = (dot(grad_branch, out_turned_ref[...]) * slope).astype(MXB)
    grad_in_ref[...] += dot_tn(hidden_three, grad_inner)
    in_sums_ref[...] += eight_rows(grad_inner.astype(F32))
    grad_hidden = dot(grad_inner, in_turned_ref[...])
    sums_ref[6] += eight_rows(grad_hidden)
    sums_ref[7] += eight_rows(grad_hidden * normed_three)
    grad_field = grad_field + normalise_back(grad_hidden, normed_three, rate_three, mode(7))

    sums_ref[5] += eight_rows(grad_field * branch_two)
    grad_branch = (mode(5) * grad_field).astype(MXB)
    grad_to_ref[...] += dot_tn(attn_two, grad_branch)
    sums_ref[10] += eight_rows(grad_branch.astype(F32))
    grad_attn = dot(grad_branch, to_turned_ref[...]).astype(MXB)
    grad_queries = []
    grad_keys = []
    grad_values = []
    for pair in range(pairs):
        lanes = slice(2 * HEAD_DIM * pair, 2 * HEAD_DIM * (pair + 1))
        grad = halves(grad_attn[:, lanes])
        values = mixed[:, 2 * width :][:, lanes]
        grad_query = []
        terms = []
        for half in range(2):
            weights = exact[2 * pair + half]
            grad_weights = dot_nt(values, grad[half])
            delta = jnp.sum(weights * grad_weights, axis=0, keepdims=True)
            term = (weights * (grad_weights - delta)).astype(MXB)
            terms.append(term)
            grad_query.append(dot(keys_across[pair][half * HEAD_DIM : (half + 1) * HEAD_DIM], term))
        both = jnp.concatenate(terms, axis=1)
        grad_queries.append((jnp.concatenate(grad_query, axis=0).T * scale_factor).astype(MXB))
        grad_keys.append(dot(both, jnp.concatenate(queries[pair], axis=0)).astype(MXB))
        grad_values.append(
            dot(
                jnp.concatenate([rounded[2 * pair], rounded[2 * pair + 1]], axis=1),
                jnp.concatenate(grad, axis=0),
            ).astype(MXB)
        )
    grad_mix = jnp.concatenate(grad_queries + grad_keys + grad_values, axis=1)
    grad_t_ref[...] += dot_tn(hidden_two, grad_mix)
    t_sums_ref[...] += eight_rows(grad_mix.astype(F32))
    grad_hidden = dot(grad_mix, t_turned_ref[...])
    sums_ref[3] += eight_rows(grad_hidden)
    sums_ref[4] += eight_rows(grad_hidden * normed_two)
    grad_field = grad_field + normalise_back(grad_hidden, normed_two, rate_two, mode(4))

    sums_ref[2] += eight_rows(grad_field * branch_one)
    grad_branch = (mode(2) * grad_field).astype(MXB)
    grad_so_ref[...] += dot_tn(attn_one, grad_branch)
    sums_ref[9] += eight_rows(grad_branch.astype(F32))
    g1_ref[...] = grad_field.reshape(frames, tile, width)
    grad_attn = dot(grad_branch, so_turned_ref[...]).astype(MXB).reshape(frames, tile, width)

    @pl.when(at_step == 0)
    def _():
        greeted(peers)

    def sent(at_step):
        da_keep(at_step).wait()
        for step, peer, _ in peers:
            da_copy(at_step, step, peer).wait_send()

    @pl.when(at_step >= 2)
    def _():
        sent(at_step - 2)

    da_ref[lax.rem(at_step, 2)] = grad_attn
    da_keep(at_step).start()
    for step, peer, _ in peers:
        da_copy(at_step, step, peer).start()

    @pl.when(at_step == steps - 1)
    def _():
        @pl.when(steps > 1)
        def _():
            sent(steps - 2)

        sent(steps - 1)
        for step, _, source in peers:
            da_landed(step, source).wait_recv()


def whole_spec(shape):
    rank = len(shape)
    return pl.BlockSpec(shape, lambda *_: (0,) * rank, pipeline_mode=pl.Buffered(1))


def acc_spec(shape):
    rank = len(shape)
    return pl.BlockSpec(shape, lambda *_: (0,) * rank)


def params(number):
    return pltpu.CompilerParams(vmem_limit_bytes=VMEM_BYTES, collective_id=number, has_side_effects=True)


def any_spec():
    return pl.BlockSpec(memory_space=pl.ANY)


def cost(flops, moved):
    return pl.CostEstimate(flops=flops, bytes_accessed=moved, transcendentals=0)


def fast_body(
    tokens, conditioning, timesteps, out_grad, ada_weight, ada_bias, spatial_proj, spatial_bias, spatial_out,
    spatial_out_bias, temporal_proj, temporal_bias, temporal_out, temporal_out_bias, hidden_in, hidden_in_bias,
    hidden_out, hidden_out_bias,
):
    _, frames, stripe, width = tokens.shape
    hidden = hidden_in.shape[1]
    pairs = width // (2 * HEAD_DIM)
    cond_act = jax.nn.silu(conditioning.astype(F32)).astype(MXB)
    modes = (jnp.dot(cond_act, ada_weight, preferred_element_type=F32) + ada_bias).reshape(9, width)

    def widen(bias):
        return jnp.concatenate([bias[:width], jnp.zeros((width,), F32), bias[width:]])[None, :]

    x_patches = tokens[0]
    count = lax.axis_size("sp")
    mine, patches = frames // count, stripe * count
    block = min(1024, patches)
    frame_shape = jax.ShapeDtypeStruct((mine, patches, width), MXB)
    patch_shape = jax.ShapeDtypeStruct((frames, stripe, width), MXB)
    dma = pltpu.SemaphoreType.DMA
    x_frames, queries, keys, values, attn_frames, attn_patches, logs = pl.pallas_call(
        partial(spatial_forward, rows=256, block=block, part=512, count=count),
        in_specs=[any_spec()] + [pl.BlockSpec(memory_space=pltpu.VMEM)] * 3,
        out_specs=[any_spec()] * 6 + [pl.BlockSpec(memory_space=pltpu.VMEM)],
        out_shape=[frame_shape] * 5 + [patch_shape, jax.ShapeDtypeStruct((mine, pairs, 2, patches), F32)],
        scratch_shapes=[pltpu.VMEM((mine, patches, width), MXB)] * 5
        + [pltpu.VMEM((2 * pairs, HEAD_DIM + 16, patches), MXB)]
        + [dma((mine, count)), dma((mine, count)), dma((mine,))]
        + [dma((mine, pairs, count)), dma((mine, pairs, count)), dma((mine, pairs)), dma((5, mine))],
        compiler_params=params(0),
        cost_estimate=cost(10**11, 10**7),
    )(x_patches, modes, spatial_proj, widen(spatial_bias))

    slope = jnp.tan((timesteps.astype(F32) / TSTEPS + 0.008) / 1.008 * (0.5 * math.pi))
    loss_weight = jnp.minimum(1.0, 5.0 * slope * slope).reshape(1, 1)
    place = jnp.arange(frames * TILE) % TILE
    mask = jnp.where(place[:, None] == place[None, :], 0.0, -1e30).astype(F32)
    tile_spec = pl.BlockSpec((frames, TILE, width), lambda i: (0, i, 0))
    small = (
        loss_weight * jnp.ones((1, width), F32), modes, mask,
        spatial_out, spatial_out.T, spatial_out_bias[None, :],
        temporal_proj, temporal_proj.T, widen(temporal_bias),
        temporal_out, temporal_out.T, temporal_out_bias[None, :],
        hidden_in, hidden_in.T, hidden_in_bias[None, :],
        hidden_out, hidden_out.T, hidden_out_bias[None, :],
    )
    sums_shapes = [
        (width, width), (width, 3 * width), (width, width), (width, hidden), (width, hidden),
        (12, 8, width), (8, 3 * width), (8, hidden),
    ]
    out_shapes = [
        patch_shape,
        jax.ShapeDtypeStruct((frames, stripe, width), F32),
        frame_shape,
    ] + [jax.ShapeDtypeStruct(s, F32) for s in sums_shapes]
    (
        block_out, g1, da_frames, grad_so, grad_t, grad_to, grad_in, grad_out_turned, sums, t_sums, in_sums,
    ) = pl.pallas_call(
        partial(middle, peer_count=count),
        grid=(stripe // TILE,),
        in_specs=[tile_spec] * 3 + [whole_spec(a.shape) for a in small],
        out_specs=[tile_spec] * 2 + [any_spec()] + [acc_spec(s) for s in sums_shapes],
        out_shape=out_shapes,
        scratch_shapes=[pltpu.VMEM((2, frames, TILE, width), MXB), dma((2, count)), dma((count,)), dma((2,))],
        compiler_params=params(1),
        cost_estimate=cost(10**11, 10**7),
    )(x_patches, attn_patches, out_grad[0], *small)
    frame_spec = pl.BlockSpec((1, patches, width), lambda f: (f, 0, 0))
    log_spec = pl.BlockSpec((1, pairs, 2, patches), lambda f: (f, 0, 0, 0))
    sum_shapes = [(width, 3 * width), (2, 8, width), (8, 3 * width)]
    dx_patches, grad_sp, sp_sums, sp_bias_sums = pl.pallas_call(
        partial(spatial_backward, rows=256, block=block, part=512, count=count),
        grid=(mine,),
        in_specs=[frame_spec] * 5 + [log_spec, frame_spec, whole_spec((9, width)), whole_spec((3 * width, width))],
        out_specs=[any_spec()] + [acc_spec(s) for s in sum_shapes],
        out_shape=[patch_shape] + [jax.ShapeDtypeStruct(s, F32) for s in sum_shapes],
        scratch_shapes=[
            pltpu.VMEM((mine, patches, width), MXB),
            pltpu.VMEM((patches, 3 * width), MXB),
            pltpu.VMEM((pairs, 2, patches), F32),
            pltpu.VMEM((patches, 2 * HEAD_DIM), F32),
            pltpu.VMEM((patches, 2 * HEAD_DIM), F32),
            dma((mine, count)),
            dma((mine, count)),
            dma((mine,)),
        ],
        compiler_params=params(2),
        cost_estimate=cost(2 * 10**11, 10**7),
    )(da_frames, attn_frames, queries, keys, values, logs, x_frames, modes, spatial_proj.T)
    input_grad = (g1 + dx_patches.astype(F32)).astype(MXB)

    clip_at = lax.axis_index("clip")
    clips = lax.axis_size("clip")
    vector = jnp.sum(sums, axis=1)
    sp_vector = jnp.sum(sp_sums, axis=1)
    grad_modes = jnp.concatenate([sp_vector, vector[2:9]], axis=0).reshape(1, 9 * width)
    mine_only = (jnp.arange(clips) == clip_at)[:, None]
    first_on_sp = (lax.axis_index("sp") == 0).astype(F32)
    early = lax.psum((grad_so, grad_t, grad_to, grad_in, grad_out_turned), ("clip", "sp"))
    early, grad_sp, sp_bias_sums = lax.optimization_barrier((early, grad_sp, sp_bias_sums))
    sp_bias = jnp.sum(sp_bias_sums, axis=0)
    t_bias = jnp.sum(t_sums, axis=0)
    pieces = (
        jnp.where(mine_only, grad_modes, 0.0),
        jnp.where(mine_only, cond_act.astype(F32) * first_on_sp, 0.0),
        sp_bias,
        t_bias,
        jnp.sum(in_sums, axis=0),
        vector[9:12],
    )
    flat = jnp.concatenate([p.reshape(-1) for p in pieces])
    flat, grad_sp = lax.psum((flat, grad_sp), ("clip", "sp"))
    found = []
    start = 0
    for piece in pieces:
        found.append(flat[start : start + piece.size].reshape(piece.shape))
        start += piece.size
    all_modes, all_cond, sp_bias, t_bias, in_bias, out_biases = found
    grad_ada_weight = jnp.dot(all_cond.T, all_modes, precision=lax.Precision.HIGHEST)
    grad_ada_bias = jnp.sum(all_modes, axis=0)
    return (
        block_out[None],
        input_grad[None],
        grad_ada_weight,
        grad_ada_bias,
        grad_sp,
        jnp.concatenate([sp_bias[:width], sp_bias[2 * width :]]),
        early[0],
        out_biases[0],
        early[1],
        jnp.concatenate([t_bias[:width], t_bias[2 * width :]]),
        early[2],
        out_biases[1],
        early[3],
        in_bias,
        early[4].T,
        out_biases[2],
    )


def chosen(tokens, *others):
    _, frames, stripe, _ = tokens.shape
    if tokens.shape[0] == 1 and frames % lax.axis_size("sp") == 0 and stripe % TILE == 0:
        return fast_body(tokens, *others)
    return body(tokens, *others)


def solution(mesh):
    return jax.shard_map(
        chosen,
        mesh=mesh,
        in_specs=(
            P("clip", None, "sp", None),
            P("clip", None),
            P("clip"),
            P("clip", None, "sp", None),
            P(),
            P(),
            P(),
            P(),
            P(),
            P(),
            P(),
            P(),
            P(),
            P(),
            P(),
            P(),
            P(),
            P(),
        ),
        out_specs=(
            P("clip", None, "sp", None),
            P("clip", None, "sp", None),
            P(),
            P(),
            P(),
            P(),
            P(),
            P(),
            P(),
            P(),
            P(),
            P(),
            P(),
            P(),
            P(),
            P(),
        ),
        check_vma=False,
    )
```

```python
from functools import partial, reduce
import math

import jax
import jax.numpy as jnp
from jax import lax
from jax.experimental import pallas as pl
from jax.experimental.pallas import tpu as pltpu
from jax.sharding import PartitionSpec as P

HEADS = 6
HEAD_DIM = 64
FRAME_BLOCK = 8
TSTEPS = 1000
GELU_RATE = math.sqrt(2.0 / math.pi)
SP_BIAS = 9
T_BIAS = 12
SO_BIAS = 15
TO_BIAS = 16
OUT_BIAS = 17
IN_BIAS = 18
WEIGHT = 22
COND = 23
ROWS = 24


def modulate(field, shift, scale):
    centred = field - jnp.mean(field, axis=-1, keepdims=True)
    normed = centred * lax.rsqrt(jnp.mean(centred * centred, axis=-1, keepdims=True) + 1e-06)
    return normed * (1.0 + scale) + shift


def loss_weights(timesteps):
    phase = (timesteps.astype(jnp.float32) / TSTEPS + 0.008) / 1.008 * (0.5 * math.pi)
    slope = jnp.tan(phase)
    return jnp.minimum(1.0, 5.0 * slope * slope)


def split_heads(array):
    return array.reshape(array.shape[:-1] + (HEADS, HEAD_DIM))


def join_heads(array):
    return array.reshape(array.shape[:-2] + (HEADS * HEAD_DIM,))


def attend(queries, keys, values):
    scores = jnp.einsum(
        "csqhe,cskhe->cshqk", queries, keys, preferred_element_type=jnp.float32
    ) * HEAD_DIM ** (-0.5)
    row_max = jnp.max(scores, axis=-1, keepdims=True)
    exponent = jnp.exp(scores - row_max)
    total = jnp.sum(exponent, axis=-1, keepdims=True)
    soft_weights = (exponent / total).astype(jnp.bfloat16)
    mixed = jnp.einsum(
        "cshqk,cskhe->csqhe", soft_weights, values, preferred_element_type=jnp.float32
    )
    return (mixed, row_max[..., 0] + jnp.log(total[..., 0]))


def probabilities(queries, keys, values, grads, log_total):
    scores = jnp.einsum(
        "csqhe,cskhe->cshqk", queries, keys, preferred_element_type=jnp.float32
    ) * HEAD_DIM ** (-0.5)
    soft_weights = jnp.exp(scores - log_total[..., None])
    grad_weights = jnp.einsum(
        "csqhe,cskhe->cshqk", grads, values, preferred_element_type=jnp.float32
    )
    return (soft_weights, grad_weights)


def query_pass(queries, keys, values, grads, log_total):
    soft_weights, grad_weights = probabilities(queries, keys, values, grads, log_total)
    delta = jnp.sum(soft_weights * grad_weights, axis=-1)
    grad_scores = (soft_weights * (grad_weights - delta[..., None]) * HEAD_DIM ** (-0.5)).astype(
        jnp.bfloat16
    )
    grad_queries = jnp.einsum(
        "cshqk,cskhe->csqhe", grad_scores, keys, preferred_element_type=jnp.float32
    )
    return (grad_queries, delta)


def key_pass(queries, keys, values, grads, log_total, delta):
    soft_weights, grad_weights = probabilities(queries, keys, values, grads, log_total)
    grad_scores = (soft_weights * (grad_weights - delta[..., None]) * HEAD_DIM ** (-0.5)).astype(
        jnp.bfloat16
    )
    grad_keys = jnp.einsum(
        "cshqk,csqhe->cskhe", grad_scores, queries, preferred_element_type=jnp.float32
    )
    grad_values = jnp.einsum(
        "cshqk,csqhe->cskhe",
        soft_weights.astype(jnp.bfloat16),
        grads,
        preferred_element_type=jnp.float32,
    )
    return jnp.concatenate([join_heads(grad_keys), join_heads(grad_values)], axis=-1)


def column_sums(array):
    return jnp.sum(array.astype(jnp.float32), axis=(0, 1, 2))


def body(
    tokens,
    conditioning,
    timesteps,
    out_grad,
    ada_weight,
    ada_bias,
    spatial_proj,
    spatial_bias,
    spatial_out,
    spatial_out_bias,
    temporal_proj,
    temporal_bias,
    temporal_out,
    temporal_out_bias,
    hidden_in,
    hidden_in_bias,
    hidden_out,
    hidden_out_bias,
):
    clips, frames, stripe, width = tokens.shape
    blocks = frames // FRAME_BLOCK
    scale_factor = HEAD_DIM ** (-0.5)
    field = tokens.astype(jnp.float32)
    cond_act = jax.nn.silu(conditioning.astype(jnp.float32)).astype(jnp.bfloat16)
    modes = jnp.dot(cond_act, ada_weight, preferred_element_type=jnp.float32) + ada_bias
    modes = modes.reshape(clips, 9, 1, 1, width)
    hidden_one, back_one = jax.vjp(modulate, field, modes[:, 0], modes[:, 1])
    hidden_one = hidden_one.astype(jnp.bfloat16)
    query_mix = jnp.einsum(
        "cfpd,de->cfpe", hidden_one, spatial_proj[:, :width], preferred_element_type=jnp.float32
    )
    queries = (query_mix + spatial_bias[:width]).astype(jnp.bfloat16)
    keyval_mix = jnp.einsum(
        "cfpd,de->cfpe", hidden_one, spatial_proj[:, width:], preferred_element_type=jnp.float32
    )
    keyval_bias = jnp.concatenate([jnp.zeros((width,), jnp.float32), spatial_bias[width:]])
    keyvals = (keyval_mix + keyval_bias).astype(jnp.bfloat16)
    query_heads = split_heads(queries)
    mixed_parts = []
    log_parts = []
    for index in range(blocks):
        first = index * FRAME_BLOCK
        whole = lax.all_gather(keyvals[:, first : first + FRAME_BLOCK], "sp", axis=2, tiled=True)
        mixed_part, log_part = attend(
            query_heads[:, first : first + FRAME_BLOCK],
            split_heads(whole[..., :width]),
            split_heads(whole[..., width:]),
        )
        mixed_parts.append(join_heads(mixed_part))
        log_parts.append(log_part)
    attn_one = jnp.concatenate(mixed_parts, axis=1).astype(jnp.bfloat16)
    spatial_log = jnp.concatenate(log_parts, axis=1)
    branch_one = (
        jnp.einsum("cfpd,de->cfpe", attn_one, spatial_out, preferred_element_type=jnp.float32)
        + spatial_out_bias
    )
    field_one = field + modes[:, 2] * branch_one
    hidden_two, back_two = jax.vjp(modulate, field_one, modes[:, 3], modes[:, 4])
    hidden_two = hidden_two.astype(jnp.bfloat16)
    time_mix = jnp.einsum(
        "cfpd,de->cfpe", hidden_two, temporal_proj, preferred_element_type=jnp.float32
    )
    time_queries = split_heads((time_mix[..., :width] + temporal_bias[:width]).astype(jnp.bfloat16))
    time_keys = split_heads(time_mix[..., width : 2 * width].astype(jnp.bfloat16))
    time_values = split_heads(
        (time_mix[..., 2 * width :] + temporal_bias[width:]).astype(jnp.bfloat16)
    )
    time_scores = (
        jnp.einsum(
            "cfphe,cgphe->cphfg", time_queries, time_keys, preferred_element_type=jnp.float32
        )
        * scale_factor
    )
    time_max = jnp.max(time_scores, axis=-1, keepdims=True)
    time_exponent = jnp.exp(time_scores - time_max)
    time_weights = time_exponent / jnp.sum(time_exponent, axis=-1, keepdims=True)
    time_rounded = time_weights.astype(jnp.bfloat16)
    attn_two = join_heads(
        jnp.einsum(
            "cphfg,cgphe->cfphe", time_rounded, time_values, preferred_element_type=jnp.float32
        )
    ).astype(jnp.bfloat16)
    branch_two = (
        jnp.einsum("cfpd,de->cfpe", attn_two, temporal_out, preferred_element_type=jnp.float32)
        + temporal_out_bias
    )
    field_two = field_one + modes[:, 5] * branch_two
    hidden_three, back_three = jax.vjp(modulate, field_two, modes[:, 6], modes[:, 7])
    hidden_three = hidden_three.astype(jnp.bfloat16)
    inner = (
        jnp.einsum("cfpd,dk->cfpk", hidden_three, hidden_in, preferred_element_type=jnp.float32)
        + hidden_in_bias
    )
    active, gelu_back = jax.vjp(partial(jax.nn.gelu, approximate=True), inner)
    active = active.astype(jnp.bfloat16)
    branch_three = (
        jnp.einsum("cfpk,kd->cfpd", active, hidden_out, preferred_element_type=jnp.float32)
        + hidden_out_bias
    )
    block_out = (field_two + modes[:, 8] * branch_three).astype(jnp.bfloat16)
    weights = loss_weights(timesteps)
    grad_field = out_grad.astype(jnp.float32) * weights[:, None, None, None]
    grad_gate_three = jnp.sum(grad_field * branch_three, axis=(1, 2))
    grad_branch = (modes[:, 8] * grad_field).astype(jnp.bfloat16)
    grad_hidden_out = jnp.einsum(
        "cfpk,cfpd->kd", active, grad_branch, preferred_element_type=jnp.float32
    )
    grad_hidden_out_bias = column_sums(grad_branch)
    grad_active = jnp.einsum(
        "cfpd,kd->cfpk", grad_branch, hidden_out, preferred_element_type=jnp.float32
    )
    grad_inner = gelu_back(grad_active)[0].astype(jnp.bfloat16)
    grad_hidden_in = jnp.einsum(
        "cfpd,cfpk->dk", hidden_three, grad_inner, preferred_element_type=jnp.float32
    )
    grad_hidden_in_bias = column_sums(grad_inner)
    grad_hidden = jnp.einsum(
        "cfpk,dk->cfpd", grad_inner, hidden_in, preferred_element_type=jnp.float32
    )
    grad_input, grad_shift_three, grad_scale_three = back_three(grad_hidden)
    grad_field = grad_field + grad_input
    grad_gate_two = jnp.sum(grad_field * branch_two, axis=(1, 2))
    grad_branch = (modes[:, 5] * grad_field).astype(jnp.bfloat16)
    grad_temporal_out = jnp.einsum(
        "cfpd,cfpe->de", attn_two, grad_branch, preferred_element_type=jnp.float32
    )
    grad_temporal_out_bias = column_sums(grad_branch)
    grad_attn = split_heads(
        jnp.einsum(
            "cfpe,de->cfpd", grad_branch, temporal_out, preferred_element_type=jnp.float32
        ).astype(jnp.bfloat16)
    )
    grad_weights = jnp.einsum(
        "cfphe,cgphe->cphfg", grad_attn, time_values, preferred_element_type=jnp.float32
    )
    delta = jnp.sum(time_weights * grad_weights, axis=-1, keepdims=True)
    grad_scores = (time_weights * (grad_weights - delta) * scale_factor).astype(jnp.bfloat16)
    grad_time_queries = jnp.einsum(
        "cphfg,cgphe->cfphe", grad_scores, time_keys, preferred_element_type=jnp.float32
    )
    grad_time_keys = jnp.einsum(
        "cphfg,cfphe->cgphe", grad_scores, time_queries, preferred_element_type=jnp.float32
    )
    grad_time_values = jnp.einsum(
        "cphfg,cfphe->cgphe", time_rounded, grad_attn, preferred_element_type=jnp.float32
    )
    grad_time_mix = jnp.concatenate(
        [join_heads(grad_time_queries), join_heads(grad_time_keys), join_heads(grad_time_values)],
        axis=-1,
    ).astype(jnp.bfloat16)
    grad_temporal_proj = jnp.einsum(
        "cfpd,cfpe->de", hidden_two, grad_time_mix, preferred_element_type=jnp.float32
    )
    grad_temporal_bias = jnp.concatenate(
        [column_sums(grad_time_mix[..., :width]), column_sums(grad_time_mix[..., 2 * width :])]
    )
    grad_hidden = jnp.einsum(
        "cfpe,de->cfpd", grad_time_mix, temporal_proj, preferred_element_type=jnp.float32
    )
    grad_input, grad_shift_two, grad_scale_two = back_two(grad_hidden)
    grad_field = grad_field + grad_input
    grad_gate_one = jnp.sum(grad_field * branch_one, axis=(1, 2))
    grad_branch = (modes[:, 2] * grad_field).astype(jnp.bfloat16)
    grad_spatial_out = jnp.einsum(
        "cfpd,cfpe->de", attn_one, grad_branch, preferred_element_type=jnp.float32
    )
    grad_spatial_out_bias = column_sums(grad_branch)
    grad_attn = jnp.einsum(
        "cfpe,de->cfpd", grad_branch, spatial_out, preferred_element_type=jnp.float32
    ).astype(jnp.bfloat16)
    query_parts = []
    key_parts = []
    for index in range(blocks):
        first = index * FRAME_BLOCK
        whole = lax.all_gather(keyvals[:, first : first + FRAME_BLOCK], "sp", axis=2, tiled=True)
        piece = query_heads[:, first : first + FRAME_BLOCK]
        grad_piece = split_heads(grad_attn[:, first : first + FRAME_BLOCK])
        log_piece = spatial_log[:, first : first + FRAME_BLOCK]
        grad_query_part, delta = query_pass(
            piece,
            split_heads(whole[..., :width]),
            split_heads(whole[..., width:]),
            grad_piece,
            log_piece,
        )
        term = key_pass(
            piece,
            split_heads(whole[..., :width]),
            split_heads(whole[..., width:]),
            grad_piece,
            log_piece,
            delta,
        )
        owned = lax.psum_scatter(
            jnp.transpose(term, (2, 0, 1, 3)).astype(jnp.bfloat16),
            "sp",
            scatter_dimension=0,
            tiled=True,
        ).astype(jnp.float32)
        query_parts.append(join_heads(grad_query_part))
        key_parts.append(jnp.transpose(owned, (1, 2, 0, 3)))
    grad_queries = jnp.concatenate(query_parts, axis=1)
    grad_keyvals = jnp.concatenate(key_parts, axis=1)
    grad_queries = grad_queries.astype(jnp.bfloat16)
    grad_keyvals = grad_keyvals.astype(jnp.bfloat16)
    grad_spatial_proj = jnp.concatenate(
        [
            jnp.einsum(
                "cfpd,cfpe->de", hidden_one, grad_queries, preferred_element_type=jnp.float32
            ),
            jnp.einsum(
                "cfpd,cfpe->de", hidden_one, grad_keyvals, preferred_element_type=jnp.float32
            ),
        ],
        axis=1,
    )
    grad_spatial_bias = jnp.concatenate(
        [column_sums(grad_queries), column_sums(grad_keyvals[..., width:])]
    )
    grad_hidden = jnp.einsum(
        "cfpe,de->cfpd", grad_queries, spatial_proj[:, :width], preferred_element_type=jnp.float32
    )
    grad_hidden = grad_hidden + jnp.einsum(
        "cfpe,de->cfpd", grad_keyvals, spatial_proj[:, width:], preferred_element_type=jnp.float32
    )
    grad_input, grad_shift_one, grad_scale_one = back_one(grad_hidden)
    input_grad = (grad_field + grad_input).astype(jnp.bfloat16)
    grad_modes = jnp.stack(
        [
            grad_shift_one.reshape(clips, width),
            grad_scale_one.reshape(clips, width),
            grad_gate_one,
            grad_shift_two.reshape(clips, width),
            grad_scale_two.reshape(clips, width),
            grad_gate_two,
            grad_shift_three.reshape(clips, width),
            grad_scale_three.reshape(clips, width),
            grad_gate_three,
        ],
        axis=1,
    ).reshape(clips, 9 * width)
    grad_ada_weight = jnp.dot(
        cond_act.astype(jnp.float32).T, grad_modes, precision=lax.Precision.HIGHEST
    )
    grad_ada_bias = jnp.sum(grad_modes, axis=0)
    summed = lax.psum(
        (
            grad_ada_weight,
            grad_ada_bias,
            grad_spatial_proj,
            grad_spatial_bias,
            grad_spatial_out,
            grad_spatial_out_bias,
            grad_temporal_proj,
            grad_temporal_bias,
            grad_temporal_out,
            grad_temporal_out_bias,
            grad_hidden_in,
            grad_hidden_in_bias,
            grad_hidden_out,
            grad_hidden_out_bias,
        ),
        ("clip", "sp"),
    )
    return (
        block_out,
        input_grad,
        summed[0],
        summed[1],
        summed[2],
        summed[3],
        summed[4],
        summed[5],
        summed[6],
        summed[7],
        summed[8],
        summed[9],
        summed[10],
        summed[11],
        summed[12],
        summed[13],
    )


MXB = jnp.bfloat16
F32 = jnp.float32
TILE = 32
GROUP = 8
VMEM_BYTES = 60 * 2**20


def dot(left, right):
    return jnp.dot(left, right, preferred_element_type=F32)


def dot_nt(left, right):
    return lax.dot_general(left, right, (((1,), (1,)), ((), ())), preferred_element_type=F32)


def dot_tn(left, right):
    return lax.dot_general(left, right, (((0,), (0,)), ((), ())), preferred_element_type=F32)


def turned(array):
    return array.astype(F32).T.astype(array.dtype)


def normalise(field):
    centred = field - jnp.mean(field, axis=-1, keepdims=True)
    rate = lax.rsqrt(jnp.mean(centred * centred, axis=-1, keepdims=True) + 1e-06)
    return centred * rate, rate


def normalise_back(grad, normed, rate, scale):
    inner = grad * (1.0 + scale)
    mean = jnp.mean(inner, axis=-1, keepdims=True)
    slope = jnp.mean(inner * normed, axis=-1, keepdims=True)
    return rate * (inner - mean - normed * slope)


def eight_rows(array):
    return jnp.sum(array.reshape(array.shape[0] // 8, 8, array.shape[1]), axis=0)


def wide(ref, first, rows):
    return jnp.concatenate([ref[first + row : first + row + 1, :] for row in range(rows)], axis=1)


def low_lanes():
    return lax.broadcasted_iota(jnp.int32, (1, 2 * HEAD_DIM), 1) < HEAD_DIM


def halves(pair):
    low = low_lanes()
    zero = jnp.zeros_like(pair)
    return jnp.where(low, pair, zero), jnp.where(low, zero, pair)


def others(count, axis="sp"):
    me = lax.axis_index(axis)
    return me, [(step, lax.rem(me + step, count), lax.rem(me + count - step, count)) for step in range(1, count)]


def send(source, target, send_sem, recv_sem, peer, axis="sp"):
    return pltpu.make_async_remote_copy(
        src_ref=source, dst_ref=target, send_sem=send_sem, recv_sem=recv_sem,
        device_id={axis: peer}, device_id_type=pl.DeviceIdType.MESH,
    )


def greet(peers, axis="sp"):
    barrier = pltpu.get_barrier_semaphore()
    for _, peer, _ in peers:
        pl.semaphore_signal(barrier, inc=1, device_id={axis: peer}, device_id_type=pl.DeviceIdType.MESH)


def greeted(peers):
    pl.semaphore_wait(pltpu.get_barrier_semaphore(), len(peers))


def spatial_forward(
    tokens_ref, modes_ref, proj_ref,
    x_out, q_out, k_out, v_out, attn_out, patches_out, log_ref,
    x_ref, q_ref, k_ref, v_ref, attn_ref, turned_ref,
    x_send, x_recv, x_own, a_send, a_recv, a_own, save_sem,
    rows, block, part, count,
):
    mine, tokens, width = x_ref.shape
    stripe = tokens // count
    pairs = width // (2 * HEAD_DIM)
    near = block // stripe
    blocks = tokens // block
    me, peers = others(count)
    shift = modes_ref[0:1, :]
    scale = modes_ref[1:2, :]
    bias = wide(modes_ref, SP_BIAS, 3)

    def x_copy(frame, step, peer):
        return send(
            tokens_ref.at[peer * mine + frame],
            x_ref.at[frame, pl.ds(pl.multiple_of(me * stripe, stripe), stripe), :],
            x_send.at[frame, step], x_recv.at[frame, step], peer,
        )

    def x_keep(frame):
        return pltpu.make_async_copy(
            tokens_ref.at[me * mine + frame],
            x_ref.at[frame, pl.ds(pl.multiple_of(me * stripe, stripe), stripe), :],
            x_own.at[frame],
        )

    def saves(frame):
        return [
            pltpu.make_async_copy(held.at[frame], kept.at[frame], save_sem.at[place, frame])
            for place, (held, kept) in enumerate(
                ((x_ref, x_out), (q_ref, q_out), (k_ref, k_out), (v_ref, v_out), (attn_ref, attn_out))
            )
        ]

    def a_copy(frame, pair, peer):
        lanes = pl.ds(pl.multiple_of(pair * 2 * HEAD_DIM, 2 * HEAD_DIM), 2 * HEAD_DIM)
        return send(
            attn_ref.at[frame, pl.ds(pl.multiple_of(peer * stripe, stripe), stripe), lanes],
            patches_out.at[me * mine + frame, :, lanes],
            a_send.at[frame, pair, peer], a_recv.at[frame, pair, me], peer,
        )

    def a_landed(frame, pair, peer):
        lanes = pl.ds(pl.multiple_of(pair * 2 * HEAD_DIM, 2 * HEAD_DIM), 2 * HEAD_DIM)
        return send(
            attn_ref.at[frame, pl.ds(pl.multiple_of(peer * stripe, stripe), stripe), lanes],
            patches_out.at[peer * mine + frame, :, lanes],
            a_send.at[frame, pair, peer], a_recv.at[frame, pair, peer], peer,
        )

    def a_keep(frame, pair):
        lanes = pl.ds(pl.multiple_of(pair * 2 * HEAD_DIM, 2 * HEAD_DIM), 2 * HEAD_DIM)
        return pltpu.make_async_copy(
            attn_ref.at[frame, pl.ds(pl.multiple_of(me * stripe, stripe), stripe), lanes],
            patches_out.at[me * mine + frame, :, lanes],
            a_own.at[frame, pair],
        )

    greet(peers)
    greeted(peers)
    order = sorted(range(1, count), key=lambda step: -min(step, count - step))
    for frame in range(mine):
        for step in order:
            x_copy(frame, step, lax.rem(me + step, count)).start()
        x_keep(frame).start()
    turned_ref[:, HEAD_DIM:, :] = jnp.ones((2 * pairs, turned_ref.shape[1] - HEAD_DIM, tokens), MXB)

    def one_frame(frame, carry):
        x_keep(frame).wait()
        for step, _, source in peers:
            x_copy(frame, step, source).wait_recv()
        saves(frame)[0].start()

        def project(index, carry):
            at = pl.ds(pl.multiple_of(index * rows, rows), rows)
            normed, _ = normalise(x_ref[frame, at, :].astype(F32))
            hidden = (normed * (1.0 + scale) + shift).astype(MXB)
            mixed = dot(hidden, proj_ref[...]) + bias
            q_ref[frame, at, :] = mixed[:, :width].astype(MXB)
            k_ref[frame, at, :] = mixed[:, width : 2 * width].astype(MXB)
            value = mixed[:, 2 * width :].astype(MXB)
            v_ref[frame, at, :] = value
            across = turned(value)
            for head in range(2 * pairs):
                turned_ref[head, :HEAD_DIM, at] = across[head * HEAD_DIM : (head + 1) * HEAD_DIM]
            return carry

        lax.fori_loop(0, tokens // rows, project, 0)
        for copy in saves(frame)[1:4]:
            copy.start()

        def attend_block(index, carry):
            pair = lax.rem(index, pairs)
            chunk = lax.rem(lax.div(index, pairs) + lax.div(me, near) + 1, blocks)
            at = pl.ds(pl.multiple_of(chunk * block, block), block)
            lanes = pl.ds(pl.multiple_of(pair * 2 * HEAD_DIM, 2 * HEAD_DIM), 2 * HEAD_DIM)
            scores = []
            tops = []
            for query in halves(q_ref[frame, at, lanes] * MXB(HEAD_DIM**-0.5)):
                each = [
                    dot_nt(k_ref[frame, first : first + part, lanes], query)
                    for first in range(0, tokens, part)
                ]
                top = [jnp.max(s.reshape(part // 8, 8, block), axis=0) for s in each]
                scores.append(each)
                tops.append(jnp.max(reduce(jnp.maximum, top), axis=0, keepdims=True))
            mixed = []
            for half in range(2):
                total = jnp.zeros((turned_ref.shape[1], block), F32)
                for number, s in enumerate(scores[half]):
                    weights = jnp.exp(s - tops[half]).astype(MXB)
                    values = turned_ref[2 * pair + half, :, number * part : (number + 1) * part]
                    total = total + dot(values, weights)
                mass = total[HEAD_DIM : HEAD_DIM + 1]
                log_ref[frame, pair, half : half + 1, at] = tops[half] + jnp.log(mass)
                mixed.append(total[:HEAD_DIM] / mass)
            attn_ref[frame, at, lanes] = jnp.concatenate(mixed, axis=0).T.astype(MXB)
            for place in range(near):
                peer = chunk * near + place

                @pl.when(peer != me)
                def _():
                    a_copy(frame, pair, peer).start()

                @pl.when(peer == me)
                def _():
                    a_keep(frame, pair).start()

            return carry

        lax.fori_loop(0, pairs * blocks, attend_block, 0)
        saves(frame)[4].start()
        return carry

    lax.fori_loop(0, mine, one_frame, 0)

    for frame in range(mine):
        for copy in saves(frame):
            copy.wait()
        for step, peer, _ in peers:
            x_copy(frame, step, peer).wait_send()
        for pair in range(pairs):
            a_keep(frame, pair).wait()
            for _, peer, _ in peers:
                a_copy(frame, pair, peer).wait_send()
                a_landed(frame, pair, peer).wait_recv()


def spatial_backward(
    da_ref, attn_ref, q_ref, k_ref, v_ref, log_ref, x_ref, modes_ref, proj_ref, mid_sums_ref, t_sums_ref, in_sums_ref,
    patches_out, grad_proj_ref, ada_ref, total_ref,
    dx_ref, mix_ref, delta_ref, dk_ref, dv_ref, sums_ref, bias_sums_ref,
    clip_out_ref, clip_in_ref, unit_out_ref, unit_in_ref, piece_ref, all_ref, vec_ref, vec_in_ref, row_ref, row_in_ref,
    send_sem, recv_sem, own_sem, g1_send, g1_recv, g2_send, g2_recv, g3_send, g3_recv, g4_send, g4_recv,
    v1_send, v1_recv, v2_send, v2_recv, rows, block, part, count, clips,
):
    tokens, width = x_ref.shape[1:]
    mine = dx_ref.shape[0]
    stripe = tokens // count
    frame = pl.program_id(0)
    me, peers = others(count)
    clip, clip_peers = others(clips, "clip")
    span_rows = width // clips
    unit = 16 * (-(-span_rows // (16 * count)))
    owners = span_rows // unit

    def g1_copy(peer, slot):
        return send(
            clip_out_ref.at[peer], clip_in_ref.at[slot], g1_send.at[peer], g1_recv.at[slot], peer, "clip"
        )

    def g2_copy(peer, slot):
        return send(unit_out_ref.at[peer], unit_in_ref.at[slot], g2_send.at[peer], g2_recv.at[slot], peer)

    def g3_copy(peer, slot):
        part_rows = pl.ds(pl.multiple_of(slot * unit, unit), unit)
        return send(piece_ref.at[part_rows, :], piece_ref.at[part_rows, :], g3_send.at[peer], g3_recv.at[slot], peer)

    def g4_copy(peer, slot):
        return send(piece_ref, all_ref.at[slot], g4_send.at[peer], g4_recv.at[slot], peer, "clip")

    def v1_copy(peer, slot):
        return send(vec_ref, vec_in_ref.at[slot], v1_send.at[peer], v1_recv.at[slot], peer)

    def v2_copy(peer, slot):
        return send(row_ref, row_in_ref.at[slot], v2_send.at[peer], v2_recv.at[slot], peer, "clip")

    def dx_copy(frame, peer):
        return send(
            dx_ref.at[frame, pl.ds(pl.multiple_of(peer * stripe, stripe), stripe), :],
            patches_out.at[me * mine + frame], send_sem.at[frame, peer], recv_sem.at[frame, me], peer,
        )

    def dx_landed(frame, peer):
        return send(
            dx_ref.at[frame, pl.ds(pl.multiple_of(peer * stripe, stripe), stripe), :],
            patches_out.at[peer * mine + frame], send_sem.at[frame, peer], recv_sem.at[frame, peer], peer,
        )

    def dx_keep(frame):
        return pltpu.make_async_copy(
            dx_ref.at[frame, pl.ds(pl.multiple_of(me * stripe, stripe), stripe), :],
            patches_out.at[me * mine + frame], own_sem.at[frame],
        )

    @pl.when(frame == 0)
    def _():
        greet(peers)
        greet(clip_peers, "clip")

    pairs = width // (2 * HEAD_DIM)
    scale_factor = HEAD_DIM**-0.5

    @pl.when(frame == 0)
    def _():
        grad_proj_ref[...] = jnp.zeros_like(grad_proj_ref)
        sums_ref[...] = jnp.zeros_like(sums_ref)
        bias_sums_ref[...] = jnp.zeros_like(bias_sums_ref)

    head_of = lax.broadcasted_iota(jnp.int32, (8, width), 1) // HEAD_DIM
    picks = jnp.where(head_of == lax.broadcasted_iota(jnp.int32, (8, width), 0), 1.0, 0.0).astype(MXB)

    def deltas(index, carry):
        at = pl.ds(pl.multiple_of(index * rows, rows), rows)
        product = da_ref[0, at, :].astype(F32) * attn_ref[0, at, :].astype(F32)
        high = product.astype(MXB)
        rest = (product - high.astype(F32)).astype(MXB)
        summed = dot_nt(picks, high) + dot_nt(picks, rest)
        for pair in range(pairs):
            delta_ref[pair, 0:2, at] = summed[2 * pair : 2 * pair + 2]
        return carry

    lax.fori_loop(0, tokens // rows, deltas, 0)

    for pair in range(pairs):
        first_lane = 2 * HEAD_DIM * pair
        lanes = slice(first_lane, first_lane + 2 * HEAD_DIM)
        dk_ref[...] = jnp.zeros_like(dk_ref)
        dv_ref[...] = jnp.zeros_like(dv_ref)
        keys_across = turned(k_ref[0, :, lanes])

        def queries_block(index, carry, pair=pair, lanes=lanes, keys_across=keys_across):
            at = pl.ds(pl.multiple_of(index * block, block), block)
            query = halves(q_ref[0, at, lanes] * MXB(scale_factor))
            grad = halves(da_ref[0, at, lanes])
            query_both = jnp.concatenate(query, axis=0)
            grad_both = jnp.concatenate(grad, axis=0)
            grad_query = [jnp.zeros((HEAD_DIM, block), F32), jnp.zeros((HEAD_DIM, block), F32)]
            for first in range(0, tokens, part):
                span = slice(first, first + part)
                keys = k_ref[0, span, lanes]
                values = v_ref[0, span, lanes]
                weights = []
                grad_scores = []
                for half in range(2):
                    scores = dot_nt(keys, query[half])
                    exact = jnp.exp(scores - log_ref[0, pair, half : half + 1, at])
                    grad_weights = dot_nt(values, grad[half])
                    term = (exact * (grad_weights - delta_ref[pair, half : half + 1, at])).astype(MXB)
                    weights.append(exact.astype(MXB))
                    grad_scores.append(term)
                    grad_query[half] = grad_query[half] + dot(
                        keys_across[half * HEAD_DIM : (half + 1) * HEAD_DIM, span], term
                    )
                dv_ref[span, :] += dot(jnp.concatenate(weights, axis=1), grad_both)
                dk_ref[span, :] += dot(jnp.concatenate(grad_scores, axis=1), query_both)
            mix_ref[at, lanes] = (jnp.concatenate(grad_query, axis=0).T * scale_factor).astype(MXB)
            return carry

        lax.fori_loop(0, tokens // block, queries_block, 0)
        mix_ref[:, width + first_lane : width + first_lane + 2 * HEAD_DIM] = dk_ref[...].astype(MXB)
        mix_ref[:, 2 * width + first_lane : 2 * width + first_lane + 2 * HEAD_DIM] = dv_ref[...].astype(MXB)

    shift = modes_ref[0:1, :]
    scale = modes_ref[1:2, :]

    @pl.when(frame == 0)
    def _():
        greeted(peers + clip_peers)

    def hidden_of(at):
        normed, rate = normalise(x_ref[0, at, :].astype(F32))
        return normed, rate, (normed * (1.0 + scale) + shift).astype(MXB)

    def weigh(index, carry):
        at = pl.ds(pl.multiple_of(index * rows, rows), rows)
        _, _, hidden = hidden_of(at)
        grad_mix = mix_ref[at, :]
        grad_proj_ref[...] += dot_tn(hidden, grad_mix)
        bias_sums_ref[...] += eight_rows(grad_mix.astype(F32))
        return carry

    lax.fori_loop(0, tokens // rows, weigh, 0)
    last = frame == mine - 1

    @pl.when(last)
    def _():
        for each in range(clips):
            clip_out_ref[each] = grad_proj_ref[each * span_rows : (each + 1) * span_rows, :].astype(MXB)
        for _, peer, _ in clip_peers:
            g1_copy(peer, clip).start()

    def finish(index, carry):
        peer = lax.rem(me + count // 2 + index, count)
        at = pl.ds(pl.multiple_of(peer * stripe, stripe), stripe)
        normed, rate, _ = hidden_of(at)
        grad_hidden = dot_nt(mix_ref[at, :], proj_ref[...])
        sums_ref[0] += eight_rows(grad_hidden)
        sums_ref[1] += eight_rows(grad_hidden * normed)
        dx_ref[frame, at, :] = normalise_back(grad_hidden, normed, rate, scale).astype(MXB)

        @pl.when(peer != me)
        def _():
            dx_copy(frame, peer).start()

        @pl.when(peer == me)
        def _():
            dx_keep(frame).start()

        return carry

    lax.fori_loop(0, count // 2, finish, 0)

    @pl.when(last)
    def _():
        total = grad_proj_ref[pl.ds(pl.multiple_of(clip * span_rows, span_rows), span_rows), :]
        for _, _, source in clip_peers:
            g1_copy(source, source).wait_recv()
            total = total + clip_in_ref[source].astype(F32)
        for owner in range(owners):
            unit_out_ref[owner] = total[owner * unit : (owner + 1) * unit].astype(MXB)

            @pl.when(owner != me)
            def _():
                g2_copy(owner, me).start()

    lax.fori_loop(count // 2, count, finish, 0)

    @pl.when(last)
    def _():
        def row_sum(array):
            return jnp.sum(array, axis=0, keepdims=True)

        def rows_of(array):
            flat = row_sum(array)
            return [flat[:, first : first + width] for first in range(0, flat.shape[1], width)]

        lines = [row_sum(sums_ref[0]), row_sum(sums_ref[1])]
        lines += [row_sum(mid_sums_ref[line]) for line in range(2, 9)]
        lines += rows_of(bias_sums_ref[...]) + rows_of(t_sums_ref[...])
        lines += [row_sum(mid_sums_ref[line]) for line in range(9, 12)]
        lines += rows_of(in_sums_ref[...])
        lines += [modes_ref[COND : COND + 1, :]] * (ROWS - len(lines))
        vec_ref[...] = jnp.concatenate(lines, axis=0)
        for _, peer, _ in peers:
            v1_copy(peer, me).start()

        @pl.when(me < owners)
        def _():
            total = unit_out_ref[me].astype(F32)
            for _, _, source in peers:
                g2_copy(me, source).wait_recv()
                total = total + unit_in_ref[source].astype(F32)
            piece_ref[pl.ds(pl.multiple_of(me * unit, unit), unit), :] = total.astype(MXB)
            for _, peer, _ in peers:
                g3_copy(peer, me).start()

        total = vec_ref[...]
        for _, _, source in peers:
            v1_copy(source, source).wait_recv()
            total = total + vec_in_ref[source]
        at_row = lax.broadcasted_iota(jnp.int32, (ROWS, width), 0)
        row_ref[...] = jnp.where(at_row < COND, total, vec_ref[...])
        for _, peer, _ in clip_peers:
            v2_copy(peer, clip).start()

        for owner in range(owners):

            @pl.when(owner != me)
            def _():
                g3_copy(owner, owner).wait_recv()

        for _, peer, _ in clip_peers:
            g4_copy(peer, clip).start()
        grad_proj_ref[pl.ds(pl.multiple_of(clip * span_rows, span_rows), span_rows), :] = piece_ref[...].astype(F32)

        row_in_ref[clip] = row_ref[...]
        for _, _, source in clip_peers:
            v2_copy(source, source).wait_recv()
        total = row_in_ref[0]
        for each in range(1, clips):
            total = total + row_in_ref[each]
        total_ref[...] = total
        tall = [row_in_ref[each][ROWS - 8 :].T[:, 7:8] for each in range(clips)]
        for block_at in range(9):
            outer = tall[0] * row_in_ref[0, block_at : block_at + 1, :]
            for each in range(1, clips):
                outer = outer + tall[each] * row_in_ref[each, block_at : block_at + 1, :]
            ada_ref[:, block_at * width : (block_at + 1) * width] = outer

        for _, _, source in clip_peers:
            g4_copy(source, source).wait_recv()
            grad_proj_ref[pl.ds(pl.multiple_of(source * span_rows, span_rows), span_rows), :] = all_ref[source].astype(F32)

        for _, peer, _ in clip_peers:
            g1_copy(peer, clip).wait_send()
            g4_copy(peer, clip).wait_send()
            v2_copy(peer, clip).wait_send()
        for _, peer, _ in peers:
            v1_copy(peer, me).wait_send()

        for owner in range(owners):

            @pl.when(owner != me)
            def _():
                g2_copy(owner, me).wait_send()

        @pl.when(me < owners)
        def _():
            for _, peer, _ in peers:
                g3_copy(peer, me).wait_send()

        for each in range(mine):
            dx_keep(each).wait()
            for _, peer, _ in peers:
                dx_copy(each, peer).wait_send()
                dx_landed(each, peer).wait_recv()


def middle(
    x_ref, attn_ref, og_ref, modes_ref, so_ref, t_ref, to_ref, in_ref, out_ref,
    block_ref, g1_ref, da_out,
    grad_so_ref, grad_t_ref, grad_to_ref, grad_in_ref, grad_out_ref, sums_ref, t_sums_ref, in_sums_ref,
    da_ref, send_sem, recv_sem, own_sem, peer_count,
):
    frames, tile, width = x_ref.shape
    count = frames * tile
    pairs = width // (2 * HEAD_DIM)
    scale_factor = HEAD_DIM**-0.5
    mine = frames // peer_count
    steps = pl.num_programs(0)
    stripe = da_out.shape[1] // peer_count
    at_step = pl.program_id(0)
    me, peers = others(peer_count)

    def da_copy(at_step, step, peer):
        first = pl.multiple_of(me * stripe + at_step * tile, tile)
        slot = lax.rem(at_step, 2)
        return send(
            da_ref.at[slot, pl.ds(peer * mine, mine)], da_out.at[:, pl.ds(first, tile), :],
            send_sem.at[slot, step], recv_sem.at[step], peer,
        )

    def da_keep(at_step):
        first = pl.multiple_of(me * stripe + at_step * tile, tile)
        slot = lax.rem(at_step, 2)
        return pltpu.make_async_copy(
            da_ref.at[slot, pl.ds(me * mine, mine)], da_out.at[:, pl.ds(first, tile), :], own_sem.at[slot]
        )

    def da_landed(step, source):
        rows = da_out.at[:, pl.ds(pl.multiple_of(source * stripe, stripe), stripe), :]
        return send(rows, rows, send_sem.at[0, step], recv_sem.at[step], source)

    @pl.when(at_step == 0)
    def _():
        greet(peers)
        for ref in (grad_so_ref, grad_t_ref, grad_to_ref, grad_in_ref, grad_out_ref, sums_ref, t_sums_ref, in_sums_ref):
            ref[...] = jnp.zeros_like(ref)

    def mode(row):
        return modes_ref[row : row + 1, :]

    cell = frames * GROUP
    groups = tile // GROUP

    def gather(ref):
        whole = ref[...].astype(F32)
        return jnp.concatenate(
            [whole[:, g * GROUP : (g + 1) * GROUP, :].reshape(cell, width) for g in range(groups)], axis=0
        )

    def scatter(value):
        return jnp.concatenate(
            [value[g * cell : (g + 1) * cell].reshape(frames, GROUP, width) for g in range(groups)], axis=1
        )

    field = gather(x_ref)
    attn_one = gather(attn_ref).astype(MXB)
    branch_one = dot(attn_one, so_ref[...]) + mode(SO_BIAS)
    field_one = field + mode(2) * branch_one
    normed_two, rate_two = normalise(field_one)
    hidden_two = (normed_two * (1.0 + mode(4)) + mode(3)).astype(MXB)
    mixed = (dot(hidden_two, t_ref[...]) + wide(modes_ref, T_BIAS, 3)).astype(MXB)
    row_at = lax.broadcasted_iota(jnp.int32, (cell, 2 * cell), 0)
    lane_at = lax.broadcasted_iota(jnp.int32, (cell, 2 * cell), 1)
    mask = jnp.where(lax.rem(row_at, GROUP) == lax.rem(lane_at, GROUP), 0.0, -1e30).astype(F32)
    exact = []
    rounded = []
    queries = []
    attn_rows = []
    for g in range(groups):
        of_group = mixed[g * cell : (g + 1) * cell]
        attn_parts = []
        for pair in range(pairs):
            lanes = slice(2 * HEAD_DIM * pair, 2 * HEAD_DIM * (pair + 1))
            query = jnp.concatenate(halves(of_group[:, lanes] * MXB(scale_factor)), axis=0)
            queries.append(query)
            scores = dot_nt(of_group[:, width:][:, lanes], query) + mask
            exponent = jnp.exp(scores - jnp.max(scores, axis=0, keepdims=True))
            weights = exponent * (1.0 / jnp.sum(exponent, axis=0, keepdims=True))
            exact.append(weights)
            rounded.append(weights.astype(MXB))
            both = dot_tn(of_group[:, 2 * width :][:, lanes], rounded[-1])
            attn_parts.append(jnp.concatenate([both[:HEAD_DIM, :cell], both[HEAD_DIM:, cell:]], axis=0).T.astype(MXB))
        attn_rows.append(jnp.concatenate(attn_parts, axis=1))
    attn_two = jnp.concatenate(attn_rows, axis=0)
    branch_two = dot(attn_two, to_ref[...]) + mode(TO_BIAS)
    field_two = field_one + mode(5) * branch_two
    normed_three, rate_three = normalise(field_two)
    hidden_three = (normed_three * (1.0 + mode(7)) + mode(6)).astype(MXB)
    inner = dot(hidden_three, in_ref[...]) + wide(modes_ref, IN_BIAS, in_ref.shape[1] // width)
    square = inner * inner
    bend = jnp.tanh(inner * (GELU_RATE + GELU_RATE * 0.044715 * square))
    half_up = 0.5 + 0.5 * bend
    active = (inner * half_up).astype(MXB)
    slope = half_up + inner * (0.5 - 0.5 * bend * bend) * (GELU_RATE + 3.0 * GELU_RATE * 0.044715 * square)
    branch_three = dot(active, out_ref[...]) + mode(OUT_BIAS)
    block_ref[...] = scatter(field_two + mode(8) * branch_three).astype(MXB)

    grad_field = gather(og_ref).astype(F32) * mode(WEIGHT)
    sums_ref[8] += eight_rows(grad_field * branch_three)
    grad_branch = (mode(8) * grad_field).astype(MXB)
    grad_out_ref[...] += dot_tn(grad_branch, active)
    sums_ref[11] += eight_rows(grad_branch.astype(F32))
    grad_inner = (dot_nt(grad_branch, out_ref[...]) * slope).astype(MXB)
    grad_in_ref[...] += dot_tn(hidden_three, grad_inner)
    in_sums_ref[...] += eight_rows(grad_inner.astype(F32))
    grad_hidden = dot_nt(grad_inner, in_ref[...])
    sums_ref[6] += eight_rows(grad_hidden)
    sums_ref[7] += eight_rows(grad_hidden * normed_three)
    grad_field = grad_field + normalise_back(grad_hidden, normed_three, rate_three, mode(7))

    sums_ref[5] += eight_rows(grad_field * branch_two)
    grad_branch = (mode(5) * grad_field).astype(MXB)
    grad_to_ref[...] += dot_tn(attn_two, grad_branch)
    sums_ref[10] += eight_rows(grad_branch.astype(F32))
    grad_attn = dot_nt(grad_branch, to_ref[...]).astype(MXB)
    mix_rows = []
    for g in range(groups):
        of_group = mixed[g * cell : (g + 1) * cell]
        grad_queries = []
        grad_keys = []
        grad_values = []
        for pair in range(pairs):
            lanes = slice(2 * HEAD_DIM * pair, 2 * HEAD_DIM * (pair + 1))
            grad = jnp.concatenate(halves(grad_attn[g * cell : (g + 1) * cell, lanes]), axis=0)
            at = g * pairs + pair
            grad_weights = dot_nt(of_group[:, 2 * width :][:, lanes], grad)
            delta = jnp.sum(exact[at] * grad_weights, axis=0, keepdims=True)
            term = (exact[at] * (grad_weights - delta)).astype(MXB)
            both = dot_tn(of_group[:, width:][:, lanes], term)
            grad_query = jnp.concatenate([both[:HEAD_DIM, :cell], both[HEAD_DIM:, cell:]], axis=0).T
            grad_queries.append((grad_query * scale_factor).astype(MXB))
            grad_keys.append(dot(term, queries[at]).astype(MXB))
            grad_values.append(dot(rounded[at], grad).astype(MXB))
        mix_rows.append(jnp.concatenate(grad_queries + grad_keys + grad_values, axis=1))
    grad_mix = jnp.concatenate(mix_rows, axis=0)
    grad_t_ref[...] += dot_tn(hidden_two, grad_mix)
    t_sums_ref[...] += eight_rows(grad_mix.astype(F32))
    grad_hidden = dot_nt(grad_mix, t_ref[...])
    sums_ref[3] += eight_rows(grad_hidden)
    sums_ref[4] += eight_rows(grad_hidden * normed_two)
    grad_field = grad_field + normalise_back(grad_hidden, normed_two, rate_two, mode(4))

    sums_ref[2] += eight_rows(grad_field * branch_one)
    grad_branch = (mode(2) * grad_field).astype(MXB)
    grad_so_ref[...] += dot_tn(attn_one, grad_branch)
    sums_ref[9] += eight_rows(grad_branch.astype(F32))
    g1_ref[...] = scatter(grad_field)
    grad_attn = scatter(dot_nt(grad_branch, so_ref[...])).astype(MXB)

    @pl.when(at_step == 0)
    def _():
        greeted(peers)

    def sent(at_step):
        da_keep(at_step).wait()
        for step, peer, _ in peers:
            da_copy(at_step, step, peer).wait_send()

    @pl.when(at_step >= 2)
    def _():
        sent(at_step - 2)

    da_ref[lax.rem(at_step, 2)] = grad_attn
    da_keep(at_step).start()
    for step, peer, _ in peers:
        da_copy(at_step, step, peer).start()

    @pl.when(at_step == steps - 1)
    def _():
        @pl.when(steps > 1)
        def _():
            sent(steps - 2)

        sent(steps - 1)
        for step, _, source in peers:
            da_landed(step, source).wait_recv()


def whole_spec(shape):
    rank = len(shape)
    return pl.BlockSpec(shape, lambda *_: (0,) * rank, pipeline_mode=pl.Buffered(1))


def acc_spec(shape):
    rank = len(shape)
    return pl.BlockSpec(shape, lambda *_: (0,) * rank)


def params(number):
    return pltpu.CompilerParams(vmem_limit_bytes=VMEM_BYTES, collective_id=number, has_side_effects=True)


def any_spec():
    return pl.BlockSpec(memory_space=pl.ANY)


def cost(flops, moved):
    return pl.CostEstimate(flops=flops, bytes_accessed=moved, transcendentals=0)


def fast_body(
    tokens, conditioning, timesteps, out_grad, ada_weight, ada_bias, spatial_proj, spatial_bias, spatial_out,
    spatial_out_bias, temporal_proj, temporal_bias, temporal_out, temporal_out_bias, hidden_in, hidden_in_bias,
    hidden_out, hidden_out_bias,
):
    _, frames, stripe, width = tokens.shape
    hidden = hidden_in.shape[1]
    pairs = width // (2 * HEAD_DIM)
    cond_act = jax.nn.silu(conditioning.astype(F32)).astype(MXB)
    modes = jnp.dot(cond_act, ada_weight, preferred_element_type=F32) + ada_bias
    slope = jnp.tan((timesteps.astype(F32) / TSTEPS + 0.008) / 1.008 * (0.5 * math.pi))
    loss_weight = jnp.minimum(1.0, 5.0 * slope * slope)
    blank = jnp.zeros((width,), F32)
    modes = jnp.concatenate(
        [
            modes.reshape(-1),
            spatial_bias[:width], blank, spatial_bias[width:],
            temporal_bias[:width], blank, temporal_bias[width:],
            spatial_out_bias, temporal_out_bias, hidden_out_bias, hidden_in_bias,
            jnp.broadcast_to(loss_weight, (width,)),
            cond_act.astype(F32).reshape(-1),
        ]
    ).reshape(ROWS, width)

    x_patches = tokens[0]
    count = lax.axis_size("sp")
    mine, patches = frames // count, stripe * count
    block = min(1024, patches)
    frame_shape = jax.ShapeDtypeStruct((mine, patches, width), MXB)
    patch_shape = jax.ShapeDtypeStruct((frames, stripe, width), MXB)
    dma = pltpu.SemaphoreType.DMA
    x_frames, queries, keys, values, attn_frames, attn_patches, logs = pl.pallas_call(
        partial(spatial_forward, rows=256, block=block, part=512, count=count),
        in_specs=[any_spec()] + [pl.BlockSpec(memory_space=pltpu.VMEM)] * 2,
        out_specs=[any_spec()] * 6 + [pl.BlockSpec(memory_space=pltpu.VMEM)],
        out_shape=[frame_shape] * 5 + [patch_shape, jax.ShapeDtypeStruct((mine, pairs, 2, patches), F32)],
        scratch_shapes=[pltpu.VMEM((mine, patches, width), MXB)] * 5
        + [pltpu.VMEM((2 * pairs, HEAD_DIM + 16, patches), MXB)]
        + [dma((mine, count)), dma((mine, count)), dma((mine,))]
        + [dma((mine, pairs, count)), dma((mine, pairs, count)), dma((mine, pairs)), dma((5, mine))],
        compiler_params=params(0),
        cost_estimate=cost(10**11, 10**7),
    )(x_patches, modes, spatial_proj)

    tile_spec = pl.BlockSpec((frames, TILE, width), lambda i: (0, i, 0))
    small = (modes, spatial_out, temporal_proj, temporal_out, hidden_in, hidden_out)
    sums_shapes = [
        (width, width), (width, 3 * width), (width, width), (width, hidden), (width, hidden),
        (12, 8, width), (8, 3 * width), (8, hidden),
    ]
    out_shapes = [
        patch_shape,
        jax.ShapeDtypeStruct((frames, stripe, width), F32),
        frame_shape,
    ] + [jax.ShapeDtypeStruct(s, F32) for s in sums_shapes]
    (
        block_out, g1, da_frames, grad_so, grad_t, grad_to, grad_in, grad_out_turned, sums, t_sums, in_sums,
    ) = pl.pallas_call(
        partial(middle, peer_count=count),
        grid=(stripe // TILE,),
        in_specs=[tile_spec] * 3 + [whole_spec(a.shape) for a in small],
        out_specs=[tile_spec] * 2 + [any_spec()] + [acc_spec(s) for s in sums_shapes],
        out_shape=out_shapes,
        scratch_shapes=[pltpu.VMEM((2, frames, TILE, width), MXB), dma((2, count)), dma((count,)), dma((2,))],
        compiler_params=params(1),
        cost_estimate=cost(10**11, 10**7),
    )(x_patches, attn_patches, out_grad[0], *small)
    frame_spec = pl.BlockSpec((1, patches, width), lambda f: (f, 0, 0))
    log_spec = pl.BlockSpec((1, pairs, 2, patches), lambda f: (f, 0, 0, 0))
    clips = lax.axis_size("clip")
    span_rows = width // clips
    unit = 16 * (-(-span_rows // (16 * count)))
    sum_shapes = [(width, 3 * width), (width, 9 * width), (ROWS, width)]
    dx_patches, grad_sp, grad_ada, total = pl.pallas_call(
        partial(spatial_backward, rows=512, block=block, part=512, count=count, clips=clips),
        grid=(mine,),
        in_specs=[frame_spec] * 5
        + [log_spec, frame_spec, whole_spec((ROWS, width)), whole_spec((width, 3 * width))]
        + [whole_spec(a.shape) for a in (sums, t_sums, in_sums)],
        out_specs=[any_spec()] + [acc_spec(s) for s in sum_shapes],
        out_shape=[patch_shape] + [jax.ShapeDtypeStruct(s, F32) for s in sum_shapes],
        scratch_shapes=[
            pltpu.VMEM((mine, patches, width), MXB),
            pltpu.VMEM((patches, 3 * width), MXB),
            pltpu.VMEM((pairs, 2, patches), F32),
            pltpu.VMEM((patches, 2 * HEAD_DIM), F32),
            pltpu.VMEM((patches, 2 * HEAD_DIM), F32),
            pltpu.VMEM((2, 8, width), F32),
            pltpu.VMEM((8, 3 * width), F32),
            pltpu.VMEM((clips, span_rows, 3 * width), MXB),
            pltpu.VMEM((clips, span_rows, 3 * width), MXB),
            pltpu.VMEM((count, unit, 3 * width), MXB),
            pltpu.VMEM((count, unit, 3 * width), MXB),
            pltpu.VMEM((span_rows, 3 * width), MXB),
            pltpu.VMEM((clips, span_rows, 3 * width), MXB),
            pltpu.VMEM((ROWS, width), F32),
            pltpu.VMEM((count, ROWS, width), F32),
            pltpu.VMEM((ROWS, width), F32),
            pltpu.VMEM((clips, ROWS, width), F32),
            dma((mine, count)),
            dma((mine, count)),
            dma((mine,)),
        ]
        + [dma((clips,))] * 2
        + [dma((count,))] * 4
        + [dma((clips,))] * 2
        + [dma((count,))] * 2
        + [dma((clips,))] * 2,
        compiler_params=params(2),
        cost_estimate=cost(2 * 10**11, 10**7),
    )(da_frames, attn_frames, queries, keys, values, logs, x_frames, modes, spatial_proj, sums, t_sums, in_sums)
    input_grad = (g1 + dx_patches.astype(F32)).astype(MXB)
    early = lax.psum((grad_so, grad_t, grad_to, grad_in, grad_out_turned), ("clip", "sp"))
    flat = total.reshape(-1)

    def lines(first, rows=1):
        return flat[first * width : (first + rows) * width]

    return (
        block_out[None],
        input_grad[None],
        grad_ada,
        lines(0, 9),
        grad_sp,
        jnp.concatenate([lines(SP_BIAS), lines(SP_BIAS + 2)]),
        early[0],
        lines(SO_BIAS),
        early[1],
        jnp.concatenate([lines(T_BIAS), lines(T_BIAS + 2)]),
        early[2],
        lines(TO_BIAS),
        early[3],
        lines(IN_BIAS, hidden // width),
        early[4].T,
        lines(OUT_BIAS),
    )


def chosen(tokens, *others):
    _, frames, stripe, _ = tokens.shape
    if tokens.shape[0] == 1 and frames % lax.axis_size("sp") == 0 and stripe % TILE == 0:
        return fast_body(tokens, *others)
    return body(tokens, *others)


def solution(mesh):
    return jax.shard_map(
        chosen,
        mesh=mesh,
        in_specs=(
            P("clip", None, "sp", None),
            P("clip", None),
            P("clip"),
            P("clip", None, "sp", None),
            P(),
            P(),
            P(),
            P(),
            P(),
            P(),
            P(),
            P(),
            P(),
            P(),
            P(),
            P(),
            P(),
            P(),
        ),
        out_specs=(
            P("clip", None, "sp", None),
            P("clip", None, "sp", None),
            P(),
            P(),
            P(),
            P(),
            P(),
            P(),
            P(),
            P(),
            P(),
            P(),
            P(),
            P(),
            P(),
            P(),
        ),
        check_vma=False,
    )
```

```python
from functools import partial, reduce
import math

import jax
import jax.numpy as jnp
from jax import lax
from jax.experimental import pallas as pl
from jax.experimental.pallas import tpu as pltpu
from jax.sharding import PartitionSpec as P

HEADS = 6
HEAD_DIM = 64
FRAME_BLOCK = 8
TSTEPS = 1000
GELU_RATE = math.sqrt(2.0 / math.pi)
SP_BIAS = 9
T_BIAS = 12
SO_BIAS = 15
TO_BIAS = 16
OUT_BIAS = 17
IN_BIAS = 18
WEIGHT = 22
COND = 23
ROWS = 24


def modulate(field, shift, scale):
    centred = field - jnp.mean(field, axis=-1, keepdims=True)
    normed = centred * lax.rsqrt(jnp.mean(centred * centred, axis=-1, keepdims=True) + 1e-06)
    return normed * (1.0 + scale) + shift


def loss_weights(timesteps):
    phase = (timesteps.astype(jnp.float32) / TSTEPS + 0.008) / 1.008 * (0.5 * math.pi)
    slope = jnp.tan(phase)
    return jnp.minimum(1.0, 5.0 * slope * slope)


def split_heads(array):
    return array.reshape(array.shape[:-1] + (HEADS, HEAD_DIM))


def join_heads(array):
    return array.reshape(array.shape[:-2] + (HEADS * HEAD_DIM,))


def attend(queries, keys, values):
    scores = jnp.einsum(
        "csqhe,cskhe->cshqk", queries, keys, preferred_element_type=jnp.float32
    ) * HEAD_DIM ** (-0.5)
    row_max = jnp.max(scores, axis=-1, keepdims=True)
    exponent = jnp.exp(scores - row_max)
    total = jnp.sum(exponent, axis=-1, keepdims=True)
    soft_weights = (exponent / total).astype(jnp.bfloat16)
    mixed = jnp.einsum(
        "cshqk,cskhe->csqhe", soft_weights, values, preferred_element_type=jnp.float32
    )
    return (mixed, row_max[..., 0] + jnp.log(total[..., 0]))


def probabilities(queries, keys, values, grads, log_total):
    scores = jnp.einsum(
        "csqhe,cskhe->cshqk", queries, keys, preferred_element_type=jnp.float32
    ) * HEAD_DIM ** (-0.5)
    soft_weights = jnp.exp(scores - log_total[..., None])
    grad_weights = jnp.einsum(
        "csqhe,cskhe->cshqk", grads, values, preferred_element_type=jnp.float32
    )
    return (soft_weights, grad_weights)


def query_pass(queries, keys, values, grads, log_total):
    soft_weights, grad_weights = probabilities(queries, keys, values, grads, log_total)
    delta = jnp.sum(soft_weights * grad_weights, axis=-1)
    grad_scores = (soft_weights * (grad_weights - delta[..., None]) * HEAD_DIM ** (-0.5)).astype(
        jnp.bfloat16
    )
    grad_queries = jnp.einsum(
        "cshqk,cskhe->csqhe", grad_scores, keys, preferred_element_type=jnp.float32
    )
    return (grad_queries, delta)


def key_pass(queries, keys, values, grads, log_total, delta):
    soft_weights, grad_weights = probabilities(queries, keys, values, grads, log_total)
    grad_scores = (soft_weights * (grad_weights - delta[..., None]) * HEAD_DIM ** (-0.5)).astype(
        jnp.bfloat16
    )
    grad_keys = jnp.einsum(
        "cshqk,csqhe->cskhe", grad_scores, queries, preferred_element_type=jnp.float32
    )
    grad_values = jnp.einsum(
        "cshqk,csqhe->cskhe",
        soft_weights.astype(jnp.bfloat16),
        grads,
        preferred_element_type=jnp.float32,
    )
    return jnp.concatenate([join_heads(grad_keys), join_heads(grad_values)], axis=-1)


def column_sums(array):
    return jnp.sum(array.astype(jnp.float32), axis=(0, 1, 2))


def body(
    tokens,
    conditioning,
    timesteps,
    out_grad,
    ada_weight,
    ada_bias,
    spatial_proj,
    spatial_bias,
    spatial_out,
    spatial_out_bias,
    temporal_proj,
    temporal_bias,
    temporal_out,
    temporal_out_bias,
    hidden_in,
    hidden_in_bias,
    hidden_out,
    hidden_out_bias,
):
    clips, frames, stripe, width = tokens.shape
    blocks = frames // FRAME_BLOCK
    scale_factor = HEAD_DIM ** (-0.5)
    field = tokens.astype(jnp.float32)
    cond_act = jax.nn.silu(conditioning.astype(jnp.float32)).astype(jnp.bfloat16)
    modes = jnp.dot(cond_act, ada_weight, preferred_element_type=jnp.float32) + ada_bias
    modes = modes.reshape(clips, 9, 1, 1, width)
    hidden_one, back_one = jax.vjp(modulate, field, modes[:, 0], modes[:, 1])
    hidden_one = hidden_one.astype(jnp.bfloat16)
    query_mix = jnp.einsum(
        "cfpd,de->cfpe", hidden_one, spatial_proj[:, :width], preferred_element_type=jnp.float32
    )
    queries = (query_mix + spatial_bias[:width]).astype(jnp.bfloat16)
    keyval_mix = jnp.einsum(
        "cfpd,de->cfpe", hidden_one, spatial_proj[:, width:], preferred_element_type=jnp.float32
    )
    keyval_bias = jnp.concatenate([jnp.zeros((width,), jnp.float32), spatial_bias[width:]])
    keyvals = (keyval_mix + keyval_bias).astype(jnp.bfloat16)
    query_heads = split_heads(queries)
    mixed_parts = []
    log_parts = []
    for index in range(blocks):
        first = index * FRAME_BLOCK
        whole = lax.all_gather(keyvals[:, first : first + FRAME_BLOCK], "sp", axis=2, tiled=True)
        mixed_part, log_part = attend(
            query_heads[:, first : first + FRAME_BLOCK],
            split_heads(whole[..., :width]),
            split_heads(whole[..., width:]),
        )
        mixed_parts.append(join_heads(mixed_part))
        log_parts.append(log_part)
    attn_one = jnp.concatenate(mixed_parts, axis=1).astype(jnp.bfloat16)
    spatial_log = jnp.concatenate(log_parts, axis=1)
    branch_one = (
        jnp.einsum("cfpd,de->cfpe", attn_one, spatial_out, preferred_element_type=jnp.float32)
        + spatial_out_bias
    )
    field_one = field + modes[:, 2] * branch_one
    hidden_two, back_two = jax.vjp(modulate, field_one, modes[:, 3], modes[:, 4])
    hidden_two = hidden_two.astype(jnp.bfloat16)
    time_mix = jnp.einsum(
        "cfpd,de->cfpe", hidden_two, temporal_proj, preferred_element_type=jnp.float32
    )
    time_queries = split_heads((time_mix[..., :width] + temporal_bias[:width]).astype(jnp.bfloat16))
    time_keys = split_heads(time_mix[..., width : 2 * width].astype(jnp.bfloat16))
    time_values = split_heads(
        (time_mix[..., 2 * width :] + temporal_bias[width:]).astype(jnp.bfloat16)
    )
    time_scores = (
        jnp.einsum(
            "cfphe,cgphe->cphfg", time_queries, time_keys, preferred_element_type=jnp.float32
        )
        * scale_factor
    )
    time_max = jnp.max(time_scores, axis=-1, keepdims=True)
    time_exponent = jnp.exp(time_scores - time_max)
    time_weights = time_exponent / jnp.sum(time_exponent, axis=-1, keepdims=True)
    time_rounded = time_weights.astype(jnp.bfloat16)
    attn_two = join_heads(
        jnp.einsum(
            "cphfg,cgphe->cfphe", time_rounded, time_values, preferred_element_type=jnp.float32
        )
    ).astype(jnp.bfloat16)
    branch_two = (
        jnp.einsum("cfpd,de->cfpe", attn_two, temporal_out, preferred_element_type=jnp.float32)
        + temporal_out_bias
    )
    field_two = field_one + modes[:, 5] * branch_two
    hidden_three, back_three = jax.vjp(modulate, field_two, modes[:, 6], modes[:, 7])
    hidden_three = hidden_three.astype(jnp.bfloat16)
    inner = (
        jnp.einsum("cfpd,dk->cfpk", hidden_three, hidden_in, preferred_element_type=jnp.float32)
        + hidden_in_bias
    )
    active, gelu_back = jax.vjp(partial(jax.nn.gelu, approximate=True), inner)
    active = active.astype(jnp.bfloat16)
    branch_three = (
        jnp.einsum("cfpk,kd->cfpd", active, hidden_out, preferred_element_type=jnp.float32)
        + hidden_out_bias
    )
    block_out = (field_two + modes[:, 8] * branch_three).astype(jnp.bfloat16)
    weights = loss_weights(timesteps)
    grad_field = out_grad.astype(jnp.float32) * weights[:, None, None, None]
    grad_gate_three = jnp.sum(grad_field * branch_three, axis=(1, 2))
    grad_branch = (modes[:, 8] * grad_field).astype(jnp.bfloat16)
    grad_hidden_out = jnp.einsum(
        "cfpk,cfpd->kd", active, grad_branch, preferred_element_type=jnp.float32
    )
    grad_hidden_out_bias = column_sums(grad_branch)
    grad_active = jnp.einsum(
        "cfpd,kd->cfpk", grad_branch, hidden_out, preferred_element_type=jnp.float32
    )
    grad_inner = gelu_back(grad_active)[0].astype(jnp.bfloat16)
    grad_hidden_in = jnp.einsum(
        "cfpd,cfpk->dk", hidden_three, grad_inner, preferred_element_type=jnp.float32
    )
    grad_hidden_in_bias = column_sums(grad_inner)
    grad_hidden = jnp.einsum(
        "cfpk,dk->cfpd", grad_inner, hidden_in, preferred_element_type=jnp.float32
    )
    grad_input, grad_shift_three, grad_scale_three = back_three(grad_hidden)
    grad_field = grad_field + grad_input
    grad_gate_two = jnp.sum(grad_field * branch_two, axis=(1, 2))
    grad_branch = (modes[:, 5] * grad_field).astype(jnp.bfloat16)
    grad_temporal_out = jnp.einsum(
        "cfpd,cfpe->de", attn_two, grad_branch, preferred_element_type=jnp.float32
    )
    grad_temporal_out_bias = column_sums(grad_branch)
    grad_attn = split_heads(
        jnp.einsum(
            "cfpe,de->cfpd", grad_branch, temporal_out, preferred_element_type=jnp.float32
        ).astype(jnp.bfloat16)
    )
    grad_weights = jnp.einsum(
        "cfphe,cgphe->cphfg", grad_attn, time_values, preferred_element_type=jnp.float32
    )
    delta = jnp.sum(time_weights * grad_weights, axis=-1, keepdims=True)
    grad_scores = (time_weights * (grad_weights - delta) * scale_factor).astype(jnp.bfloat16)
    grad_time_queries = jnp.einsum(
        "cphfg,cgphe->cfphe", grad_scores, time_keys, preferred_element_type=jnp.float32
    )
    grad_time_keys = jnp.einsum(
        "cphfg,cfphe->cgphe", grad_scores, time_queries, preferred_element_type=jnp.float32
    )
    grad_time_values = jnp.einsum(
        "cphfg,cfphe->cgphe", time_rounded, grad_attn, preferred_element_type=jnp.float32
    )
    grad_time_mix = jnp.concatenate(
        [join_heads(grad_time_queries), join_heads(grad_time_keys), join_heads(grad_time_values)],
        axis=-1,
    ).astype(jnp.bfloat16)
    grad_temporal_proj = jnp.einsum(
        "cfpd,cfpe->de", hidden_two, grad_time_mix, preferred_element_type=jnp.float32
    )
    grad_temporal_bias = jnp.concatenate(
        [column_sums(grad_time_mix[..., :width]), column_sums(grad_time_mix[..., 2 * width :])]
    )
    grad_hidden = jnp.einsum(
        "cfpe,de->cfpd", grad_time_mix, temporal_proj, preferred_element_type=jnp.float32
    )
    grad_input, grad_shift_two, grad_scale_two = back_two(grad_hidden)
    grad_field = grad_field + grad_input
    grad_gate_one = jnp.sum(grad_field * branch_one, axis=(1, 2))
    grad_branch = (modes[:, 2] * grad_field).astype(jnp.bfloat16)
    grad_spatial_out = jnp.einsum(
        "cfpd,cfpe->de", attn_one, grad_branch, preferred_element_type=jnp.float32
    )
    grad_spatial_out_bias = column_sums(grad_branch)
    grad_attn = jnp.einsum(
        "cfpe,de->cfpd", grad_branch, spatial_out, preferred_element_type=jnp.float32
    ).astype(jnp.bfloat16)
    query_parts = []
    key_parts = []
    for index in range(blocks):
        first = index * FRAME_BLOCK
        whole = lax.all_gather(keyvals[:, first : first + FRAME_BLOCK], "sp", axis=2, tiled=True)
        piece = query_heads[:, first : first + FRAME_BLOCK]
        grad_piece = split_heads(grad_attn[:, first : first + FRAME_BLOCK])
        log_piece = spatial_log[:, first : first + FRAME_BLOCK]
        grad_query_part, delta = query_pass(
            piece,
            split_heads(whole[..., :width]),
            split_heads(whole[..., width:]),
            grad_piece,
            log_piece,
        )
        term = key_pass(
            piece,
            split_heads(whole[..., :width]),
            split_heads(whole[..., width:]),
            grad_piece,
            log_piece,
            delta,
        )
        owned = lax.psum_scatter(
            jnp.transpose(term, (2, 0, 1, 3)).astype(jnp.bfloat16),
            "sp",
            scatter_dimension=0,
            tiled=True,
        ).astype(jnp.float32)
        query_parts.append(join_heads(grad_query_part))
        key_parts.append(jnp.transpose(owned, (1, 2, 0, 3)))
    grad_queries = jnp.concatenate(query_parts, axis=1)
    grad_keyvals = jnp.concatenate(key_parts, axis=1)
    grad_queries = grad_queries.astype(jnp.bfloat16)
    grad_keyvals = grad_keyvals.astype(jnp.bfloat16)
    grad_spatial_proj = jnp.concatenate(
        [
            jnp.einsum(
                "cfpd,cfpe->de", hidden_one, grad_queries, preferred_element_type=jnp.float32
            ),
            jnp.einsum(
                "cfpd,cfpe->de", hidden_one, grad_keyvals, preferred_element_type=jnp.float32
            ),
        ],
        axis=1,
    )
    grad_spatial_bias = jnp.concatenate(
        [column_sums(grad_queries), column_sums(grad_keyvals[..., width:])]
    )
    grad_hidden = jnp.einsum(
        "cfpe,de->cfpd", grad_queries, spatial_proj[:, :width], preferred_element_type=jnp.float32
    )
    grad_hidden = grad_hidden + jnp.einsum(
        "cfpe,de->cfpd", grad_keyvals, spatial_proj[:, width:], preferred_element_type=jnp.float32
    )
    grad_input, grad_shift_one, grad_scale_one = back_one(grad_hidden)
    input_grad = (grad_field + grad_input).astype(jnp.bfloat16)
    grad_modes = jnp.stack(
        [
            grad_shift_one.reshape(clips, width),
            grad_scale_one.reshape(clips, width),
            grad_gate_one,
            grad_shift_two.reshape(clips, width),
            grad_scale_two.reshape(clips, width),
            grad_gate_two,
            grad_shift_three.reshape(clips, width),
            grad_scale_three.reshape(clips, width),
            grad_gate_three,
        ],
        axis=1,
    ).reshape(clips, 9 * width)
    grad_ada_weight = jnp.dot(
        cond_act.astype(jnp.float32).T, grad_modes, precision=lax.Precision.HIGHEST
    )
    grad_ada_bias = jnp.sum(grad_modes, axis=0)
    summed = lax.psum(
        (
            grad_ada_weight,
            grad_ada_bias,
            grad_spatial_proj,
            grad_spatial_bias,
            grad_spatial_out,
            grad_spatial_out_bias,
            grad_temporal_proj,
            grad_temporal_bias,
            grad_temporal_out,
            grad_temporal_out_bias,
            grad_hidden_in,
            grad_hidden_in_bias,
            grad_hidden_out,
            grad_hidden_out_bias,
        ),
        ("clip", "sp"),
    )
    return (
        block_out,
        input_grad,
        summed[0],
        summed[1],
        summed[2],
        summed[3],
        summed[4],
        summed[5],
        summed[6],
        summed[7],
        summed[8],
        summed[9],
        summed[10],
        summed[11],
        summed[12],
        summed[13],
    )


MXB = jnp.bfloat16
F32 = jnp.float32
TILE = 32
GROUP = 8
VMEM_BYTES = 60 * 2**20


def dot(left, right):
    return jnp.dot(left, right, preferred_element_type=F32)


def dot_nt(left, right):
    return lax.dot_general(left, right, (((1,), (1,)), ((), ())), preferred_element_type=F32)


def dot_tn(left, right):
    return lax.dot_general(left, right, (((0,), (0,)), ((), ())), preferred_element_type=F32)


def turned(array):
    return array.astype(F32).T.astype(array.dtype)


def normalise(field):
    centred = field - jnp.mean(field, axis=-1, keepdims=True)
    rate = lax.rsqrt(jnp.mean(centred * centred, axis=-1, keepdims=True) + 1e-06)
    return centred * rate, rate


def normalise_back(grad, normed, rate, scale):
    inner = grad * (1.0 + scale)
    mean = jnp.mean(inner, axis=-1, keepdims=True)
    slope = jnp.mean(inner * normed, axis=-1, keepdims=True)
    return rate * (inner - mean - normed * slope)


def eight_rows(array):
    return jnp.sum(array.reshape(array.shape[0] // 8, 8, array.shape[1]), axis=0)


def wide(ref, first, rows):
    return jnp.concatenate([ref[first + row : first + row + 1, :] for row in range(rows)], axis=1)


def low_lanes():
    return lax.broadcasted_iota(jnp.int32, (1, 2 * HEAD_DIM), 1) < HEAD_DIM


def halves(pair):
    low = low_lanes()
    zero = jnp.zeros_like(pair)
    return jnp.where(low, pair, zero), jnp.where(low, zero, pair)


def others(count, axis="sp"):
    me = lax.axis_index(axis)
    return me, [(step, lax.rem(me + step, count), lax.rem(me + count - step, count)) for step in range(1, count)]


def send(source, target, send_sem, recv_sem, peer, axis="sp"):
    return pltpu.make_async_remote_copy(
        src_ref=source, dst_ref=target, send_sem=send_sem, recv_sem=recv_sem,
        device_id={axis: peer}, device_id_type=pl.DeviceIdType.MESH,
    )


def greet(peers, axis="sp"):
    barrier = pltpu.get_barrier_semaphore()
    for _, peer, _ in peers:
        pl.semaphore_signal(barrier, inc=1, device_id={axis: peer}, device_id_type=pl.DeviceIdType.MESH)


def greeted(peers):
    pl.semaphore_wait(pltpu.get_barrier_semaphore(), len(peers))


def spatial_forward(
    tokens_ref, modes_ref, proj_ref,
    x_out, q_out, k_out, v_out, attn_out, patches_out, log_ref,
    x_ref, q_ref, k_ref, v_ref, attn_ref, turned_ref, mixed_ref, top_ref,
    x_send, x_recv, x_own, a_send, a_recv, a_own, save_sem,
    block, part, count,
):
    mine, tokens, width = x_ref.shape
    stripe = tokens // count
    pairs = width // (2 * HEAD_DIM)
    near = block // stripe
    soon = patches_out.shape[1]
    me, peers = others(count)
    shift = modes_ref[0:1, :]
    scale = modes_ref[1:2, :]
    bias = wide(modes_ref, SP_BIAS, 3)

    def x_copy(frame, peer):
        return send(
            tokens_ref.at[peer * mine + frame],
            x_ref.at[frame, pl.ds(pl.multiple_of(me * stripe, stripe), stripe), :],
            x_send.at[frame, peer], x_recv.at[frame, me], peer,
        )

    def x_landed(frame, source):
        rows = x_ref.at[frame, pl.ds(pl.multiple_of(source * stripe, stripe), stripe), :]
        return send(rows, rows, x_send.at[frame, source], x_recv.at[frame, source], source)

    def x_keep(frame):
        return pltpu.make_async_copy(
            tokens_ref.at[me * mine + frame],
            x_ref.at[frame, pl.ds(pl.multiple_of(me * stripe, stripe), stripe), :],
            x_own.at[frame],
        )

    def saves(frame):
        return [
            pltpu.make_async_copy(held.at[frame], kept.at[frame], save_sem.at[place, frame])
            for place, (held, kept) in enumerate(
                ((x_ref, x_out), (q_ref, q_out), (k_ref, k_out), (v_ref, v_out), (attn_ref, attn_out))
            )
        ]

    def a_copy(frame, pair, peer):
        lanes = pl.ds(pl.multiple_of(pair * 2 * HEAD_DIM, 2 * HEAD_DIM), 2 * HEAD_DIM)
        return send(
            attn_ref.at[frame, pl.ds(pl.multiple_of(peer * stripe, stripe), soon), lanes],
            patches_out.at[me * mine + frame, :, lanes],
            a_send.at[frame, pair, peer], a_recv.at[frame, pair, me], peer,
        )

    def a_landed(frame, pair, peer):
        lanes = pl.ds(pl.multiple_of(pair * 2 * HEAD_DIM, 2 * HEAD_DIM), 2 * HEAD_DIM)
        return send(
            attn_ref.at[frame, pl.ds(pl.multiple_of(peer * stripe, stripe), soon), lanes],
            patches_out.at[peer * mine + frame, :, lanes],
            a_send.at[frame, pair, peer], a_recv.at[frame, pair, peer], peer,
        )

    def a_keep(frame, pair):
        lanes = pl.ds(pl.multiple_of(pair * 2 * HEAD_DIM, 2 * HEAD_DIM), 2 * HEAD_DIM)
        return pltpu.make_async_copy(
            attn_ref.at[frame, pl.ds(pl.multiple_of(me * stripe, stripe), soon), lanes],
            patches_out.at[me * mine + frame, :, lanes],
            a_own.at[frame, pair],
        )

    near_source = lax.div(me, near) * near
    far_source = near - near_source

    def x_sends(frame, first, stop, far):
        for place in range(first, stop):
            peer = (far_source if far else near_source) + lax.rem(me + place, near)
            x_copy(frame, peer).start()

    greet(peers)
    greeted(peers)
    for frame in range(mine):
        x_keep(frame).start()
    x_sends(0, 1, near, False)
    x_sends(0, 0, near // 2, True)
    for frame in range(1, mine):
        x_sends(frame, 1, near, False)
    x_sends(0, near // 2, near, True)
    for frame in range(1, mine):
        x_sends(frame, 0, near, True)
    turned_ref[:, :, HEAD_DIM:, :] = jnp.ones(
        (mine, 2 * pairs, turned_ref.shape[2] - HEAD_DIM, tokens), MXB
    )
    mixed_ref[...] = jnp.zeros_like(mixed_ref)
    top_ref[...] = jnp.full_like(top_ref, -1e30)

    def stage(index, carry):
        pair = lax.rem(index, pairs)
        group = lax.div(index, pairs)
        early = group < mine
        place = lax.rem(jnp.maximum(group - mine, 0), 3)
        frame = jnp.where(early, group, lax.div(jnp.maximum(group - mine, 0), 3))

        @pl.when((pair == 0) & (early | (place == 0)))
        def _():
            first_source = jnp.where(early, near_source, far_source)

            def project(index, carry):
                source = first_source + index
                at = pl.ds(pl.multiple_of(source * stripe, stripe), stripe)

                @pl.when(source == me)
                def _():
                    x_keep(frame).wait()

                @pl.when(source != me)
                def _():
                    x_landed(frame, source).wait_recv()

                normed, _ = normalise(x_ref[frame, at, :].astype(F32))
                hidden = (normed * (1.0 + scale) + shift).astype(MXB)
                mixed = dot(hidden, proj_ref[...]) + bias
                q_ref[frame, at, :] = mixed[:, :width].astype(MXB)
                k_ref[frame, at, :] = mixed[:, width : 2 * width].astype(MXB)
                value = mixed[:, 2 * width :].astype(MXB)
                v_ref[frame, at, :] = value
                across = turned(value)
                for head in range(2 * pairs):
                    turned_ref[frame, head, :HEAD_DIM, at] = across[head * HEAD_DIM : (head + 1) * HEAD_DIM]
                return carry

            lax.fori_loop(0, near, project, 0)

            @pl.when(group >= mine)
            def _():
                for copy in saves(frame)[:4]:
                    copy.start()

        query_source = jnp.where(early | (place == 2), near_source, far_source)
        key_source = jnp.where(early | (place == 0), near_source, far_source)
        at = pl.ds(pl.multiple_of(query_source * stripe, block), block)
        lanes = pl.ds(pl.multiple_of(pair * 2 * HEAD_DIM, 2 * HEAD_DIM), 2 * HEAD_DIM)
        spans = [pl.ds(pl.multiple_of(key_source * stripe + first, part), part) for first in range(0, block, part)]
        scores = []
        tops = []
        decays = []
        for side, query in enumerate(halves(q_ref[frame, at, lanes] * MXB(HEAD_DIM**-0.5))):
            each = [dot_nt(k_ref[frame, span, lanes], query) for span in spans]
            top = [jnp.max(s.reshape(part // 8, 8, block), axis=0) for s in each]
            before = top_ref[frame, pair, side : side + 1, at]
            now = jnp.maximum(before, jnp.max(reduce(jnp.maximum, top), axis=0, keepdims=True))
            top_ref[frame, pair, side : side + 1, at] = now
            scores.append(each)
            tops.append(now)
            decays.append(jnp.exp(before - now))
        for side in range(2):
            total = mixed_ref[frame, 2 * pair + side, :, at] * decays[side]
            for span, s in zip(spans, scores[side]):
                weights = jnp.exp(s - tops[side]).astype(MXB)
                total = total + dot(turned_ref[frame, 2 * pair + side, :, span], weights)
            mixed_ref[frame, 2 * pair + side, :, at] = total

        @pl.when((group >= mine) & (place >= 1))
        def _():
            mixed = []
            for side in range(2):
                total = mixed_ref[frame, 2 * pair + side, :, at]
                mass = total[HEAD_DIM : HEAD_DIM + 1]
                log_ref[frame, pair, side : side + 1, at] = tops[side] + jnp.log(mass)
                mixed.append(total[:HEAD_DIM] / mass)
            attn_ref[frame, at, lanes] = jnp.concatenate(mixed, axis=0).T.astype(MXB)
            for other in range(near):
                peer = query_source + other

                @pl.when(peer != me)
                def _():
                    a_copy(frame, pair, peer).start()

                @pl.when(peer == me)
                def _():
                    a_keep(frame, pair).start()

        @pl.when((group >= mine) & (place == 2) & (pair == pairs - 1))
        def _():
            saves(frame)[4].start()

        return carry

    lax.fori_loop(0, 4 * mine * pairs, stage, 0)

    for frame in range(mine):
        for copy in saves(frame):
            copy.wait()
        for _, peer, _ in peers:
            x_copy(frame, peer).wait_send()
        for pair in range(pairs):
            a_keep(frame, pair).wait()
            for _, peer, _ in peers:
                a_copy(frame, pair, peer).wait_send()
                a_landed(frame, pair, peer).wait_recv()


def spatial_backward(
    da_ref, attn_ref, q_ref, k_ref, v_ref, log_ref, x_ref, modes_ref, proj_ref, mid_sums_ref, t_sums_ref, in_sums_ref,
    patches_out, proj_out, row_out,
    grad_proj_ref, dx_ref, mix_ref, delta_ref, dq_ref, dk_ref, dv_ref, across_ref, sums_ref, bias_sums_ref,
    clip_out_ref, clip_in_ref, unit_out_ref, unit_in_ref, piece_ref, all_ref, vec_ref, vec_in_ref, row_ref, row_in_ref,
    send_sem, recv_sem, own_sem, g1_send, g1_recv, g2_send, g2_recv, g3_send, g3_recv, g4_send, g4_recv,
    v1_send, v1_recv, v2_send, v2_recv, rows, part, count, clips,
):
    tokens, width = x_ref.shape[1:]
    mine = dx_ref.shape[0]
    stripe = tokens // count
    frame = pl.program_id(0)
    me, peers = others(count)
    clip, clip_peers = others(clips, "clip")
    span_rows = width // clips
    unit = 16 * (-(-span_rows // (16 * count)))
    owners = span_rows // unit

    def g1_copy(peer, slot):
        return send(
            clip_out_ref.at[peer], clip_in_ref.at[slot], g1_send.at[peer], g1_recv.at[slot], peer, "clip"
        )

    def g2_copy(peer, slot):
        return send(unit_out_ref.at[peer], unit_in_ref.at[slot], g2_send.at[peer], g2_recv.at[slot], peer)

    def g3_copy(peer, slot):
        part_rows = pl.ds(pl.multiple_of(slot * unit, unit), unit)
        return send(piece_ref.at[part_rows, :], piece_ref.at[part_rows, :], g3_send.at[peer], g3_recv.at[slot], peer)

    def g4_copy(peer, slot):
        return send(piece_ref, all_ref.at[slot], g4_send.at[peer], g4_recv.at[slot], peer, "clip")

    def v1_copy(peer, slot):
        return send(vec_ref, vec_in_ref.at[slot], v1_send.at[peer], v1_recv.at[slot], peer)

    def v2_copy(peer, slot):
        return send(row_ref, row_in_ref.at[slot], v2_send.at[peer], v2_recv.at[slot], peer, "clip")

    def dx_copy(frame, peer):
        return send(
            dx_ref.at[frame, pl.ds(pl.multiple_of(peer * stripe, stripe), stripe), :],
            patches_out.at[me * mine + frame], send_sem.at[frame, peer], recv_sem.at[frame, me], peer,
        )

    def dx_landed(frame, peer):
        return send(
            dx_ref.at[frame, pl.ds(pl.multiple_of(peer * stripe, stripe), stripe), :],
            patches_out.at[peer * mine + frame], send_sem.at[frame, peer], recv_sem.at[frame, peer], peer,
        )

    def dx_keep(frame):
        return pltpu.make_async_copy(
            dx_ref.at[frame, pl.ds(pl.multiple_of(me * stripe, stripe), stripe), :],
            patches_out.at[me * mine + frame], own_sem.at[frame],
        )

    @pl.when(frame == 0)
    def _():
        greet(peers)
        greet(clip_peers, "clip")

    pairs = width // (2 * HEAD_DIM)
    scale_factor = HEAD_DIM**-0.5

    @pl.when(frame == 0)
    def _():
        grad_proj_ref[...] = jnp.zeros_like(grad_proj_ref)
        sums_ref[...] = jnp.zeros_like(sums_ref)
        bias_sums_ref[...] = jnp.zeros_like(bias_sums_ref)

    head_of = lax.broadcasted_iota(jnp.int32, (8, width), 1) // HEAD_DIM
    picks = jnp.where(head_of == lax.broadcasted_iota(jnp.int32, (8, width), 0), 1.0, 0.0).astype(MXB)

    def deltas(index, carry):
        at = pl.ds(pl.multiple_of(index * rows, rows), rows)
        product = da_ref[0, at, :].astype(F32) * attn_ref[0, at, :].astype(F32)
        high = product.astype(MXB)
        rest = (product - high.astype(F32)).astype(MXB)
        summed = dot_nt(picks, high) + dot_nt(picks, rest)
        for pair in range(pairs):
            delta_ref[pair, 0:2, at] = summed[2 * pair : 2 * pair + 2]
        return carry

    lax.fori_loop(0, tokens // rows, deltas, 0)

    def turn_keys(pair, carry):
        lanes = pl.ds(pl.multiple_of(pair * 2 * HEAD_DIM, 2 * HEAD_DIM), 2 * HEAD_DIM)
        across_ref[pair] = turned(k_ref[0, :, lanes])
        dq_ref[pair] = jnp.zeros(dq_ref.shape[1:], F32)
        dk_ref[:, lanes] = jnp.zeros((tokens, 2 * HEAD_DIM), F32)
        dv_ref[:, lanes] = jnp.zeros((tokens, 2 * HEAD_DIM), F32)
        return carry

    lax.fori_loop(0, pairs, turn_keys, 0)

    @pl.when(frame == 0)
    def _():
        greeted(peers + clip_peers)

    half = tokens // 2
    near = half // stripe
    near_first = lax.div(me, near) * half
    far_first = half - near_first
    last = frame == mine - 1
    shift = modes_ref[0:1, :]
    scale = modes_ref[1:2, :]

    def hidden_of(at):
        normed, rate = normalise(x_ref[0, at, :].astype(F32))
        return normed, rate, (normed * (1.0 + scale) + shift).astype(MXB)

    def phase_pass(phase, carry):
        def step_pass(index, carry):
            pair = lax.rem(index, pairs)
            step = lax.div(index, pairs) + 3 * phase
            lanes = pl.ds(pl.multiple_of(pair * 2 * HEAD_DIM, 2 * HEAD_DIM), 2 * HEAD_DIM)
            query_first = jnp.where(step >= 2, near_first, far_first)
            key_first = jnp.where(lax.rem(step, 2) == 1, near_first, far_first)
            at = pl.ds(pl.multiple_of(query_first, half), half)
            query = halves(q_ref[0, at, lanes] * MXB(scale_factor))
            grad = halves(da_ref[0, at, lanes])
            query_both = jnp.concatenate(query, axis=0)
            grad_both = jnp.concatenate(grad, axis=0)
            grad_query = [jnp.zeros((HEAD_DIM, half), F32), jnp.zeros((HEAD_DIM, half), F32)]
            for first in range(0, half, part):
                span = pl.ds(pl.multiple_of(key_first + first, part), part)
                keys = k_ref[0, span, lanes]
                values = v_ref[0, span, lanes]
                weights = []
                grad_scores = []
                for side in range(2):
                    scores = dot_nt(keys, query[side])
                    exact = jnp.exp(scores - log_ref[0, pair, side : side + 1, at])
                    grad_weights = dot_nt(values, grad[side])
                    term = (exact * (grad_weights - delta_ref[pair, side : side + 1, at])).astype(MXB)
                    weights.append(exact.astype(MXB))
                    grad_scores.append(term)
                    across = across_ref[pair, side * HEAD_DIM : (side + 1) * HEAD_DIM, span]
                    grad_query[side] = grad_query[side] + dot(across, term)
                dv_ref[span, lanes] += dot(jnp.concatenate(weights, axis=1), grad_both)
                dk_ref[span, lanes] += dot(jnp.concatenate(grad_scores, axis=1), query_both)
            for side in range(2):
                dq_ref[pair, side * HEAD_DIM : (side + 1) * HEAD_DIM, at] += grad_query[side]
            return carry

        lax.fori_loop(0, jnp.where(phase == 0, 3 * pairs, pairs), step_pass, 0)
        first_row = jnp.where(phase == 0, far_first, near_first)

        def weigh(index, carry):
            at = pl.ds(pl.multiple_of(first_row + index * rows, rows), rows)
            for pair in range(pairs):
                lanes = slice(2 * HEAD_DIM * pair, 2 * HEAD_DIM * (pair + 1))
                mix_ref[at, lanes] = (dq_ref[pair, :, at].T * scale_factor).astype(MXB)
            mix_ref[at, width : 2 * width] = dk_ref[at, :].astype(MXB)
            mix_ref[at, 2 * width :] = dv_ref[at, :].astype(MXB)
            _, _, hidden = hidden_of(at)
            grad_mix = mix_ref[at, :]
            grad_proj_ref[...] += dot_tn(hidden, grad_mix)
            bias_sums_ref[...] += eight_rows(grad_mix.astype(F32))
            return carry

        lax.fori_loop(0, half // rows, weigh, 0)

        @pl.when(last & (phase == 1))
        def _():
            for each in range(clips):
                clip_out_ref[each] = grad_proj_ref[each * span_rows : (each + 1) * span_rows, :].astype(MXB)
            for _, peer, _ in clip_peers:
                g1_copy(peer, clip).start()

        def finish(index, carry):
            peer = lax.div(first_row, stripe) + index
            at = pl.ds(pl.multiple_of(first_row + index * stripe, stripe), stripe)
            normed, rate, _ = hidden_of(at)
            grad_hidden = dot_nt(mix_ref[at, :], proj_ref[...])
            sums_ref[0] += eight_rows(grad_hidden)
            sums_ref[1] += eight_rows(grad_hidden * normed)
            dx_ref[frame, at, :] = normalise_back(grad_hidden, normed, rate, scale).astype(MXB)

            @pl.when(peer != me)
            def _():
                dx_copy(frame, peer).start()

            @pl.when(peer == me)
            def _():
                dx_keep(frame).start()

            return carry

        lax.fori_loop(0, near, finish, 0)
        return carry

    lax.fori_loop(0, 2, phase_pass, 0)

    @pl.when(last)
    def _():
        total = grad_proj_ref[pl.ds(pl.multiple_of(clip * span_rows, span_rows), span_rows), :]
        for _, _, source in clip_peers:
            g1_copy(source, source).wait_recv()
            total = total + clip_in_ref[source].astype(F32)
        for owner in range(owners):
            unit_out_ref[owner] = total[owner * unit : (owner + 1) * unit].astype(MXB)

            @pl.when(owner != me)
            def _():
                g2_copy(owner, me).start()

        def row_sum(array):
            return jnp.sum(array, axis=0, keepdims=True)

        def rows_of(array):
            flat = row_sum(array)
            return [flat[:, first : first + width] for first in range(0, flat.shape[1], width)]

        lines = [row_sum(sums_ref[0]), row_sum(sums_ref[1])]
        lines += [row_sum(mid_sums_ref[line]) for line in range(2, 9)]
        lines += rows_of(bias_sums_ref[...]) + rows_of(t_sums_ref[...])
        lines += [row_sum(mid_sums_ref[line]) for line in range(9, 12)]
        lines += rows_of(in_sums_ref[...])
        lines += [modes_ref[COND : COND + 1, :]] * (ROWS - len(lines))
        vec_ref[...] = jnp.concatenate(lines, axis=0)
        for _, peer, _ in peers:
            v1_copy(peer, me).start()

        @pl.when(me < owners)
        def _():
            total = unit_out_ref[me].astype(F32)
            for _, _, source in peers:
                g2_copy(me, source).wait_recv()
                total = total + unit_in_ref[source].astype(F32)
            piece_ref[pl.ds(pl.multiple_of(me * unit, unit), unit), :] = total.astype(MXB)
            for _, peer, _ in peers:
                g3_copy(peer, me).start()

        total = vec_ref[...]
        for _, _, source in peers:
            v1_copy(source, source).wait_recv()
            total = total + vec_in_ref[source]
        at_row = lax.broadcasted_iota(jnp.int32, (ROWS, width), 0)
        row_ref[...] = jnp.where(at_row < COND, total, vec_ref[...])
        for _, peer, _ in clip_peers:
            v2_copy(peer, clip).start()

        for owner in range(owners):

            @pl.when(owner != me)
            def _():
                g3_copy(owner, owner).wait_recv()

        for _, peer, _ in clip_peers:
            g4_copy(peer, clip).start()
        proj_out[pl.ds(pl.multiple_of(clip * span_rows, span_rows), span_rows), :] = piece_ref[...]
        row_in_ref[clip] = row_ref[...]
        for _, _, source in clip_peers:
            v2_copy(source, source).wait_recv()
        row_out[...] = row_in_ref[...]
        for _, _, source in clip_peers:
            g4_copy(source, source).wait_recv()
            proj_out[pl.ds(pl.multiple_of(source * span_rows, span_rows), span_rows), :] = all_ref[source]

        for _, peer, _ in clip_peers:
            g1_copy(peer, clip).wait_send()
            g4_copy(peer, clip).wait_send()
            v2_copy(peer, clip).wait_send()
        for _, peer, _ in peers:
            v1_copy(peer, me).wait_send()

        for owner in range(owners):

            @pl.when(owner != me)
            def _():
                g2_copy(owner, me).wait_send()

        @pl.when(me < owners)
        def _():
            for _, peer, _ in peers:
                g3_copy(peer, me).wait_send()

        for each in range(mine):
            dx_keep(each).wait()
            for _, peer, _ in peers:
                dx_copy(each, peer).wait_send()
                dx_landed(each, peer).wait_recv()


def middle(
    x_ref, soon_ref, og_ref, attn_hbm, modes_ref, so_ref, t_ref, to_ref, in_ref, out_ref,
    block_ref, g1_ref, da_out,
    so_out, t_out, to_out, in_out, out_out, sums_ref, t_sums_ref, in_sums_ref,
    grad_so_ref, grad_t_ref, grad_to_ref, grad_in_ref, grad_out_ref,
    da_ref, attn_ref, late_ref, send_sem, recv_sem, own_sem, late_send, late_recv, late_own, peer_count,
):
    frames, tile, width = x_ref.shape
    count = frames * tile
    pairs = width // (2 * HEAD_DIM)
    scale_factor = HEAD_DIM**-0.5
    mine = frames // peer_count
    steps = pl.num_programs(0)
    stripe = da_out.shape[1] // peer_count
    at_step = pl.program_id(0)
    me, peers = others(peer_count)

    def da_copy(at_step, step, peer):
        first = pl.multiple_of(me * stripe + at_step * tile, tile)
        slot = lax.rem(at_step, 2)
        return send(
            da_ref.at[slot, pl.ds(peer * mine, mine)], da_out.at[:, pl.ds(first, tile), :],
            send_sem.at[slot, step], recv_sem.at[step], peer,
        )

    def da_keep(at_step):
        first = pl.multiple_of(me * stripe + at_step * tile, tile)
        slot = lax.rem(at_step, 2)
        return pltpu.make_async_copy(
            da_ref.at[slot, pl.ds(me * mine, mine)], da_out.at[:, pl.ds(first, tile), :], own_sem.at[slot]
        )

    def da_landed(step, source):
        rows = da_out.at[:, pl.ds(pl.multiple_of(source * stripe, stripe), stripe), :]
        return send(rows, rows, send_sem.at[0, step], recv_sem.at[step], source)

    soon_steps = (stripe - late_ref.shape[1]) // tile
    late = late_ref.shape[1]

    def late_copy(frame, step, peer):
        rows = pl.ds(pl.multiple_of(peer * stripe + stripe - late, tile), late)
        return send(
            attn_hbm.at[frame, rows, :], late_ref.at[me * mine + frame],
            late_send.at[frame, step], late_recv.at[frame, step], peer,
        )

    def late_landed(frame, step, source):
        rows = late_ref.at[source * mine + frame]
        return send(rows, rows, late_send.at[frame, step], late_recv.at[frame, step], source)

    def late_keep(frame):
        rows = pl.ds(pl.multiple_of(me * stripe + stripe - late, tile), late)
        return pltpu.make_async_copy(attn_hbm.at[frame, rows, :], late_ref.at[me * mine + frame], late_own.at[frame])

    @pl.when(at_step == 0)
    def _():
        greet(peers)
        greeted(peers)
        for frame in range(mine):
            late_keep(frame).start()
            for step, peer, _ in peers:
                late_copy(frame, step, peer).start()
        for ref in (grad_so_ref, grad_t_ref, grad_to_ref, grad_in_ref, grad_out_ref, sums_ref, t_sums_ref, in_sums_ref):
            ref[...] = jnp.zeros_like(ref)

    def mode(row):
        return modes_ref[row : row + 1, :]

    @pl.when(at_step < soon_steps)
    def _():
        attn_ref[...] = soon_ref[...]

    @pl.when(at_step == soon_steps)
    def _():
        for frame in range(mine):
            late_keep(frame).wait()
            for step, _, source in peers:
                late_landed(frame, step, source).wait_recv()

    @pl.when(at_step >= soon_steps)
    def _():
        attn_ref[...] = late_ref[:, pl.ds(pl.multiple_of((at_step - soon_steps) * tile, tile), tile), :]

    cell = frames * GROUP
    groups = tile // GROUP

    def gather(ref):
        whole = ref[...].astype(F32)
        return jnp.concatenate(
            [whole[:, g * GROUP : (g + 1) * GROUP, :].reshape(cell, width) for g in range(groups)], axis=0
        )

    def scatter(value):
        return jnp.concatenate(
            [value[g * cell : (g + 1) * cell].reshape(frames, GROUP, width) for g in range(groups)], axis=1
        )

    field = gather(x_ref)
    attn_one = gather(attn_ref).astype(MXB)
    branch_one = dot(attn_one, so_ref[...]) + mode(SO_BIAS)
    field_one = field + mode(2) * branch_one
    normed_two, rate_two = normalise(field_one)
    hidden_two = (normed_two * (1.0 + mode(4)) + mode(3)).astype(MXB)
    mixed = (dot(hidden_two, t_ref[...]) + wide(modes_ref, T_BIAS, 3)).astype(MXB)
    row_at = lax.broadcasted_iota(jnp.int32, (cell, 2 * cell), 0)
    lane_at = lax.broadcasted_iota(jnp.int32, (cell, 2 * cell), 1)
    mask = jnp.where(lax.rem(row_at, GROUP) == lax.rem(lane_at, GROUP), 0.0, -1e30).astype(F32)
    exact = []
    rounded = []
    queries = []
    attn_rows = []
    for g in range(groups):
        of_group = mixed[g * cell : (g + 1) * cell]
        attn_parts = []
        for pair in range(pairs):
            lanes = slice(2 * HEAD_DIM * pair, 2 * HEAD_DIM * (pair + 1))
            query = jnp.concatenate(halves(of_group[:, lanes] * MXB(scale_factor)), axis=0)
            queries.append(query)
            scores = dot_nt(of_group[:, width:][:, lanes], query) + mask
            exponent = jnp.exp(scores - jnp.max(scores, axis=0, keepdims=True))
            weights = exponent * (1.0 / jnp.sum(exponent, axis=0, keepdims=True))
            exact.append(weights)
            rounded.append(weights.astype(MXB))
            both = dot_tn(of_group[:, 2 * width :][:, lanes], rounded[-1])
            attn_parts.append(jnp.concatenate([both[:HEAD_DIM, :cell], both[HEAD_DIM:, cell:]], axis=0).T.astype(MXB))
        attn_rows.append(jnp.concatenate(attn_parts, axis=1))
    attn_two = jnp.concatenate(attn_rows, axis=0)
    branch_two = dot(attn_two, to_ref[...]) + mode(TO_BIAS)
    field_two = field_one + mode(5) * branch_two
    normed_three, rate_three = normalise(field_two)
    hidden_three = (normed_three * (1.0 + mode(7)) + mode(6)).astype(MXB)
    inner = dot(hidden_three, in_ref[...]) + wide(modes_ref, IN_BIAS, in_ref.shape[1] // width)
    square = inner * inner
    bend = jnp.tanh(inner * (GELU_RATE + GELU_RATE * 0.044715 * square))
    half_up = 0.5 + 0.5 * bend
    active = (inner * half_up).astype(MXB)
    slope = half_up + inner * (0.5 - 0.5 * bend * bend) * (GELU_RATE + 3.0 * GELU_RATE * 0.044715 * square)
    branch_three = dot(active, out_ref[...]) + mode(OUT_BIAS)
    block_ref[...] = scatter(field_two + mode(8) * branch_three).astype(MXB)

    grad_field = gather(og_ref).astype(F32) * mode(WEIGHT)
    sums_ref[8] += eight_rows(grad_field * branch_three)
    grad_branch = (mode(8) * grad_field).astype(MXB)
    grad_out_ref[...] += dot_tn(grad_branch, active)
    sums_ref[11] += eight_rows(grad_branch.astype(F32))
    grad_inner = (dot_nt(grad_branch, out_ref[...]) * slope).astype(MXB)
    grad_in_ref[...] += dot_tn(hidden_three, grad_inner)
    in_sums_ref[...] += eight_rows(grad_inner.astype(F32))
    grad_hidden = dot_nt(grad_inner, in_ref[...])
    sums_ref[6] += eight_rows(grad_hidden)
    sums_ref[7] += eight_rows(grad_hidden * normed_three)
    grad_field = grad_field + normalise_back(grad_hidden, normed_three, rate_three, mode(7))

    sums_ref[5] += eight_rows(grad_field * branch_two)
    grad_branch = (mode(5) * grad_field).astype(MXB)
    grad_to_ref[...] += dot_tn(attn_two, grad_branch)
    sums_ref[10] += eight_rows(grad_branch.astype(F32))
    grad_attn = dot_nt(grad_branch, to_ref[...]).astype(MXB)
    mix_rows = []
    for g in range(groups):
        of_group = mixed[g * cell : (g + 1) * cell]
        grad_queries = []
        grad_keys = []
        grad_values = []
        for pair in range(pairs):
            lanes = slice(2 * HEAD_DIM * pair, 2 * HEAD_DIM * (pair + 1))
            grad = jnp.concatenate(halves(grad_attn[g * cell : (g + 1) * cell, lanes]), axis=0)
            at = g * pairs + pair
            grad_weights = dot_nt(of_group[:, 2 * width :][:, lanes], grad)
            delta = jnp.sum(exact[at] * grad_weights, axis=0, keepdims=True)
            term = (exact[at] * (grad_weights - delta)).astype(MXB)
            both = dot_tn(of_group[:, width:][:, lanes], term)
            grad_query = jnp.concatenate([both[:HEAD_DIM, :cell], both[HEAD_DIM:, cell:]], axis=0).T
            grad_queries.append((grad_query * scale_factor).astype(MXB))
            grad_keys.append(dot(term, queries[at]).astype(MXB))
            grad_values.append(dot(rounded[at], grad).astype(MXB))
        mix_rows.append(jnp.concatenate(grad_queries + grad_keys + grad_values, axis=1))
    grad_mix = jnp.concatenate(mix_rows, axis=0)
    grad_t_ref[...] += dot_tn(hidden_two, grad_mix)
    t_sums_ref[...] += eight_rows(grad_mix.astype(F32))
    grad_hidden = dot_nt(grad_mix, t_ref[...])
    sums_ref[3] += eight_rows(grad_hidden)
    sums_ref[4] += eight_rows(grad_hidden * normed_two)
    grad_field = grad_field + normalise_back(grad_hidden, normed_two, rate_two, mode(4))

    sums_ref[2] += eight_rows(grad_field * branch_one)
    grad_branch = (mode(2) * grad_field).astype(MXB)
    grad_so_ref[...] += dot_tn(attn_one, grad_branch)
    sums_ref[9] += eight_rows(grad_branch.astype(F32))
    g1_ref[...] = scatter(grad_field)
    grad_attn = scatter(dot_nt(grad_branch, so_ref[...])).astype(MXB)

    def sent(at_step):
        da_keep(at_step).wait()
        for step, peer, _ in peers:
            da_copy(at_step, step, peer).wait_send()

    @pl.when(at_step >= 2)
    def _():
        sent(at_step - 2)

    da_ref[lax.rem(at_step, 2)] = grad_attn
    da_keep(at_step).start()
    for step, peer, _ in peers:
        da_copy(at_step, step, peer).start()

    @pl.when(at_step == steps - 1)
    def _():
        @pl.when(steps > 1)
        def _():
            sent(steps - 2)

        sent(steps - 1)
        for step, peer, source in peers:
            da_landed(step, source).wait_recv()
            for frame in range(mine):
                late_copy(frame, step, peer).wait_send()
        so_out[...] = grad_so_ref[...].astype(MXB)
        t_out[...] = grad_t_ref[...].astype(MXB)
        to_out[...] = grad_to_ref[...].astype(MXB)
        in_out[...] = grad_in_ref[...].astype(MXB)
        out_out[...] = grad_out_ref[...].astype(MXB)


def whole_spec(shape):
    rank = len(shape)
    return pl.BlockSpec(shape, lambda *_: (0,) * rank, pipeline_mode=pl.Buffered(1))


def acc_spec(shape):
    rank = len(shape)
    return pl.BlockSpec(shape, lambda *_: (0,) * rank)


def params(number):
    return pltpu.CompilerParams(vmem_limit_bytes=VMEM_BYTES, collective_id=number, has_side_effects=True)


def any_spec():
    return pl.BlockSpec(memory_space=pl.ANY)


def cost(flops, moved):
    return pl.CostEstimate(flops=flops, bytes_accessed=moved, transcendentals=0)


def fast_body(
    tokens, conditioning, timesteps, out_grad, ada_weight, ada_bias, spatial_proj, spatial_bias, spatial_out,
    spatial_out_bias, temporal_proj, temporal_bias, temporal_out, temporal_out_bias, hidden_in, hidden_in_bias,
    hidden_out, hidden_out_bias,
):
    _, frames, stripe, width = tokens.shape
    hidden = hidden_in.shape[1]
    pairs = width // (2 * HEAD_DIM)
    cond_act = jax.nn.silu(conditioning.astype(F32)).astype(MXB)
    modes = jnp.dot(cond_act, ada_weight, preferred_element_type=F32) + ada_bias
    slope = jnp.tan((timesteps.astype(F32) / TSTEPS + 0.008) / 1.008 * (0.5 * math.pi))
    loss_weight = jnp.minimum(1.0, 5.0 * slope * slope)
    blank = jnp.zeros((width,), F32)
    pieces = (
        modes.reshape(-1),
        spatial_bias[:width], blank, spatial_bias[width:],
        temporal_bias[:width], blank, temporal_bias[width:],
        spatial_out_bias, temporal_out_bias, hidden_out_bias, hidden_in_bias,
        jnp.broadcast_to(loss_weight, (width,)),
        cond_act.astype(F32).reshape(-1),
    )
    packed = jnp.zeros((ROWS * width,), F32)
    start = 0
    for piece in pieces:
        packed = packed + jnp.pad(piece, (start, ROWS * width - start - piece.size))
        start += piece.size
    modes = packed.reshape(ROWS, width)

    x_patches = tokens[0]
    count = lax.axis_size("sp")
    mine, patches = frames // count, stripe * count
    block = patches // 2
    soon = max(stripe // (2 * TILE), 1) * TILE
    frame_shape = jax.ShapeDtypeStruct((mine, patches, width), MXB)
    patch_shape = jax.ShapeDtypeStruct((frames, stripe, width), MXB)
    dma = pltpu.SemaphoreType.DMA
    x_frames, queries, keys, values, attn_frames, attn_patches, logs = pl.pallas_call(
        partial(spatial_forward, block=block, part=512, count=count),
        in_specs=[any_spec()] + [pl.BlockSpec(memory_space=pltpu.VMEM)] * 2,
        out_specs=[any_spec()] * 6 + [pl.BlockSpec(memory_space=pltpu.VMEM)],
        out_shape=[frame_shape] * 5
        + [
            jax.ShapeDtypeStruct((frames, soon, width), MXB),
            jax.ShapeDtypeStruct((mine, pairs, 2, patches), F32),
        ],
        scratch_shapes=[pltpu.VMEM((mine, patches, width), MXB)] * 5
        + [pltpu.VMEM((mine, 2 * pairs, HEAD_DIM + 16, patches), MXB)]
        + [pltpu.VMEM((mine, 2 * pairs, HEAD_DIM + 16, patches), F32), pltpu.VMEM((mine, pairs, 2, patches), F32)]
        + [dma((mine, count)), dma((mine, count)), dma((mine,))]
        + [dma((mine, pairs, count)), dma((mine, pairs, count)), dma((mine, pairs)), dma((5, mine))],
        compiler_params=params(0),
        cost_estimate=cost(10**11, 10**7),
    )(x_patches, modes, spatial_proj)

    tile_spec = pl.BlockSpec((frames, TILE, width), lambda i: (0, i, 0))
    soon_spec = pl.BlockSpec((frames, TILE, width), lambda i: (0, jnp.minimum(i, soon // TILE - 1), 0))
    small = (modes, spatial_out, temporal_proj, temporal_out, hidden_in, hidden_out)
    sums_shapes = [
        (width, width), (width, 3 * width), (width, width), (width, hidden), (width, hidden),
        (12, 8, width), (8, 3 * width), (8, hidden),
    ]
    out_shapes = [
        patch_shape,
        jax.ShapeDtypeStruct((frames, stripe, width), F32),
        frame_shape,
    ] + [jax.ShapeDtypeStruct(s, MXB if at < 5 else F32) for at, s in enumerate(sums_shapes)]
    (
        block_out, g1, da_frames, grad_so, grad_t, grad_to, grad_in, grad_out_turned, sums, t_sums, in_sums,
    ) = pl.pallas_call(
        partial(middle, peer_count=count),
        grid=(stripe // TILE,),
        in_specs=[tile_spec, soon_spec, tile_spec, any_spec()] + [whole_spec(a.shape) for a in small],
        out_specs=[tile_spec] * 2 + [any_spec()] + [acc_spec(s) for s in sums_shapes],
        out_shape=out_shapes,
        scratch_shapes=[pltpu.VMEM(s, F32) for s in sums_shapes[:5]]
        + [pltpu.VMEM((2, frames, TILE, width), MXB), pltpu.VMEM((frames, TILE, width), MXB)]
        + [pltpu.VMEM((frames, stripe - soon, width), MXB)]
        + [dma((2, count)), dma((count,)), dma((2,))]
        + [dma((mine, count)), dma((mine, count)), dma((mine,))],
        compiler_params=params(1),
        cost_estimate=cost(10**11, 10**7),
    )(x_patches, attn_patches, out_grad[0], attn_frames, *small)
    frame_spec = pl.BlockSpec((1, patches, width), lambda f: (f, 0, 0))
    log_spec = pl.BlockSpec((1, pairs, 2, patches), lambda f: (f, 0, 0, 0))
    clips = lax.axis_size("clip")
    span_rows = width // clips
    unit = 16 * (-(-span_rows // (16 * count)))
    dx_patches, grad_sp, lines_of = pl.pallas_call(
        partial(spatial_backward, rows=512, part=512, count=count, clips=clips),
        grid=(mine,),
        in_specs=[frame_spec] * 5
        + [log_spec, frame_spec, whole_spec((ROWS, width)), whole_spec((width, 3 * width))]
        + [whole_spec(a.shape) for a in (sums, t_sums, in_sums)],
        out_specs=[any_spec(), acc_spec((width, 3 * width)), acc_spec((clips, ROWS, width))],
        out_shape=[
            patch_shape,
            jax.ShapeDtypeStruct((width, 3 * width), MXB),
            jax.ShapeDtypeStruct((clips, ROWS, width), F32),
        ],
        scratch_shapes=[
            pltpu.VMEM((width, 3 * width), F32),
            pltpu.VMEM((mine, patches, width), MXB),
            pltpu.VMEM((patches, 3 * width), MXB),
            pltpu.VMEM((pairs, 2, patches), F32),
            pltpu.VMEM((pairs, 2 * HEAD_DIM, patches), F32),
            pltpu.VMEM((patches, width), F32),
            pltpu.VMEM((patches, width), F32),
            pltpu.VMEM((pairs, 2 * HEAD_DIM, patches), MXB),
            pltpu.VMEM((2, 8, width), F32),
            pltpu.VMEM((8, 3 * width), F32),
            pltpu.VMEM((clips, span_rows, 3 * width), MXB),
            pltpu.VMEM((clips, span_rows, 3 * width), MXB),
            pltpu.VMEM((count, unit, 3 * width), MXB),
            pltpu.VMEM((count, unit, 3 * width), MXB),
            pltpu.VMEM((span_rows, 3 * width), MXB),
            pltpu.VMEM((clips, span_rows, 3 * width), MXB),
            pltpu.VMEM((ROWS, width), F32),
            pltpu.VMEM((count, ROWS, width), F32),
            pltpu.VMEM((ROWS, width), F32),
            pltpu.VMEM((clips, ROWS, width), F32),
            dma((mine, count)),
            dma((mine, count)),
            dma((mine,)),
        ]
        + [dma((clips,))] * 2
        + [dma((count,))] * 4
        + [dma((clips,))] * 2
        + [dma((count,))] * 2
        + [dma((clips,))] * 2,
        compiler_params=params(2),
        cost_estimate=cost(2 * 10**11, 10**7),
    )(da_frames, attn_frames, queries, keys, values, logs, x_frames, modes, spatial_proj, sums, t_sums, in_sums)
    input_grad = (g1 + dx_patches.astype(F32)).astype(MXB)
    early = lax.psum((grad_so, grad_t, grad_to, grad_in, grad_out_turned), ("clip", "sp"))
    early = tuple(g.astype(F32) for g in early)
    flat = jnp.sum(lines_of, axis=0).reshape(-1)
    conds = lines_of[:, COND]
    grads = lines_of[:, :9].reshape(clips, 9 * width)
    grad_ada = sum(conds[at][:, None] * grads[at][None, :] for at in range(clips))

    def lines(first, rows=1):
        return flat[first * width : (first + rows) * width]

    return (
        block_out[None],
        input_grad[None],
        grad_ada,
        lines(0, 9),
        grad_sp.astype(F32),
        jnp.concatenate([lines(SP_BIAS), lines(SP_BIAS + 2)]),
        early[0],
        lines(SO_BIAS),
        early[1],
        jnp.concatenate([lines(T_BIAS), lines(T_BIAS + 2)]),
        early[2],
        lines(TO_BIAS),
        early[3],
        lines(IN_BIAS, hidden // width),
        early[4].T,
        lines(OUT_BIAS),
    )


def chosen(tokens, *others):
    _, frames, stripe, _ = tokens.shape
    if tokens.shape[0] == 1 and frames % lax.axis_size("sp") == 0 and stripe % TILE == 0:
        return fast_body(tokens, *others)
    return body(tokens, *others)


def solution(mesh):
    return jax.shard_map(
        chosen,
        mesh=mesh,
        in_specs=(
            P("clip", None, "sp", None),
            P("clip", None),
            P("clip"),
            P("clip", None, "sp", None),
            P(),
            P(),
            P(),
            P(),
            P(),
            P(),
            P(),
            P(),
            P(),
            P(),
            P(),
            P(),
            P(),
            P(),
        ),
        out_specs=(
            P("clip", None, "sp", None),
            P("clip", None, "sp", None),
            P(),
            P(),
            P(),
            P(),
            P(),
            P(),
            P(),
            P(),
            P(),
            P(),
            P(),
            P(),
            P(),
            P(),
        ),
        check_vma=False,
    )
```

```python
from functools import partial, reduce
import math

import jax
import jax.numpy as jnp
from jax import lax
from jax.experimental import pallas as pl
from jax.experimental.pallas import tpu as pltpu
from jax.sharding import PartitionSpec as P

HEADS = 6
HEAD_DIM = 64
FRAME_BLOCK = 8
TSTEPS = 1000
GELU_RATE = math.sqrt(2.0 / math.pi)
SP_BIAS = 9
T_BIAS = 12
SO_BIAS = 15
TO_BIAS = 16
OUT_BIAS = 17
IN_BIAS = 18
WEIGHT = 22
COND = 23
ROWS = 24


def modulate(field, shift, scale):
    centred = field - jnp.mean(field, axis=-1, keepdims=True)
    normed = centred * lax.rsqrt(jnp.mean(centred * centred, axis=-1, keepdims=True) + 1e-06)
    return normed * (1.0 + scale) + shift


def loss_weights(timesteps):
    phase = (timesteps.astype(jnp.float32) / TSTEPS + 0.008) / 1.008 * (0.5 * math.pi)
    slope = jnp.tan(phase)
    return jnp.minimum(1.0, 5.0 * slope * slope)


def split_heads(array):
    return array.reshape(array.shape[:-1] + (HEADS, HEAD_DIM))


def join_heads(array):
    return array.reshape(array.shape[:-2] + (HEADS * HEAD_DIM,))


def attend(queries, keys, values):
    scores = jnp.einsum(
        "csqhe,cskhe->cshqk", queries, keys, preferred_element_type=jnp.float32
    ) * HEAD_DIM ** (-0.5)
    row_max = jnp.max(scores, axis=-1, keepdims=True)
    exponent = jnp.exp(scores - row_max)
    total = jnp.sum(exponent, axis=-1, keepdims=True)
    soft_weights = (exponent / total).astype(jnp.bfloat16)
    mixed = jnp.einsum(
        "cshqk,cskhe->csqhe", soft_weights, values, preferred_element_type=jnp.float32
    )
    return (mixed, row_max[..., 0] + jnp.log(total[..., 0]))


def probabilities(queries, keys, values, grads, log_total):
    scores = jnp.einsum(
        "csqhe,cskhe->cshqk", queries, keys, preferred_element_type=jnp.float32
    ) * HEAD_DIM ** (-0.5)
    soft_weights = jnp.exp(scores - log_total[..., None])
    grad_weights = jnp.einsum(
        "csqhe,cskhe->cshqk", grads, values, preferred_element_type=jnp.float32
    )
    return (soft_weights, grad_weights)


def query_pass(queries, keys, values, grads, log_total):
    soft_weights, grad_weights = probabilities(queries, keys, values, grads, log_total)
    delta = jnp.sum(soft_weights * grad_weights, axis=-1)
    grad_scores = (soft_weights * (grad_weights - delta[..., None]) * HEAD_DIM ** (-0.5)).astype(
        jnp.bfloat16
    )
    grad_queries = jnp.einsum(
        "cshqk,cskhe->csqhe", grad_scores, keys, preferred_element_type=jnp.float32
    )
    return (grad_queries, delta)


def key_pass(queries, keys, values, grads, log_total, delta):
    soft_weights, grad_weights = probabilities(queries, keys, values, grads, log_total)
    grad_scores = (soft_weights * (grad_weights - delta[..., None]) * HEAD_DIM ** (-0.5)).astype(
        jnp.bfloat16
    )
    grad_keys = jnp.einsum(
        "cshqk,csqhe->cskhe", grad_scores, queries, preferred_element_type=jnp.float32
    )
    grad_values = jnp.einsum(
        "cshqk,csqhe->cskhe",
        soft_weights.astype(jnp.bfloat16),
        grads,
        preferred_element_type=jnp.float32,
    )
    return jnp.concatenate([join_heads(grad_keys), join_heads(grad_values)], axis=-1)


def column_sums(array):
    return jnp.sum(array.astype(jnp.float32), axis=(0, 1, 2))


def body(
    tokens,
    conditioning,
    timesteps,
    out_grad,
    ada_weight,
    ada_bias,
    spatial_proj,
    spatial_bias,
    spatial_out,
    spatial_out_bias,
    temporal_proj,
    temporal_bias,
    temporal_out,
    temporal_out_bias,
    hidden_in,
    hidden_in_bias,
    hidden_out,
    hidden_out_bias,
):
    clips, frames, stripe, width = tokens.shape
    blocks = frames // FRAME_BLOCK
    scale_factor = HEAD_DIM ** (-0.5)
    field = tokens.astype(jnp.float32)
    cond_act = jax.nn.silu(conditioning.astype(jnp.float32)).astype(jnp.bfloat16)
    modes = jnp.dot(cond_act, ada_weight, preferred_element_type=jnp.float32) + ada_bias
    modes = modes.reshape(clips, 9, 1, 1, width)
    hidden_one, back_one = jax.vjp(modulate, field, modes[:, 0], modes[:, 1])
    hidden_one = hidden_one.astype(jnp.bfloat16)
    query_mix = jnp.einsum(
        "cfpd,de->cfpe", hidden_one, spatial_proj[:, :width], preferred_element_type=jnp.float32
    )
    queries = (query_mix + spatial_bias[:width]).astype(jnp.bfloat16)
    keyval_mix = jnp.einsum(
        "cfpd,de->cfpe", hidden_one, spatial_proj[:, width:], preferred_element_type=jnp.float32
    )
    keyval_bias = jnp.concatenate([jnp.zeros((width,), jnp.float32), spatial_bias[width:]])
    keyvals = (keyval_mix + keyval_bias).astype(jnp.bfloat16)
    query_heads = split_heads(queries)
    mixed_parts = []
    log_parts = []
    for index in range(blocks):
        first = index * FRAME_BLOCK
        whole = lax.all_gather(keyvals[:, first : first + FRAME_BLOCK], "sp", axis=2, tiled=True)
        mixed_part, log_part = attend(
            query_heads[:, first : first + FRAME_BLOCK],
            split_heads(whole[..., :width]),
            split_heads(whole[..., width:]),
        )
        mixed_parts.append(join_heads(mixed_part))
        log_parts.append(log_part)
    attn_one = jnp.concatenate(mixed_parts, axis=1).astype(jnp.bfloat16)
    spatial_log = jnp.concatenate(log_parts, axis=1)
    branch_one = (
        jnp.einsum("cfpd,de->cfpe", attn_one, spatial_out, preferred_element_type=jnp.float32)
        + spatial_out_bias
    )
    field_one = field + modes[:, 2] * branch_one
    hidden_two, back_two = jax.vjp(modulate, field_one, modes[:, 3], modes[:, 4])
    hidden_two = hidden_two.astype(jnp.bfloat16)
    time_mix = jnp.einsum(
        "cfpd,de->cfpe", hidden_two, temporal_proj, preferred_element_type=jnp.float32
    )
    time_queries = split_heads((time_mix[..., :width] + temporal_bias[:width]).astype(jnp.bfloat16))
    time_keys = split_heads(time_mix[..., width : 2 * width].astype(jnp.bfloat16))
    time_values = split_heads(
        (time_mix[..., 2 * width :] + temporal_bias[width:]).astype(jnp.bfloat16)
    )
    time_scores = (
        jnp.einsum(
            "cfphe,cgphe->cphfg", time_queries, time_keys, preferred_element_type=jnp.float32
        )
        * scale_factor
    )
    time_max = jnp.max(time_scores, axis=-1, keepdims=True)
    time_exponent = jnp.exp(time_scores - time_max)
    time_weights = time_exponent / jnp.sum(time_exponent, axis=-1, keepdims=True)
    time_rounded = time_weights.astype(jnp.bfloat16)
    attn_two = join_heads(
        jnp.einsum(
            "cphfg,cgphe->cfphe", time_rounded, time_values, preferred_element_type=jnp.float32
        )
    ).astype(jnp.bfloat16)
    branch_two = (
        jnp.einsum("cfpd,de->cfpe", attn_two, temporal_out, preferred_element_type=jnp.float32)
        + temporal_out_bias
    )
    field_two = field_one + modes[:, 5] * branch_two
    hidden_three, back_three = jax.vjp(modulate, field_two, modes[:, 6], modes[:, 7])
    hidden_three = hidden_three.astype(jnp.bfloat16)
    inner = (
        jnp.einsum("cfpd,dk->cfpk", hidden_three, hidden_in, preferred_element_type=jnp.float32)
        + hidden_in_bias
    )
    active, gelu_back = jax.vjp(partial(jax.nn.gelu, approximate=True), inner)
    active = active.astype(jnp.bfloat16)
    branch_three = (
        jnp.einsum("cfpk,kd->cfpd", active, hidden_out, preferred_element_type=jnp.float32)
        + hidden_out_bias
    )
    block_out = (field_two + modes[:, 8] * branch_three).astype(jnp.bfloat16)
    weights = loss_weights(timesteps)
    grad_field = out_grad.astype(jnp.float32) * weights[:, None, None, None]
    grad_gate_three = jnp.sum(grad_field * branch_three, axis=(1, 2))
    grad_branch = (modes[:, 8] * grad_field).astype(jnp.bfloat16)
    grad_hidden_out = jnp.einsum(
        "cfpk,cfpd->kd", active, grad_branch, preferred_element_type=jnp.float32
    )
    grad_hidden_out_bias = column_sums(grad_branch)
    grad_active = jnp.einsum(
        "cfpd,kd->cfpk", grad_branch, hidden_out, preferred_element_type=jnp.float32
    )
    grad_inner = gelu_back(grad_active)[0].astype(jnp.bfloat16)
    grad_hidden_in = jnp.einsum(
        "cfpd,cfpk->dk", hidden_three, grad_inner, preferred_element_type=jnp.float32
    )
    grad_hidden_in_bias = column_sums(grad_inner)
    grad_hidden = jnp.einsum(
        "cfpk,dk->cfpd", grad_inner, hidden_in, preferred_element_type=jnp.float32
    )
    grad_input, grad_shift_three, grad_scale_three = back_three(grad_hidden)
    grad_field = grad_field + grad_input
    grad_gate_two = jnp.sum(grad_field * branch_two, axis=(1, 2))
    grad_branch = (modes[:, 5] * grad_field).astype(jnp.bfloat16)
    grad_temporal_out = jnp.einsum(
        "cfpd,cfpe->de", attn_two, grad_branch, preferred_element_type=jnp.float32
    )
    grad_temporal_out_bias = column_sums(grad_branch)
    grad_attn = split_heads(
        jnp.einsum(
            "cfpe,de->cfpd", grad_branch, temporal_out, preferred_element_type=jnp.float32
        ).astype(jnp.bfloat16)
    )
    grad_weights = jnp.einsum(
        "cfphe,cgphe->cphfg", grad_attn, time_values, preferred_element_type=jnp.float32
    )
    delta = jnp.sum(time_weights * grad_weights, axis=-1, keepdims=True)
    grad_scores = (time_weights * (grad_weights - delta) * scale_factor).astype(jnp.bfloat16)
    grad_time_queries = jnp.einsum(
        "cphfg,cgphe->cfphe", grad_scores, time_keys, preferred_element_type=jnp.float32
    )
    grad_time_keys = jnp.einsum(
        "cphfg,cfphe->cgphe", grad_scores, time_queries, preferred_element_type=jnp.float32
    )
    grad_time_values = jnp.einsum(
        "cphfg,cfphe->cgphe", time_rounded, grad_attn, preferred_element_type=jnp.float32
    )
    grad_time_mix = jnp.concatenate(
        [join_heads(grad_time_queries), join_heads(grad_time_keys), join_heads(grad_time_values)],
        axis=-1,
    ).astype(jnp.bfloat16)
    grad_temporal_proj = jnp.einsum(
        "cfpd,cfpe->de", hidden_two, grad_time_mix, preferred_element_type=jnp.float32
    )
    grad_temporal_bias = jnp.concatenate(
        [column_sums(grad_time_mix[..., :width]), column_sums(grad_time_mix[..., 2 * width :])]
    )
    grad_hidden = jnp.einsum(
        "cfpe,de->cfpd", grad_time_mix, temporal_proj, preferred_element_type=jnp.float32
    )
    grad_input, grad_shift_two, grad_scale_two = back_two(grad_hidden)
    grad_field = grad_field + grad_input
    grad_gate_one = jnp.sum(grad_field * branch_one, axis=(1, 2))
    grad_branch = (modes[:, 2] * grad_field).astype(jnp.bfloat16)
    grad_spatial_out = jnp.einsum(
        "cfpd,cfpe->de", attn_one, grad_branch, preferred_element_type=jnp.float32
    )
    grad_spatial_out_bias = column_sums(grad_branch)
    grad_attn = jnp.einsum(
        "cfpe,de->cfpd", grad_branch, spatial_out, preferred_element_type=jnp.float32
    ).astype(jnp.bfloat16)
    query_parts = []
    key_parts = []
    for index in range(blocks):
        first = index * FRAME_BLOCK
        whole = lax.all_gather(keyvals[:, first : first + FRAME_BLOCK], "sp", axis=2, tiled=True)
        piece = query_heads[:, first : first + FRAME_BLOCK]
        grad_piece = split_heads(grad_attn[:, first : first + FRAME_BLOCK])
        log_piece = spatial_log[:, first : first + FRAME_BLOCK]
        grad_query_part, delta = query_pass(
            piece,
            split_heads(whole[..., :width]),
            split_heads(whole[..., width:]),
            grad_piece,
            log_piece,
        )
        term = key_pass(
            piece,
            split_heads(whole[..., :width]),
            split_heads(whole[..., width:]),
            grad_piece,
            log_piece,
            delta,
        )
        owned = lax.psum_scatter(
            jnp.transpose(term, (2, 0, 1, 3)).astype(jnp.bfloat16),
            "sp",
            scatter_dimension=0,
            tiled=True,
        ).astype(jnp.float32)
        query_parts.append(join_heads(grad_query_part))
        key_parts.append(jnp.transpose(owned, (1, 2, 0, 3)))
    grad_queries = jnp.concatenate(query_parts, axis=1)
    grad_keyvals = jnp.concatenate(key_parts, axis=1)
    grad_queries = grad_queries.astype(jnp.bfloat16)
    grad_keyvals = grad_keyvals.astype(jnp.bfloat16)
    grad_spatial_proj = jnp.concatenate(
        [
            jnp.einsum(
                "cfpd,cfpe->de", hidden_one, grad_queries, preferred_element_type=jnp.float32
            ),
            jnp.einsum(
                "cfpd,cfpe->de", hidden_one, grad_keyvals, preferred_element_type=jnp.float32
            ),
        ],
        axis=1,
    )
    grad_spatial_bias = jnp.concatenate(
        [column_sums(grad_queries), column_sums(grad_keyvals[..., width:])]
    )
    grad_hidden = jnp.einsum(
        "cfpe,de->cfpd", grad_queries, spatial_proj[:, :width], preferred_element_type=jnp.float32
    )
    grad_hidden = grad_hidden + jnp.einsum(
        "cfpe,de->cfpd", grad_keyvals, spatial_proj[:, width:], preferred_element_type=jnp.float32
    )
    grad_input, grad_shift_one, grad_scale_one = back_one(grad_hidden)
    input_grad = (grad_field + grad_input).astype(jnp.bfloat16)
    grad_modes = jnp.stack(
        [
            grad_shift_one.reshape(clips, width),
            grad_scale_one.reshape(clips, width),
            grad_gate_one,
            grad_shift_two.reshape(clips, width),
            grad_scale_two.reshape(clips, width),
            grad_gate_two,
            grad_shift_three.reshape(clips, width),
            grad_scale_three.reshape(clips, width),
            grad_gate_three,
        ],
        axis=1,
    ).reshape(clips, 9 * width)
    grad_ada_weight = jnp.dot(
        cond_act.astype(jnp.float32).T, grad_modes, precision=lax.Precision.HIGHEST
    )
    grad_ada_bias = jnp.sum(grad_modes, axis=0)
    summed = lax.psum(
        (
            grad_ada_weight,
            grad_ada_bias,
            grad_spatial_proj,
            grad_spatial_bias,
            grad_spatial_out,
            grad_spatial_out_bias,
            grad_temporal_proj,
            grad_temporal_bias,
            grad_temporal_out,
            grad_temporal_out_bias,
            grad_hidden_in,
            grad_hidden_in_bias,
            grad_hidden_out,
            grad_hidden_out_bias,
        ),
        ("clip", "sp"),
    )
    return (
        block_out,
        input_grad,
        summed[0],
        summed[1],
        summed[2],
        summed[3],
        summed[4],
        summed[5],
        summed[6],
        summed[7],
        summed[8],
        summed[9],
        summed[10],
        summed[11],
        summed[12],
        summed[13],
    )


MXB = jnp.bfloat16
F32 = jnp.float32
TILE = 32
GROUP = 8
VMEM_BYTES = 60 * 2**20


def dot(left, right):
    return jnp.dot(left, right, preferred_element_type=F32)


def dot_nt(left, right):
    return lax.dot_general(left, right, (((1,), (1,)), ((), ())), preferred_element_type=F32)


def dot_tn(left, right):
    return lax.dot_general(left, right, (((0,), (0,)), ((), ())), preferred_element_type=F32)


def turned(array):
    return array.astype(F32).T.astype(array.dtype)


def normalise(field):
    centred = field - jnp.mean(field, axis=-1, keepdims=True)
    rate = lax.rsqrt(jnp.mean(centred * centred, axis=-1, keepdims=True) + 1e-06)
    return centred * rate, rate


def normalise_back(grad, normed, rate, scale):
    inner = grad * (1.0 + scale)
    mean = jnp.mean(inner, axis=-1, keepdims=True)
    slope = jnp.mean(inner * normed, axis=-1, keepdims=True)
    return rate * (inner - mean - normed * slope)


def eight_rows(array):
    return jnp.sum(array.reshape(array.shape[0] // 8, 8, array.shape[1]), axis=0)


def wide(ref, first, rows):
    return jnp.concatenate([ref[first + row : first + row + 1, :] for row in range(rows)], axis=1)


def low_lanes():
    return lax.broadcasted_iota(jnp.int32, (1, 2 * HEAD_DIM), 1) < HEAD_DIM


def halves(pair):
    low = low_lanes()
    zero = jnp.zeros_like(pair)
    return jnp.where(low, pair, zero), jnp.where(low, zero, pair)


def others(count, axis="sp"):
    me = lax.axis_index(axis)
    return me, [(step, lax.rem(me + step, count), lax.rem(me + count - step, count)) for step in range(1, count)]


def send(source, target, send_sem, recv_sem, peer, axis="sp"):
    return pltpu.make_async_remote_copy(
        src_ref=source, dst_ref=target, send_sem=send_sem, recv_sem=recv_sem,
        device_id={axis: peer}, device_id_type=pl.DeviceIdType.MESH,
    )


def greet(peers, axis="sp"):
    barrier = pltpu.get_barrier_semaphore()
    for _, peer, _ in peers:
        pl.semaphore_signal(barrier, inc=1, device_id={axis: peer}, device_id_type=pl.DeviceIdType.MESH)


def greeted(peers):
    pl.semaphore_wait(pltpu.get_barrier_semaphore(), len(peers))


def spatial_forward(
    tokens_ref, modes_ref, proj_ref,
    x_out, q_out, k_out, v_out, attn_out, patches_out, log_ref,
    x_ref, q_ref, k_ref, v_ref, attn_ref, turned_ref, mixed_ref, top_ref,
    x_send, x_recv, x_own, a_send, a_recv, a_own, save_sem,
    block, part, count,
):
    mine, tokens, width = x_ref.shape
    stripe = tokens // count
    pairs = width // (2 * HEAD_DIM)
    near = block // stripe
    soon = patches_out.shape[1]
    me, peers = others(count)
    shift = modes_ref[0:1, :]
    scale = modes_ref[1:2, :]
    bias = wide(modes_ref, SP_BIAS, 3)

    def x_copy(frame, peer):
        return send(
            tokens_ref.at[peer * mine + frame],
            x_ref.at[frame, pl.ds(pl.multiple_of(me * stripe, stripe), stripe), :],
            x_send.at[frame, peer], x_recv.at[frame, me], peer,
        )

    def x_landed(frame, source):
        rows = x_ref.at[frame, pl.ds(pl.multiple_of(source * stripe, stripe), stripe), :]
        return send(rows, rows, x_send.at[frame, source], x_recv.at[frame, source], source)

    def x_keep(frame):
        return pltpu.make_async_copy(
            tokens_ref.at[me * mine + frame],
            x_ref.at[frame, pl.ds(pl.multiple_of(me * stripe, stripe), stripe), :],
            x_own.at[frame],
        )

    def saves(frame):
        return [
            pltpu.make_async_copy(held.at[frame], kept.at[frame], save_sem.at[place, frame])
            for place, (held, kept) in enumerate(
                ((x_ref, x_out), (q_ref, q_out), (k_ref, k_out), (v_ref, v_out), (attn_ref, attn_out))
            )
        ]

    def a_copy(frame, pair, peer):
        lanes = pl.ds(pl.multiple_of(pair * 2 * HEAD_DIM, 2 * HEAD_DIM), 2 * HEAD_DIM)
        return send(
            attn_ref.at[frame, pl.ds(pl.multiple_of(peer * stripe, stripe), soon), lanes],
            patches_out.at[me * mine + frame, :, lanes],
            a_send.at[frame, pair, peer], a_recv.at[frame, pair, me], peer,
        )

    def a_landed(frame, pair, peer):
        lanes = pl.ds(pl.multiple_of(pair * 2 * HEAD_DIM, 2 * HEAD_DIM), 2 * HEAD_DIM)
        return send(
            attn_ref.at[frame, pl.ds(pl.multiple_of(peer * stripe, stripe), soon), lanes],
            patches_out.at[peer * mine + frame, :, lanes],
            a_send.at[frame, pair, peer], a_recv.at[frame, pair, peer], peer,
        )

    def a_keep(frame, pair):
        lanes = pl.ds(pl.multiple_of(pair * 2 * HEAD_DIM, 2 * HEAD_DIM), 2 * HEAD_DIM)
        return pltpu.make_async_copy(
            attn_ref.at[frame, pl.ds(pl.multiple_of(me * stripe, stripe), soon), lanes],
            patches_out.at[me * mine + frame, :, lanes],
            a_own.at[frame, pair],
        )

    near_source = lax.div(me, near) * near
    far_source = near - near_source

    def x_sends(frame, first, stop, far):
        for place in range(first, stop):
            peer = (far_source if far else near_source) + lax.rem(me + place, near)
            x_copy(frame, peer).start()

    greet(peers)
    greeted(peers)
    for frame in range(mine):
        x_keep(frame).start()
    x_sends(0, 1, near, False)
    x_sends(0, 0, near // 2, True)
    for frame in range(1, mine):
        x_sends(frame, 1, near, False)
    x_sends(0, near // 2, near, True)
    for frame in range(1, mine):
        x_sends(frame, 0, near, True)
    turned_ref[:, :, HEAD_DIM:, :] = jnp.ones(
        (mine, 2 * pairs, turned_ref.shape[2] - HEAD_DIM, tokens), MXB
    )
    mixed_ref[...] = jnp.zeros_like(mixed_ref)
    top_ref[...] = jnp.full_like(top_ref, -1e30)

    def stage(index, carry):
        pair = lax.rem(index, pairs)
        group = lax.div(index, pairs)
        early = group < mine
        place = lax.rem(jnp.maximum(group - mine, 0), 3)
        frame = jnp.where(early, group, lax.div(jnp.maximum(group - mine, 0), 3))

        @pl.when((pair == 0) & (early | (place == 0)))
        def _():
            first_source = jnp.where(early, near_source, far_source)

            def project(index, carry):
                source = first_source + index
                at = pl.ds(pl.multiple_of(source * stripe, stripe), stripe)

                @pl.when(source == me)
                def _():
                    x_keep(frame).wait()

                @pl.when(source != me)
                def _():
                    x_landed(frame, source).wait_recv()

                normed, _ = normalise(x_ref[frame, at, :].astype(F32))
                hidden = (normed * (1.0 + scale) + shift).astype(MXB)
                mixed = dot(hidden, proj_ref[...]) + bias
                q_ref[frame, at, :] = mixed[:, :width].astype(MXB)
                k_ref[frame, at, :] = mixed[:, width : 2 * width].astype(MXB)
                value = mixed[:, 2 * width :].astype(MXB)
                v_ref[frame, at, :] = value
                across = turned(value)
                for head in range(2 * pairs):
                    turned_ref[frame, head, :HEAD_DIM, at] = across[head * HEAD_DIM : (head + 1) * HEAD_DIM]
                return carry

            lax.fori_loop(0, near, project, 0)

            @pl.when(group >= mine)
            def _():
                for copy in saves(frame)[:4]:
                    copy.start()

        query_source = jnp.where(early | (place == 2), near_source, far_source)
        key_source = jnp.where(early | (place == 0), near_source, far_source)
        at = pl.ds(pl.multiple_of(query_source * stripe, block), block)
        lanes = pl.ds(pl.multiple_of(pair * 2 * HEAD_DIM, 2 * HEAD_DIM), 2 * HEAD_DIM)
        spans = [pl.ds(pl.multiple_of(key_source * stripe + first, part), part) for first in range(0, block, part)]
        scores = []
        tops = []
        decays = []
        for side, query in enumerate(halves(q_ref[frame, at, lanes] * MXB(HEAD_DIM**-0.5))):
            each = [dot_nt(k_ref[frame, span, lanes], query) for span in spans]
            top = [jnp.max(s.reshape(part // 8, 8, block), axis=0) for s in each]
            before = top_ref[frame, pair, side : side + 1, at]
            now = jnp.maximum(before, jnp.max(reduce(jnp.maximum, top), axis=0, keepdims=True))
            top_ref[frame, pair, side : side + 1, at] = now
            scores.append(each)
            tops.append(now)
            decays.append(jnp.exp(before - now))
        for side in range(2):
            total = mixed_ref[frame, 2 * pair + side, :, at] * decays[side]
            for span, s in zip(spans, scores[side]):
                weights = jnp.exp(s - tops[side]).astype(MXB)
                total = total + dot(turned_ref[frame, 2 * pair + side, :, span], weights)
            mixed_ref[frame, 2 * pair + side, :, at] = total

        @pl.when((group >= mine) & (place >= 1))
        def _():
            mixed = []
            for side in range(2):
                total = mixed_ref[frame, 2 * pair + side, :, at]
                mass = total[HEAD_DIM : HEAD_DIM + 1]
                log_ref[frame, pair, side : side + 1, at] = tops[side] + jnp.log(mass)
                mixed.append(total[:HEAD_DIM] / mass)
            attn_ref[frame, at, lanes] = jnp.concatenate(mixed, axis=0).T.astype(MXB)
            for other in range(near):
                peer = query_source + other

                @pl.when(peer != me)
                def _():
                    a_copy(frame, pair, peer).start()

                @pl.when(peer == me)
                def _():
                    a_keep(frame, pair).start()

        @pl.when((group >= mine) & (place == 2) & (pair == pairs - 1))
        def _():
            saves(frame)[4].start()

        return carry

    lax.fori_loop(0, 4 * mine * pairs, stage, 0)

    for frame in range(mine):
        for copy in saves(frame):
            copy.wait()
        for _, peer, _ in peers:
            x_copy(frame, peer).wait_send()
        for pair in range(pairs):
            a_keep(frame, pair).wait()
            for _, peer, _ in peers:
                a_copy(frame, pair, peer).wait_send()
                a_landed(frame, pair, peer).wait_recv()


def spatial_backward(
    da_ref, attn_ref, q_ref, k_ref, v_ref, log_ref, x_ref, modes_ref, proj_ref, mid_sums_ref, t_sums_ref, in_sums_ref,
    stack_hbm, patches_out, stack_out, proj_out, row_out,
    grad_proj_ref, dx_ref, mix_ref, delta_ref, dq_ref, dk_ref, dv_ref, across_ref, sums_ref, bias_sums_ref,
    clip_out_ref, clip_in_ref, unit_out_ref, unit_in_ref, piece_ref, all_ref, vec_ref, vec_in_ref, row_ref, row_in_ref,
    early_in_ref, early_out_ref, early_unit_ref, early_piece_ref,
    send_sem, recv_sem, own_sem, g1_send, g1_recv, g2_send, g2_recv, g3_send, g3_recv, g4_send, g4_recv,
    v1_send, v1_recv, v2_send, v2_recv, e1_send, e1_recv, e2_send, e2_recv, e3_send, e3_recv, e4_send, e4_recv, e_own,
    rows, part, count, clips,
):
    tokens, width = x_ref.shape[1:]
    mine = dx_ref.shape[0]
    stripe = tokens // count
    frame = pl.program_id(0)
    me, peers = others(count)
    clip, clip_peers = others(clips, "clip")
    span_rows = width // clips
    unit = 16 * (-(-span_rows // (16 * count)))
    owners = span_rows // unit

    def g1_copy(peer, slot):
        return send(
            clip_out_ref.at[peer], clip_in_ref.at[slot], g1_send.at[peer], g1_recv.at[slot], peer, "clip"
        )

    def g2_copy(peer, slot):
        return send(unit_out_ref.at[peer], unit_in_ref.at[slot], g2_send.at[peer], g2_recv.at[slot], peer)

    def g3_copy(peer, slot):
        part_rows = pl.ds(pl.multiple_of(slot * unit, unit), unit)
        return send(piece_ref.at[part_rows, :], piece_ref.at[part_rows, :], g3_send.at[peer], g3_recv.at[slot], peer)

    def g4_copy(peer, slot):
        return send(piece_ref, all_ref.at[slot], g4_send.at[peer], g4_recv.at[slot], peer, "clip")

    def clip_rows(each):
        return pl.ds(pl.multiple_of(each * span_rows, span_rows), span_rows)

    def unit_rows(each):
        return pl.ds(pl.multiple_of(each * unit, unit), unit)

    def e1_copy(peer, slot):
        return send(
            stack_hbm.at[:, clip_rows(peer), :], early_in_ref.at[slot], e1_send.at[peer], e1_recv.at[slot], peer, "clip"
        )

    def e1_keep():
        return pltpu.make_async_copy(stack_hbm.at[:, clip_rows(clip), :], early_in_ref.at[clip], e_own.at[0])

    def e2_copy(peer, slot):
        return send(early_out_ref.at[peer], early_unit_ref.at[slot], e2_send.at[peer], e2_recv.at[slot], peer)

    def e3_copy(peer, slot):
        here = early_piece_ref.at[:, unit_rows(slot), :]
        return send(here, here, e3_send.at[peer], e3_recv.at[slot], peer)

    def e4_copy(peer, slot):
        return send(
            early_piece_ref, stack_out.at[:, clip_rows(slot), :], e4_send.at[peer], e4_recv.at[slot], peer, "clip"
        )

    def e4_keep():
        return pltpu.make_async_copy(early_piece_ref, stack_out.at[:, clip_rows(clip), :], e_own.at[1])

    def early_one():
        e1_keep().start()
        for _, peer, _ in clip_peers:
            e1_copy(peer, clip).start()

    def early_two():
        e1_keep().wait()
        for _, _, source in clip_peers:
            e1_copy(source, source).wait_recv()

        def add_up(owner, carry):
            total = early_in_ref[0, :, unit_rows(owner), :].astype(F32)
            for each in range(1, clips):
                total = total + early_in_ref[each, :, unit_rows(owner), :].astype(F32)
            early_out_ref[owner] = total.astype(MXB)

            @pl.when(owner != me)
            def _():
                e2_copy(owner, me).start()

            return carry

        lax.fori_loop(0, owners, add_up, 0)

    def early_three():
        @pl.when(me < owners)
        def _():
            total = early_out_ref[me].astype(F32)
            for _, _, source in peers:
                e2_copy(me, source).wait_recv()
                total = total + early_unit_ref[source].astype(F32)
            early_piece_ref[:, unit_rows(me), :] = total.astype(MXB)
            for _, peer, _ in peers:
                e3_copy(peer, me).start()

    def early_four():
        for owner in range(owners):

            @pl.when(owner != me)
            def _():
                e3_copy(owner, owner).wait_recv()

        e4_keep().start()
        for _, peer, _ in clip_peers:
            e4_copy(peer, clip).start()

    def early_end():
        e4_keep().wait()
        for _, peer, source in clip_peers:
            e4_copy(source, source).wait_recv()
            e1_copy(peer, clip).wait_send()
            e4_copy(peer, clip).wait_send()
        for owner in range(owners):

            @pl.when(owner != me)
            def _():
                e2_copy(owner, me).wait_send()

        @pl.when(me < owners)
        def _():
            for _, peer, _ in peers:
                e3_copy(peer, me).wait_send()

    def v1_copy(peer, slot):
        return send(vec_ref, vec_in_ref.at[slot], v1_send.at[peer], v1_recv.at[slot], peer)

    def v2_copy(peer, slot):
        return send(row_ref, row_in_ref.at[slot], v2_send.at[peer], v2_recv.at[slot], peer, "clip")

    def dx_copy(frame, peer):
        return send(
            dx_ref.at[frame, pl.ds(pl.multiple_of(peer * stripe, stripe), stripe), :],
            patches_out.at[me * mine + frame], send_sem.at[frame, peer], recv_sem.at[frame, me], peer,
        )

    def dx_landed(frame, peer):
        return send(
            dx_ref.at[frame, pl.ds(pl.multiple_of(peer * stripe, stripe), stripe), :],
            patches_out.at[peer * mine + frame], send_sem.at[frame, peer], recv_sem.at[frame, peer], peer,
        )

    def dx_keep(frame):
        return pltpu.make_async_copy(
            dx_ref.at[frame, pl.ds(pl.multiple_of(me * stripe, stripe), stripe), :],
            patches_out.at[me * mine + frame], own_sem.at[frame],
        )

    @pl.when(frame == 0)
    def _():
        greet(peers)
        greet(clip_peers, "clip")

    pairs = width // (2 * HEAD_DIM)
    scale_factor = HEAD_DIM**-0.5

    @pl.when(frame == 0)
    def _():
        grad_proj_ref[...] = jnp.zeros_like(grad_proj_ref)
        sums_ref[...] = jnp.zeros_like(sums_ref)
        bias_sums_ref[...] = jnp.zeros_like(bias_sums_ref)

    head_of = lax.broadcasted_iota(jnp.int32, (8, width), 1) // HEAD_DIM
    picks = jnp.where(head_of == lax.broadcasted_iota(jnp.int32, (8, width), 0), 1.0, 0.0).astype(MXB)

    def deltas(index, carry):
        at = pl.ds(pl.multiple_of(index * rows, rows), rows)
        product = da_ref[0, at, :].astype(F32) * attn_ref[0, at, :].astype(F32)
        high = product.astype(MXB)
        rest = (product - high.astype(F32)).astype(MXB)
        summed = dot_nt(picks, high) + dot_nt(picks, rest)
        for pair in range(pairs):
            delta_ref[pair, 0:2, at] = summed[2 * pair : 2 * pair + 2]
        return carry

    lax.fori_loop(0, tokens // rows, deltas, 0)

    def turn_keys(pair, carry):
        lanes = pl.ds(pl.multiple_of(pair * 2 * HEAD_DIM, 2 * HEAD_DIM), 2 * HEAD_DIM)
        across_ref[pair] = turned(k_ref[0, :, lanes])
        dq_ref[pair] = jnp.zeros(dq_ref.shape[1:], F32)
        dk_ref[:, lanes] = jnp.zeros((tokens, 2 * HEAD_DIM), F32)
        dv_ref[:, lanes] = jnp.zeros((tokens, 2 * HEAD_DIM), F32)
        return carry

    lax.fori_loop(0, pairs, turn_keys, 0)

    @pl.when(frame == 0)
    def _():
        greeted(peers + clip_peers)
        early_one()

    half = tokens // 2
    near = half // stripe
    near_first = lax.div(me, near) * half
    far_first = half - near_first
    last = frame == mine - 1
    shift = modes_ref[0:1, :]
    scale = modes_ref[1:2, :]

    def hidden_of(at):
        normed, rate = normalise(x_ref[0, at, :].astype(F32))
        return normed, rate, (normed * (1.0 + scale) + shift).astype(MXB)

    def phase_pass(phase, carry):
        def step_pass(index, carry):
            pair = lax.rem(index, pairs)
            step = lax.div(index, pairs) + 3 * phase

            @pl.when((frame == 0) & (phase == 0) & (index == 2 * pairs))
            def _():
                early_two()

            @pl.when(last & (phase == 0) & (index == 2 * pairs))
            def _():
                early_four()

            lanes = pl.ds(pl.multiple_of(pair * 2 * HEAD_DIM, 2 * HEAD_DIM), 2 * HEAD_DIM)
            query_first = jnp.where(step >= 2, near_first, far_first)
            key_first = jnp.where(lax.rem(step, 2) == 1, near_first, far_first)
            at = pl.ds(pl.multiple_of(query_first, half), half)
            query = halves(q_ref[0, at, lanes] * MXB(scale_factor))
            grad = halves(da_ref[0, at, lanes])
            query_both = jnp.concatenate(query, axis=0)
            grad_both = jnp.concatenate(grad, axis=0)
            grad_query = [jnp.zeros((HEAD_DIM, half), F32), jnp.zeros((HEAD_DIM, half), F32)]
            for first in range(0, half, part):
                span = pl.ds(pl.multiple_of(key_first + first, part), part)
                keys = k_ref[0, span, lanes]
                values = v_ref[0, span, lanes]
                weights = []
                grad_scores = []
                for side in range(2):
                    scores = dot_nt(keys, query[side])
                    exact = jnp.exp(scores - log_ref[0, pair, side : side + 1, at])
                    grad_weights = dot_nt(values, grad[side])
                    term = (exact * (grad_weights - delta_ref[pair, side : side + 1, at])).astype(MXB)
                    weights.append(exact.astype(MXB))
                    grad_scores.append(term)
                    across = across_ref[pair, side * HEAD_DIM : (side + 1) * HEAD_DIM, span]
                    grad_query[side] = grad_query[side] + dot(across, term)
                dv_ref[span, lanes] += dot(jnp.concatenate(weights, axis=1), grad_both)
                dk_ref[span, lanes] += dot(jnp.concatenate(grad_scores, axis=1), query_both)
            for side in range(2):
                dq_ref[pair, side * HEAD_DIM : (side + 1) * HEAD_DIM, at] += grad_query[side]
            return carry

        lax.fori_loop(0, jnp.where(phase == 0, 3 * pairs, pairs), step_pass, 0)
        first_row = jnp.where(phase == 0, far_first, near_first)

        def weigh(index, carry):
            at = pl.ds(pl.multiple_of(first_row + index * rows, rows), rows)
            for pair in range(pairs):
                lanes = slice(2 * HEAD_DIM * pair, 2 * HEAD_DIM * (pair + 1))
                mix_ref[at, lanes] = (dq_ref[pair, :, at].T * scale_factor).astype(MXB)
            mix_ref[at, width : 2 * width] = dk_ref[at, :].astype(MXB)
            mix_ref[at, 2 * width :] = dv_ref[at, :].astype(MXB)
            _, _, hidden = hidden_of(at)
            grad_mix = mix_ref[at, :]
            grad_proj_ref[...] += dot_tn(hidden, grad_mix)
            bias_sums_ref[...] += eight_rows(grad_mix.astype(F32))
            return carry

        lax.fori_loop(0, half // rows, weigh, 0)

        @pl.when(last & (phase == 1))
        def _():
            for each in range(clips):
                clip_out_ref[each] = grad_proj_ref[each * span_rows : (each + 1) * span_rows, :].astype(MXB)
            for _, peer, _ in clip_peers:
                g1_copy(peer, clip).start()

        def finish(index, carry):
            peer = lax.div(first_row, stripe) + index
            at = pl.ds(pl.multiple_of(first_row + index * stripe, stripe), stripe)
            normed, rate, _ = hidden_of(at)
            grad_hidden = dot_nt(mix_ref[at, :], proj_ref[...])
            sums_ref[0] += eight_rows(grad_hidden)
            sums_ref[1] += eight_rows(grad_hidden * normed)
            dx_ref[frame, at, :] = normalise_back(grad_hidden, normed, rate, scale).astype(MXB)

            @pl.when(peer != me)
            def _():
                dx_copy(frame, peer).start()

            @pl.when(peer == me)
            def _():
                dx_keep(frame).start()

            return carry

        lax.fori_loop(0, near, finish, 0)
        stage = 2 * frame + phase

        @pl.when(stage == 1)
        def _():
            early_three()

        return carry

    lax.fori_loop(0, 2, phase_pass, 0)

    @pl.when(last)
    def _():
        total = grad_proj_ref[pl.ds(pl.multiple_of(clip * span_rows, span_rows), span_rows), :]
        for _, _, source in clip_peers:
            g1_copy(source, source).wait_recv()
            total = total + clip_in_ref[source].astype(F32)
        for owner in range(owners):
            unit_out_ref[owner] = total[owner * unit : (owner + 1) * unit].astype(MXB)

            @pl.when(owner != me)
            def _():
                g2_copy(owner, me).start()

        def row_sum(array):
            return jnp.sum(array, axis=0, keepdims=True)

        def rows_of(array):
            flat = row_sum(array)
            return [flat[:, first : first + width] for first in range(0, flat.shape[1], width)]

        lines = [row_sum(sums_ref[0]), row_sum(sums_ref[1])]
        lines += [row_sum(mid_sums_ref[line]) for line in range(2, 9)]
        lines += rows_of(bias_sums_ref[...]) + rows_of(t_sums_ref[...])
        lines += [row_sum(mid_sums_ref[line]) for line in range(9, 12)]
        lines += rows_of(in_sums_ref[...])
        lines += [modes_ref[COND : COND + 1, :]] * (ROWS - len(lines))
        vec_ref[...] = jnp.concatenate(lines, axis=0)
        for _, peer, _ in peers:
            v1_copy(peer, me).start()

        @pl.when(me < owners)
        def _():
            total = unit_out_ref[me].astype(F32)
            for _, _, source in peers:
                g2_copy(me, source).wait_recv()
                total = total + unit_in_ref[source].astype(F32)
            piece_ref[pl.ds(pl.multiple_of(me * unit, unit), unit), :] = total.astype(MXB)
            for _, peer, _ in peers:
                g3_copy(peer, me).start()

        total = vec_ref[...]
        for _, _, source in peers:
            v1_copy(source, source).wait_recv()
            total = total + vec_in_ref[source]
        at_row = lax.broadcasted_iota(jnp.int32, (ROWS, width), 0)
        row_ref[...] = jnp.where(at_row < COND, total, vec_ref[...])
        for _, peer, _ in clip_peers:
            v2_copy(peer, clip).start()

        for owner in range(owners):

            @pl.when(owner != me)
            def _():
                g3_copy(owner, owner).wait_recv()

        for _, peer, _ in clip_peers:
            g4_copy(peer, clip).start()
        proj_out[pl.ds(pl.multiple_of(clip * span_rows, span_rows), span_rows), :] = piece_ref[...]
        row_in_ref[clip] = row_ref[...]
        for _, _, source in clip_peers:
            v2_copy(source, source).wait_recv()
        row_out[...] = row_in_ref[...]
        for _, _, source in clip_peers:
            g4_copy(source, source).wait_recv()
            proj_out[pl.ds(pl.multiple_of(source * span_rows, span_rows), span_rows), :] = all_ref[source]

        for _, peer, _ in clip_peers:
            g1_copy(peer, clip).wait_send()
            g4_copy(peer, clip).wait_send()
            v2_copy(peer, clip).wait_send()
        for _, peer, _ in peers:
            v1_copy(peer, me).wait_send()

        for owner in range(owners):

            @pl.when(owner != me)
            def _():
                g2_copy(owner, me).wait_send()

        @pl.when(me < owners)
        def _():
            for _, peer, _ in peers:
                g3_copy(peer, me).wait_send()

        early_end()
        for each in range(mine):
            dx_keep(each).wait()
            for _, peer, _ in peers:
                dx_copy(each, peer).wait_send()
                dx_landed(each, peer).wait_recv()


def middle(
    x_ref, soon_ref, og_ref, attn_hbm, modes_ref, so_ref, t_ref, to_ref, in_ref, out_ref,
    block_ref, g1_ref, da_out,
    stack_out, sums_ref, t_sums_ref, in_sums_ref,
    grad_so_ref, grad_t_ref, grad_to_ref, grad_in_ref, grad_out_ref,
    da_ref, attn_ref, late_ref, send_sem, recv_sem, own_sem, late_send, late_recv, late_own, peer_count,
):
    frames, tile, width = x_ref.shape
    count = frames * tile
    pairs = width // (2 * HEAD_DIM)
    scale_factor = HEAD_DIM**-0.5
    mine = frames // peer_count
    steps = pl.num_programs(0)
    stripe = da_out.shape[1] // peer_count
    at_step = pl.program_id(0)
    me, peers = others(peer_count)

    def da_copy(at_step, step, peer):
        first = pl.multiple_of(me * stripe + at_step * tile, tile)
        slot = lax.rem(at_step, 2)
        return send(
            da_ref.at[slot, pl.ds(peer * mine, mine)], da_out.at[:, pl.ds(first, tile), :],
            send_sem.at[slot, step], recv_sem.at[step], peer,
        )

    def da_keep(at_step):
        first = pl.multiple_of(me * stripe + at_step * tile, tile)
        slot = lax.rem(at_step, 2)
        return pltpu.make_async_copy(
            da_ref.at[slot, pl.ds(me * mine, mine)], da_out.at[:, pl.ds(first, tile), :], own_sem.at[slot]
        )

    def da_landed(step, source):
        rows = da_out.at[:, pl.ds(pl.multiple_of(source * stripe, stripe), stripe), :]
        return send(rows, rows, send_sem.at[0, step], recv_sem.at[step], source)

    soon_steps = (stripe - late_ref.shape[1]) // tile
    late = late_ref.shape[1]

    def late_copy(frame, step, peer):
        rows = pl.ds(pl.multiple_of(peer * stripe + stripe - late, tile), late)
        return send(
            attn_hbm.at[frame, rows, :], late_ref.at[me * mine + frame],
            late_send.at[frame, step], late_recv.at[frame, step], peer,
        )

    def late_landed(frame, step, source):
        rows = late_ref.at[source * mine + frame]
        return send(rows, rows, late_send.at[frame, step], late_recv.at[frame, step], source)

    def late_keep(frame):
        rows = pl.ds(pl.multiple_of(me * stripe + stripe - late, tile), late)
        return pltpu.make_async_copy(attn_hbm.at[frame, rows, :], late_ref.at[me * mine + frame], late_own.at[frame])

    @pl.when(at_step == 0)
    def _():
        greet(peers)
        greeted(peers)
        for frame in range(mine):
            late_keep(frame).start()
            for step, peer, _ in peers:
                late_copy(frame, step, peer).start()
        for ref in (grad_so_ref, grad_t_ref, grad_to_ref, grad_in_ref, grad_out_ref, sums_ref, t_sums_ref, in_sums_ref):
            ref[...] = jnp.zeros_like(ref)

    def mode(row):
        return modes_ref[row : row + 1, :]

    @pl.when(at_step < soon_steps)
    def _():
        attn_ref[...] = soon_ref[...]

    @pl.when(at_step == soon_steps)
    def _():
        for frame in range(mine):
            late_keep(frame).wait()
            for step, _, source in peers:
                late_landed(frame, step, source).wait_recv()

    @pl.when(at_step >= soon_steps)
    def _():
        attn_ref[...] = late_ref[:, pl.ds(pl.multiple_of((at_step - soon_steps) * tile, tile), tile), :]

    cell = frames * GROUP
    groups = tile // GROUP

    def gather(ref):
        whole = ref[...].astype(F32)
        return jnp.concatenate(
            [whole[:, g * GROUP : (g + 1) * GROUP, :].reshape(cell, width) for g in range(groups)], axis=0
        )

    def scatter(value):
        return jnp.concatenate(
            [value[g * cell : (g + 1) * cell].reshape(frames, GROUP, width) for g in range(groups)], axis=1
        )

    field = gather(x_ref)
    attn_one = gather(attn_ref).astype(MXB)
    branch_one = dot(attn_one, so_ref[...]) + mode(SO_BIAS)
    field_one = field + mode(2) * branch_one
    normed_two, rate_two = normalise(field_one)
    hidden_two = (normed_two * (1.0 + mode(4)) + mode(3)).astype(MXB)
    mixed = (dot(hidden_two, t_ref[...]) + wide(modes_ref, T_BIAS, 3)).astype(MXB)
    row_at = lax.broadcasted_iota(jnp.int32, (cell, 2 * cell), 0)
    lane_at = lax.broadcasted_iota(jnp.int32, (cell, 2 * cell), 1)
    mask = jnp.where(lax.rem(row_at, GROUP) == lax.rem(lane_at, GROUP), 0.0, -1e30).astype(F32)
    exact = []
    rounded = []
    queries = []
    attn_rows = []
    for g in range(groups):
        of_group = mixed[g * cell : (g + 1) * cell]
        attn_parts = []
        for pair in range(pairs):
            lanes = slice(2 * HEAD_DIM * pair, 2 * HEAD_DIM * (pair + 1))
            query = jnp.concatenate(halves(of_group[:, lanes] * MXB(scale_factor)), axis=0)
            queries.append(query)
            scores = dot_nt(of_group[:, width:][:, lanes], query) + mask
            exponent = jnp.exp(scores - jnp.max(scores, axis=0, keepdims=True))
            weights = exponent * (1.0 / jnp.sum(exponent, axis=0, keepdims=True))
            exact.append(weights)
            rounded.append(weights.astype(MXB))
            both = dot_tn(of_group[:, 2 * width :][:, lanes], rounded[-1])
            attn_parts.append(jnp.concatenate([both[:HEAD_DIM, :cell], both[HEAD_DIM:, cell:]], axis=0).T.astype(MXB))
        attn_rows.append(jnp.concatenate(attn_parts, axis=1))
    attn_two = jnp.concatenate(attn_rows, axis=0)
    branch_two = dot(attn_two, to_ref[...]) + mode(TO_BIAS)
    field_two = field_one + mode(5) * branch_two
    normed_three, rate_three = normalise(field_two)
    hidden_three = (normed_three * (1.0 + mode(7)) + mode(6)).astype(MXB)
    inner = dot(hidden_three, in_ref[...]) + wide(modes_ref, IN_BIAS, in_ref.shape[1] // width)
    square = inner * inner
    bend = jnp.tanh(inner * (GELU_RATE + GELU_RATE * 0.044715 * square))
    half_up = 0.5 + 0.5 * bend
    active = (inner * half_up).astype(MXB)
    slope = half_up + inner * (0.5 - 0.5 * bend * bend) * (GELU_RATE + 3.0 * GELU_RATE * 0.044715 * square)
    branch_three = dot(active, out_ref[...]) + mode(OUT_BIAS)
    block_ref[...] = scatter(field_two + mode(8) * branch_three).astype(MXB)

    grad_field = gather(og_ref).astype(F32) * mode(WEIGHT)
    sums_ref[8] += eight_rows(grad_field * branch_three)
    grad_branch = (mode(8) * grad_field).astype(MXB)
    grad_out_ref[...] += dot_tn(grad_branch, active)
    sums_ref[11] += eight_rows(grad_branch.astype(F32))
    grad_inner = (dot_nt(grad_branch, out_ref[...]) * slope).astype(MXB)
    grad_in_ref[...] += dot_tn(hidden_three, grad_inner)
    in_sums_ref[...] += eight_rows(grad_inner.astype(F32))
    grad_hidden = dot_nt(grad_inner, in_ref[...])
    sums_ref[6] += eight_rows(grad_hidden)
    sums_ref[7] += eight_rows(grad_hidden * normed_three)
    grad_field = grad_field + normalise_back(grad_hidden, normed_three, rate_three, mode(7))

    sums_ref[5] += eight_rows(grad_field * branch_two)
    grad_branch = (mode(5) * grad_field).astype(MXB)
    grad_to_ref[...] += dot_tn(attn_two, grad_branch)
    sums_ref[10] += eight_rows(grad_branch.astype(F32))
    grad_attn = dot_nt(grad_branch, to_ref[...]).astype(MXB)
    mix_rows = []
    for g in range(groups):
        of_group = mixed[g * cell : (g + 1) * cell]
        grad_queries = []
        grad_keys = []
        grad_values = []
        for pair in range(pairs):
            lanes = slice(2 * HEAD_DIM * pair, 2 * HEAD_DIM * (pair + 1))
            grad = jnp.concatenate(halves(grad_attn[g * cell : (g + 1) * cell, lanes]), axis=0)
            at = g * pairs + pair
            grad_weights = dot_nt(of_group[:, 2 * width :][:, lanes], grad)
            delta = jnp.sum(exact[at] * grad_weights, axis=0, keepdims=True)
            term = (exact[at] * (grad_weights - delta)).astype(MXB)
            both = dot_tn(of_group[:, width:][:, lanes], term)
            grad_query = jnp.concatenate([both[:HEAD_DIM, :cell], both[HEAD_DIM:, cell:]], axis=0).T
            grad_queries.append((grad_query * scale_factor).astype(MXB))
            grad_keys.append(dot(term, queries[at]).astype(MXB))
            grad_values.append(dot(rounded[at], grad).astype(MXB))
        mix_rows.append(jnp.concatenate(grad_queries + grad_keys + grad_values, axis=1))
    grad_mix = jnp.concatenate(mix_rows, axis=0)
    grad_t_ref[...] += dot_tn(hidden_two, grad_mix)
    t_sums_ref[...] += eight_rows(grad_mix.astype(F32))
    grad_hidden = dot_nt(grad_mix, t_ref[...])
    sums_ref[3] += eight_rows(grad_hidden)
    sums_ref[4] += eight_rows(grad_hidden * normed_two)
    grad_field = grad_field + normalise_back(grad_hidden, normed_two, rate_two, mode(4))

    sums_ref[2] += eight_rows(grad_field * branch_one)
    grad_branch = (mode(2) * grad_field).astype(MXB)
    grad_so_ref[...] += dot_tn(attn_one, grad_branch)
    sums_ref[9] += eight_rows(grad_branch.astype(F32))
    g1_ref[...] = scatter(grad_field)
    grad_attn = scatter(dot_nt(grad_branch, so_ref[...])).astype(MXB)

    def sent(at_step):
        da_keep(at_step).wait()
        for step, peer, _ in peers:
            da_copy(at_step, step, peer).wait_send()

    @pl.when(at_step >= 2)
    def _():
        sent(at_step - 2)

    da_ref[lax.rem(at_step, 2)] = grad_attn
    da_keep(at_step).start()
    for step, peer, _ in peers:
        da_copy(at_step, step, peer).start()

    @pl.when(at_step == steps - 1)
    def _():
        @pl.when(steps > 1)
        def _():
            sent(steps - 2)

        sent(steps - 1)
        for step, peer, source in peers:
            da_landed(step, source).wait_recv()
            for frame in range(mine):
                late_copy(frame, step, peer).wait_send()
        place = 0
        for ref in (grad_so_ref, grad_t_ref, grad_to_ref, grad_in_ref, grad_out_ref):
            for first in range(0, ref.shape[1], width):
                square = ref[:, first : first + width]
                stack_out[place] = (square.T if ref is grad_out_ref else square).astype(MXB)
                place += 1


def whole_spec(shape):
    rank = len(shape)
    return pl.BlockSpec(shape, lambda *_: (0,) * rank, pipeline_mode=pl.Buffered(1))


def acc_spec(shape):
    rank = len(shape)
    return pl.BlockSpec(shape, lambda *_: (0,) * rank)


def params(number):
    return pltpu.CompilerParams(vmem_limit_bytes=VMEM_BYTES, collective_id=number, has_side_effects=True)


def any_spec():
    return pl.BlockSpec(memory_space=pl.ANY)


def cost(flops, moved):
    return pl.CostEstimate(flops=flops, bytes_accessed=moved, transcendentals=0)


def fast_body(
    tokens, conditioning, timesteps, out_grad, ada_weight, ada_bias, spatial_proj, spatial_bias, spatial_out,
    spatial_out_bias, temporal_proj, temporal_bias, temporal_out, temporal_out_bias, hidden_in, hidden_in_bias,
    hidden_out, hidden_out_bias,
):
    _, frames, stripe, width = tokens.shape
    hidden = hidden_in.shape[1]
    pairs = width // (2 * HEAD_DIM)
    cond_act = jax.nn.silu(conditioning.astype(F32)).astype(MXB)
    modes = jnp.dot(cond_act, ada_weight, preferred_element_type=F32) + ada_bias
    slope = jnp.tan((timesteps.astype(F32) / TSTEPS + 0.008) / 1.008 * (0.5 * math.pi))
    loss_weight = jnp.minimum(1.0, 5.0 * slope * slope)
    blank = jnp.zeros((width,), F32)
    pieces = (
        modes.reshape(-1),
        spatial_bias[:width], blank, spatial_bias[width:],
        temporal_bias[:width], blank, temporal_bias[width:],
        spatial_out_bias, temporal_out_bias, hidden_out_bias, hidden_in_bias,
        jnp.broadcast_to(loss_weight, (width,)),
        cond_act.astype(F32).reshape(-1),
    )
    packed = jnp.zeros((ROWS * width,), F32)
    start = 0
    for piece in pieces:
        packed = packed + jnp.pad(piece, (start, ROWS * width - start - piece.size))
        start += piece.size
    modes = packed.reshape(ROWS, width)

    x_patches = tokens[0]
    count = lax.axis_size("sp")
    mine, patches = frames // count, stripe * count
    block = patches // 2
    soon = max(stripe // (2 * TILE), 1) * TILE
    frame_shape = jax.ShapeDtypeStruct((mine, patches, width), MXB)
    patch_shape = jax.ShapeDtypeStruct((frames, stripe, width), MXB)
    dma = pltpu.SemaphoreType.DMA
    x_frames, queries, keys, values, attn_frames, attn_patches, logs = pl.pallas_call(
        partial(spatial_forward, block=block, part=512, count=count),
        in_specs=[any_spec()] + [pl.BlockSpec(memory_space=pltpu.VMEM)] * 2,
        out_specs=[any_spec()] * 6 + [pl.BlockSpec(memory_space=pltpu.VMEM)],
        out_shape=[frame_shape] * 5
        + [
            jax.ShapeDtypeStruct((frames, soon, width), MXB),
            jax.ShapeDtypeStruct((mine, pairs, 2, patches), F32),
        ],
        scratch_shapes=[pltpu.VMEM((mine, patches, width), MXB)] * 5
        + [pltpu.VMEM((mine, 2 * pairs, HEAD_DIM + 16, patches), MXB)]
        + [pltpu.VMEM((mine, 2 * pairs, HEAD_DIM + 16, patches), F32), pltpu.VMEM((mine, pairs, 2, patches), F32)]
        + [dma((mine, count)), dma((mine, count)), dma((mine,))]
        + [dma((mine, pairs, count)), dma((mine, pairs, count)), dma((mine, pairs)), dma((5, mine))],
        compiler_params=params(0),
        cost_estimate=cost(10**11, 10**7),
    )(x_patches, modes, spatial_proj)

    tile_spec = pl.BlockSpec((frames, TILE, width), lambda i: (0, i, 0))
    soon_spec = pl.BlockSpec((frames, TILE, width), lambda i: (0, jnp.minimum(i, soon // TILE - 1), 0))
    small = (modes, spatial_out, temporal_proj, temporal_out, hidden_in, hidden_out)
    folds = hidden // width
    squares = 5 + 2 * folds
    held_shapes = [(width, width), (width, 3 * width), (width, width), (width, hidden), (width, hidden)]
    sums_shapes = [(squares, width, width), (12, 8, width), (8, 3 * width), (8, hidden)]
    out_shapes = [
        patch_shape,
        jax.ShapeDtypeStruct((frames, stripe, width), F32),
        frame_shape,
    ] + [jax.ShapeDtypeStruct(s, MXB if at < 1 else F32) for at, s in enumerate(sums_shapes)]
    (
        block_out, g1, da_frames, stack, sums, t_sums, in_sums,
    ) = pl.pallas_call(
        partial(middle, peer_count=count),
        grid=(stripe // TILE,),
        in_specs=[tile_spec, soon_spec, tile_spec, any_spec()] + [whole_spec(a.shape) for a in small],
        out_specs=[tile_spec] * 2 + [any_spec()] + [acc_spec(s) for s in sums_shapes],
        out_shape=out_shapes,
        scratch_shapes=[pltpu.VMEM(s, F32) for s in held_shapes]
        + [pltpu.VMEM((2, frames, TILE, width), MXB), pltpu.VMEM((frames, TILE, width), MXB)]
        + [pltpu.VMEM((frames, stripe - soon, width), MXB)]
        + [dma((2, count)), dma((count,)), dma((2,))]
        + [dma((mine, count)), dma((mine, count)), dma((mine,))],
        compiler_params=params(1),
        cost_estimate=cost(10**11, 10**7),
    )(x_patches, attn_patches, out_grad[0], attn_frames, *small)
    frame_spec = pl.BlockSpec((1, patches, width), lambda f: (f, 0, 0))
    log_spec = pl.BlockSpec((1, pairs, 2, patches), lambda f: (f, 0, 0, 0))
    clips = lax.axis_size("clip")
    span_rows = width // clips
    unit = 16 * (-(-span_rows // (16 * count)))
    dx_patches, early, grad_sp, lines_of = pl.pallas_call(
        partial(spatial_backward, rows=512, part=512, count=count, clips=clips),
        grid=(mine,),
        in_specs=[frame_spec] * 5
        + [log_spec, frame_spec, whole_spec((ROWS, width)), whole_spec((width, 3 * width))]
        + [whole_spec(a.shape) for a in (sums, t_sums, in_sums)]
        + [any_spec()],
        out_specs=[any_spec(), any_spec(), acc_spec((width, 3 * width)), acc_spec((clips, ROWS, width))],
        out_shape=[
            patch_shape,
            jax.ShapeDtypeStruct((squares, width, width), MXB),
            jax.ShapeDtypeStruct((width, 3 * width), MXB),
            jax.ShapeDtypeStruct((clips, ROWS, width), F32),
        ],
        scratch_shapes=[
            pltpu.VMEM((width, 3 * width), F32),
            pltpu.VMEM((mine, patches, width), MXB),
            pltpu.VMEM((patches, 3 * width), MXB),
            pltpu.VMEM((pairs, 2, patches), F32),
            pltpu.VMEM((pairs, 2 * HEAD_DIM, patches), F32),
            pltpu.VMEM((patches, width), F32),
            pltpu.VMEM((patches, width), F32),
            pltpu.VMEM((pairs, 2 * HEAD_DIM, patches), MXB),
            pltpu.VMEM((2, 8, width), F32),
            pltpu.VMEM((8, 3 * width), F32),
            pltpu.VMEM((clips, span_rows, 3 * width), MXB),
            pltpu.VMEM((clips, span_rows, 3 * width), MXB),
            pltpu.VMEM((count, unit, 3 * width), MXB),
            pltpu.VMEM((count, unit, 3 * width), MXB),
            pltpu.VMEM((span_rows, 3 * width), MXB),
            pltpu.VMEM((clips, span_rows, 3 * width), MXB),
            pltpu.VMEM((ROWS, width), F32),
            pltpu.VMEM((count, ROWS, width), F32),
            pltpu.VMEM((ROWS, width), F32),
            pltpu.VMEM((clips, ROWS, width), F32),
            pltpu.VMEM((clips, squares, span_rows, width), MXB),
            pltpu.VMEM((count, squares, unit, width), MXB),
            pltpu.VMEM((count, squares, unit, width), MXB),
            pltpu.VMEM((squares, span_rows, width), MXB),
            dma((mine, count)),
            dma((mine, count)),
            dma((mine,)),
        ]
        + [dma((clips,))] * 2
        + [dma((count,))] * 4
        + [dma((clips,))] * 2
        + [dma((count,))] * 2
        + [dma((clips,))] * 2
        + [dma((clips,))] * 2
        + [dma((count,))] * 4
        + [dma((clips,))] * 2
        + [dma((2,))],
        compiler_params=params(2),
        cost_estimate=cost(2 * 10**11, 10**7),
    )(da_frames, attn_frames, queries, keys, values, logs, x_frames, modes, spatial_proj, sums, t_sums, in_sums, stack)
    input_grad = (g1 + dx_patches.astype(F32)).astype(MXB)

    def columns(first, number):
        return jnp.concatenate([early[first + at].astype(F32) for at in range(number)], axis=1)

    flat = jnp.sum(lines_of, axis=0).reshape(-1)
    conds = lines_of[:, COND]
    grads = lines_of[:, :9].reshape(clips, 9 * width)
    grad_ada = sum(conds[at][:, None] * grads[at][None, :] for at in range(clips))

    def lines(first, rows=1):
        return flat[first * width : (first + rows) * width]

    return (
        block_out[None],
        input_grad[None],
        grad_ada,
        lines(0, 9),
        grad_sp.astype(F32),
        jnp.concatenate([lines(SP_BIAS), lines(SP_BIAS + 2)]),
        columns(0, 1),
        lines(SO_BIAS),
        columns(1, 3),
        jnp.concatenate([lines(T_BIAS), lines(T_BIAS + 2)]),
        columns(4, 1),
        lines(TO_BIAS),
        columns(5, folds),
        lines(IN_BIAS, hidden // width),
        early[5 + folds :].astype(F32).reshape(hidden, width),
        lines(OUT_BIAS),
    )


def chosen(tokens, *others):
    clips_here, frames, stripe, width = tokens.shape
    count, clips = lax.axis_size("sp"), lax.axis_size("clip")
    fits = clips_here == 1 and count % 2 == 0 and frames % count == 0 and frames >= 2 * count
    fits = fits and stripe % (2 * TILE) == 0 and width % (16 * clips) == 0 and width <= 16 * clips * count
    if fits:
        return fast_body(tokens, *others)
    return body(tokens, *others)


def solution(mesh):
    return jax.shard_map(
        chosen,
        mesh=mesh,
        in_specs=(
            P("clip", None, "sp", None),
            P("clip", None),
            P("clip"),
            P("clip", None, "sp", None),
            P(),
            P(),
            P(),
            P(),
            P(),
            P(),
            P(),
            P(),
            P(),
            P(),
            P(),
            P(),
            P(),
            P(),
        ),
        out_specs=(
            P("clip", None, "sp", None),
            P("clip", None, "sp", None),
            P(),
            P(),
            P(),
            P(),
            P(),
            P(),
            P(),
            P(),
            P(),
            P(),
            P(),
            P(),
            P(),
            P(),
        ),
        check_vma=False,
    )
```
